128 devices in a mesh: frame: 8 (over z_lo, x), space: 16 (over z_hi, y, core).
Axes of the slice: x: 4, y: 4, z: 4 (z_hi: 2, z_lo: 2; z = z_hi * 2 + z_lo), core: 2. Of those that a mesh axis runs over, the one named last changes fastest.
Arguments:
- queries: bfloat16 [2, 8, 1920, 3072], P(None, 'frame', 'space'), may hold values from -15 to 15
- keys: bfloat16 [2, 8, 1920, 3072], P(None, 'frame', 'space'), may hold values from -15 to 15
- values: bfloat16 [2, 8, 1920, 3072], P(None, 'frame', 'space'), may hold values from -6 to 6
- grad_out: bfloat16 [2, 8, 1920, 3072], P(None, 'frame', 'space'), may hold values from -6 to 6
- head_class: int32 [2, 24], replicated, may hold values from 0 to 1, as said below
Outputs:
- grad_queries: bfloat16 [2, 8, 1920, 3072], P(None, 'frame', 'space')
- grad_keys: bfloat16 [2, 8, 1920, 3072], P(None, 'frame', 'space')
- grad_values: bfloat16 [2, 8, 1920, 3072], P(None, 'frame', 'space')
The draws below stay inside these ranges and needn't reach their ends.
Inputs may be any that keep to these rules, and one draw needn't show every extreme that they name: `head_class`: in every layer exactly 16 heads carry one label and the other 8 heads the other. The common label alternates from layer to layer: the first layer may have either, the next the other one.
All inputs are finite; a program needn't handle non-finite values.
Results may differ from the reference program's by a relative error of at most 0.012.
The reference program's roundings to bfloat16 on the way count: a program that leaves them out, or rounds other values in their place, can miss the bound.
Values may be sent and summed in bfloat16 or wider, within the bound.
No kernel may reach another device: no remote copies, remote signals or barrier semaphores. Data moves between devices by JAX's collectives and lax.ppermute only.
A program may use at most 128 MiB of HBM per device.

```python
import math
import jax
import jax.numpy as jnp
from jax import lax

H = 24
RT = 16
RS = 56
D = 3072
LAYERS = 2
SLOTS = 16
PW = 80
FRAMES = 8
POSITIONS = 1920


def shared_rows(key):
    return jnp.clip(jax.random.normal(key, (LAYERS, FRAMES, POSITIONS, D), jnp.float32), -5.0, 5.0)


def draw_keys(key, part):
    common = shared_rows(key)
    return common.astype(jnp.bfloat16)


def draw_queries(key, part):
    key = jax.random.fold_in(key, 22)
    fresh = jnp.clip(jax.random.normal(key, (LAYERS, FRAMES, POSITIONS, D), jnp.float32), -5.0, 5.0)
    return fresh.astype(jnp.bfloat16)


def draw_head_class(key, part):
    key = jax.random.fold_in(key, 5)
    first, second = jax.random.split(key)
    first_label = jax.random.randint(first, (), 0, 2)
    layer_ids = jnp.arange(LAYERS, dtype=jnp.int32)
    common_label = ((first_label + layer_ids) % 2)[:, None]
    layer_keys = jax.random.split(second, LAYERS)
    rankings = jax.vmap(lambda layer_key: jax.random.permutation(layer_key, H))(layer_keys)
    return jnp.where(rankings < SLOTS, common_label, 1 - common_label).astype(jnp.int32)


def shard_levels(rng, extent, cuts, smallest, largest):
    def one(dim, parts):
        heights = jax.random.uniform(jax.random.fold_in(jax.random.fold_in(rng, 6), dim), (parts,), jnp.float32, smallest / len(cuts), largest / len(cuts))
        return jnp.repeat(jnp.exp(heights), extent[dim] // parts).reshape((-1,) + (1,) * (len(extent) - dim - 1))

    factor_of = one(*cuts[0])
    for cut in cuts[1:]:
        factor_of = factor_of * one(*cut)
    return factor_of


def gaussian(own_key, shape, scale, most, cuts=(), kind=jnp.bfloat16):
    factor_of = shard_levels(own_key, shape, cuts, -0.22, 0.18) if cuts else 1.0
    drawn = jax.random.normal(own_key, shape, jnp.float32) * scale * factor_of
    return jnp.minimum(jnp.maximum(drawn, -most), most).astype(kind)


def setup_inputs(seed: int = 0) -> dict:
    key_of = jax.random.split(jax.random.key(seed), 6)
    queries = draw_queries(jax.random.fold_in(key_of[5], 71), 0)
    keys = draw_keys(jax.random.fold_in(key_of[5], 71), 0)
    values = gaussian(key_of[2], (LAYERS, FRAMES, POSITIONS, D), 1.0, 6.0, ((1, 8), (2, 16)))
    grad_out = gaussian(key_of[3], (LAYERS, FRAMES, POSITIONS, D), 1.0, 6.0, ((1, 8), (2, 16)))
    head_class = draw_head_class(jax.random.fold_in(key_of[5], 71), 0)
    return {"queries": queries, "keys": keys, "values": values, "grad_out": grad_out, "head_class": head_class}


THETA = 256.0

def angle_table(frame_ids, position_ids):
    head_width = RT + 2 * RS
    channel = jnp.arange(head_width, dtype=jnp.int32)
    pair_index = channel // 2
    time_pairs = RT // 2
    space_pairs = RS // 2
    is_time = pair_index < time_pairs
    is_row = jnp.logical_and(pair_index >= time_pairs, pair_index < time_pairs + space_pairs)
    local_pair = jnp.where(is_time, pair_index, jnp.where(is_row, pair_index - time_pairs, pair_index - time_pairs - space_pairs))
    part_width = jnp.where(is_time, RT, RS)
    frequency = THETA ** (-2.0 * local_pair.astype(jnp.float32) / part_width.astype(jnp.float32))
    time_value = frame_ids.astype(jnp.float32)[:, None, None]
    row_value = (position_ids // PW).astype(jnp.float32)[None, :, None]
    column_value = (position_ids % PW).astype(jnp.float32)[None, :, None]
    coordinate = jnp.where(is_time, time_value, jnp.where(is_row, row_value, column_value))
    angles = coordinate * frequency
    return (jnp.cos(angles)[:, :, None, :], jnp.sin(angles)[:, :, None, :])

def partner(values_in):
    upper = jnp.roll(values_in, -1, -1)
    lower = jnp.roll(values_in, 1, -1)
    is_even = jnp.arange(values_in.shape[-1], dtype=jnp.int32) % 2 == 0
    return jnp.where(is_even, -upper, lower)

def rotate(values_in, cosine, sine):
    return values_in * cosine + partner(values_in) * sine

def unrotate(values_in, cosine, sine):
    return values_in * cosine - partner(values_in) * sine

def selections(head_class):
    spatial = (head_class == 0).astype(jnp.int32)
    temporal = 1 - spatial
    slot_ids = jnp.arange(SLOTS, dtype=jnp.int32)[:, None]
    spatial_rank = jnp.cumsum(spatial).astype(jnp.int32) - 1
    temporal_rank = jnp.cumsum(temporal).astype(jnp.int32) - 1
    spatial_pick = jnp.logical_and(spatial_rank[None, :] == slot_ids, spatial[None, :] == 1)
    temporal_pick = jnp.logical_and(temporal_rank[None, :] == slot_ids, temporal[None, :] == 1)
    return (spatial_pick, temporal_pick)

def settle(array):
    return lax.optimization_barrier(array.astype(jnp.bfloat16))

def attend_rows(queries, key_rows, value_rows, grad_rows):
    row_count, head_width = queries.shape
    scaling = 1.0 / math.sqrt(head_width)
    blocks = 1
    while row_count // blocks > 1280 or row_count % blocks:
        blocks += 1
    block_rows = row_count // blocks

    def advance(totals, pieces):
        key_total, value_total = totals
        query_block, grad_block = pieces
        scores = jnp.dot(query_block, key_rows.T, preferred_element_type=jnp.float32) * scaling
        shifted = jnp.exp(scores - lax.optimization_barrier(jnp.max(scores, -1, keepdims=True)))
        probs = shifted / lax.optimization_barrier(jnp.sum(shifted, -1, keepdims=True))
        probs_rounded = probs.astype(jnp.bfloat16)
        grad_probs = jnp.dot(grad_block, value_rows.T, preferred_element_type=jnp.float32)
        row_delta = lax.optimization_barrier(jnp.sum(probs * grad_probs, -1, keepdims=True))
        grad_scores = (scaling * probs * (grad_probs - row_delta)).astype(jnp.bfloat16)
        grad_query = jnp.dot(grad_scores, key_rows, preferred_element_type=jnp.float32).astype(jnp.bfloat16)
        key_total = key_total + jnp.dot(grad_scores.T, query_block, preferred_element_type=jnp.float32)
        value_total = value_total + jnp.dot(probs_rounded.T, grad_block, preferred_element_type=jnp.float32)
        return ((key_total, value_total), grad_query)
    zeros = jnp.zeros((key_rows.shape[0], head_width), jnp.float32)
    (key_total, value_total), grad_query = lax.scan(advance, (zeros, zeros), (queries.reshape(blocks, block_rows, head_width), grad_rows.reshape(blocks, block_rows, head_width)))
    return (grad_query.reshape(row_count, head_width), key_total, value_total)

def attend_frames(queries, key_rows, value_rows, grad_rows):
    scaling = 1.0 / math.sqrt(queries.shape[-1])
    query_wide = queries.astype(jnp.float32)
    key_wide = key_rows.astype(jnp.float32)
    value_wide = value_rows.astype(jnp.float32)
    grad_wide = grad_rows.astype(jnp.float32)
    scores = jnp.einsum('fspe,gspe->spfg', query_wide, key_wide) * scaling
    shifted = jnp.exp(scores - lax.optimization_barrier(jnp.max(scores, -1, keepdims=True)))
    probs = shifted / lax.optimization_barrier(jnp.sum(shifted, -1, keepdims=True))
    probs_rounded = settle(probs).astype(jnp.float32)
    grad_probs = jnp.einsum('fspe,gspe->spfg', grad_wide, value_wide)
    row_delta = lax.optimization_barrier(jnp.sum(probs * grad_probs, -1, keepdims=True))
    grad_scores = settle(scaling * probs * (grad_probs - row_delta)).astype(jnp.float32)
    grad_values = jnp.einsum('spfg,fspe->gspe', probs_rounded, grad_wide).astype(jnp.bfloat16)
    grad_queries = jnp.einsum('spfg,gspe->fspe', grad_scores, key_wide).astype(jnp.bfloat16)
    grad_keys = jnp.einsum('spfg,fspe->gspe', grad_scores, query_wide).astype(jnp.bfloat16)
    return (grad_queries, grad_keys, grad_values)

def one_layer(queries, keys, values, grad_out, layer_class):
    head_width = RT + 2 * RS
    heads_shape = (FRAMES, POSITIONS, H, head_width)
    slot_shape = (FRAMES, SLOTS, POSITIONS, head_width)
    cosine, sine = angle_table(jnp.arange(FRAMES, dtype=jnp.int32), jnp.arange(POSITIONS, dtype=jnp.int32))
    rot_queries = settle(rotate(queries.reshape(heads_shape).astype(jnp.float32), cosine, sine))
    rot_keys = settle(rotate(keys.reshape(heads_shape).astype(jnp.float32), cosine, sine))
    spatial_pick, temporal_pick = selections(layer_class)
    spatial_sel = spatial_pick.astype(jnp.float32)
    temporal_sel = temporal_pick.astype(jnp.float32)

    def gather_slots(array, chooser):
        return settle(jnp.einsum('fphe,sh->fspe', array.astype(jnp.float32), chooser))
    sources = (rot_queries, rot_keys, values.reshape(heads_shape), grad_out.reshape(heads_shape))
    spatial_flat = tuple((gather_slots(array, spatial_sel).reshape(FRAMES * SLOTS, POSITIONS, head_width) for array in sources))
    spatial_dq, spatial_dk, spatial_dv = lax.map(lambda pieces: attend_rows(*pieces), spatial_flat)
    spatial_grads = (spatial_dq.reshape(slot_shape), settle(spatial_dk).reshape(slot_shape), settle(spatial_dv).reshape(slot_shape))
    temporal_parts = tuple((gather_slots(array, temporal_sel) for array in sources))
    temporal_grads = attend_frames(*temporal_parts)

    def place(spatial_term, temporal_term):
        return jnp.einsum('fspe,sh->fphe', spatial_term.astype(jnp.float32), spatial_sel) + jnp.einsum('fspe,sh->fphe', temporal_term.astype(jnp.float32), temporal_sel)
    flat_shape = (FRAMES, POSITIONS, H * head_width)
    grad_queries = unrotate(place(spatial_grads[0], temporal_grads[0]), cosine, sine).astype(jnp.bfloat16).reshape(flat_shape)
    grad_keys = unrotate(place(spatial_grads[1], temporal_grads[1]), cosine, sine).astype(jnp.bfloat16).reshape(flat_shape)
    grad_values = place(spatial_grads[2], temporal_grads[2]).astype(jnp.bfloat16).reshape(flat_shape)
    return (grad_queries, grad_keys, grad_values)

def reference(queries, keys, values, grad_out, head_class):
    results = [one_layer(queries[layer_index], keys[layer_index], values[layer_index], grad_out[layer_index], head_class[layer_index]) for layer_index in range(LAYERS)]
    grad_queries = jnp.stack([result[0] for result in results])
    grad_keys = jnp.stack([result[1] for result in results])
    grad_values = jnp.stack([result[2] for result in results])
    return (grad_queries, grad_keys, grad_values)
```

```python
import math

import jax
import jax.numpy as jnp
import numpy as np
from jax import lax
from jax.experimental import pallas as pl
from jax.experimental.pallas import tpu as pltpu
from jax.sharding import PartitionSpec as P

RT = 16
RS = 56
PW = 80
THETA = 256.0
W = RT + 2 * RS
HEADS = 24
LAYERS = 2
FRAMES = 8
SPACES = 16
ROWS = 120
POSITIONS = SPACES * ROWS
HALF = 64
BACK = 4 * ROWS + HALF
QB = 512
PADDED = 2048
KB = 480
TP = 24
GROUP = 4
VMEM = 60 * 1024 * 1024
SCALE = 1.0 / math.sqrt(W)
SCALE2 = SCALE * math.log2(math.e)
F32 = jnp.float32
BF16 = jnp.bfloat16


OUT = (LAYERS, 1, ROWS, HEADS * W)


def whole(shape):
    return pl.BlockSpec(shape, lambda i, h, p: (0,) * len(shape))


def tables():
    channel = np.arange(W)
    pair = channel // 2
    tpairs, spairs = RT // 2, RS // 2
    is_time = pair < tpairs
    is_row = (pair >= tpairs) & (pair < tpairs + spairs)
    local = np.where(is_time, pair, np.where(is_row, pair - tpairs, pair - tpairs - spairs))
    width = np.where(is_time, RT, RS)
    freq = THETA ** (-2.0 * local / width)
    sign = np.where(channel % 2 == 0, -1.0, 1.0)
    time = np.arange(FRAMES)[:, None] * freq
    position = np.arange(POSITIONS)[:, None]
    place = np.where(is_row, position // PW, position % PW) * freq
    return (
        np.cos(time).astype(np.float32),
        (np.sin(time) * sign).astype(np.float32),
        np.cos(place).astype(np.float32),
        (np.sin(place) * sign).astype(np.float32),
    )


def lane_ids(shape):
    return lax.broadcasted_iota(jnp.int32, shape, len(shape) - 1)


def swapped(x):
    up = pltpu.roll(x, W - 1, 1)
    low = pltpu.roll(x, 1, 1)
    return jnp.where(lane_ids(x.shape) % 2 == 0, up, low)


def merged(time_row, place_rows):
    return jnp.where(lane_ids(place_rows.shape) < RT, time_row, place_rows)


def rotate(x, cosine, sine):
    return x * cosine + swapped(x) * sine


def unrotate(x, cosine, sine):
    x = x.astype(BF16).astype(F32)
    return x * cosine - swapped(x) * sine


def pick_heads(hc, layers, spatial, ids):
    def look(h, n, layer):
        mine = (hc[layer, h] == 0) == spatial

        @pl.when(mine)
        def _():
            ids[n] = layer * HEADS + h

        return n + mine.astype(jnp.int32)

    found = jnp.int32(0)
    for layer in layers:
        found = lax.fori_loop(0, HEADS, lambda h, n: look(h, n, layer), found)
    return found


def lanes_of(h):
    return pl.ds(pl.multiple_of(h * W, W), W)


def pack_body(hc, place, q, k, v, g, ct, st, cp, sp, out, count, ids, cos_ref, sin_ref):
    layer = pl.program_id(0)

    @pl.when(layer == 0)
    def _():
        count[0] = 0
        frame = place[0]
        cos_ref[...] = merged(ct[pl.ds(frame, 1), :], cp[...])
        sin_ref[...] = merged(st[pl.ds(frame, 1), :], sp[...])

    first = count[0]
    found = pick_heads(hc, [layer], True, ids)
    count[0] = first + found

    def group(n, put):
        cosine, sine = cos_ref[...], sin_ref[...]
        for i in range(GROUP):
            lanes = lanes_of(ids[n * GROUP + i] - layer * HEADS)
            rq = rotate(q[0, 0, :, lanes].astype(F32), cosine, sine).astype(BF16)
            rk = rotate(k[0, 0, :, lanes].astype(F32), cosine, sine).astype(BF16)
            put(first + n * GROUP + i, rq, rk, v[0, 0, :, lanes], g[0, 0, :, lanes])

    def put_own(slot, *parts):
        for a in range(4):
            out[slot, a] = parts[a]

    def put_shared(slot, rq, rk, vv, gg):
        dest = (slot - SPACES) * 2
        out[dest, 4] = rq
        out[dest, 5] = gg
        out[dest + 1, 4] = rk
        out[dest + 1, 5] = vv

    def step(n, carry):
        own = first + n * GROUP < SPACES
        pl.when(own)(lambda: group(n, put_own))
        pl.when(jnp.logical_not(own))(lambda: group(n, put_shared))
        return carry

    lax.fori_loop(0, found // GROUP, step, 0)


SMALL = pl.BlockSpec((FRAMES, W), lambda i, h, p: (0, 0))
LOCAL = pl.BlockSpec((ROWS, W), lambda i, h, p: (p[1], 0))
PACK_COST = pl.CostEstimate(flops=20_000_000, bytes_accessed=9_000_000, transcendentals=0)


def pack_spatial(meta, arrays, tabs):
    shape = (SPACES, 6, ROWS, W)
    part = pl.BlockSpec((1, 1, ROWS, HEADS * W), lambda l, h, p: (l, 0, 0, 0))
    return pl.pallas_call(
        pack_body,
        grid_spec=pltpu.PrefetchScalarGridSpec(
            num_scalar_prefetch=2,
            grid=(LAYERS,),
            in_specs=[part] * 4 + [SMALL, SMALL, LOCAL, LOCAL],
            out_specs=pl.BlockSpec(shape, lambda l, h, p: (0, 0, 0, 0)),
            scratch_shapes=[
                pltpu.SMEM((1,), jnp.int32),
                pltpu.SMEM((HEADS,), jnp.int32),
                pltpu.VMEM((ROWS, W), F32),
                pltpu.VMEM((ROWS, W), F32),
            ],
        ),
        out_shape=jax.ShapeDtypeStruct(shape, BF16),
        compiler_params=pltpu.CompilerParams(vmem_limit_bytes=VMEM),
        cost_estimate=PACK_COST,
        name="pack_spatial",
    )(*meta, *arrays, *tabs)


def peer(place, step, forward):
    frame = place[0]
    x, z = frame % 4, frame // 4
    dx, dz = step // 2, step % 2
    x = (x + (dx if forward else 4 - dx)) % 4
    return (1 - z if dz else z) * 4 + x


def pack_temporal_body(hc, place, q, k, v, g, ct, st, cp, sp, *rest):
    outs, (ids, cos_ref, sin_ref) = rest[:FRAMES], rest[FRAMES:]
    frame = place[0]
    cos_ref[...] = merged(ct[pl.ds(frame, 1), :], cp[...])
    sin_ref[...] = merged(st[pl.ds(frame, 1), :], sp[...])
    pick_heads(hc, range(LAYERS), False, ids)
    for step in range(FRAMES):
        cosine, sine = cos_ref[...], sin_ref[...]
        dest = peer(place, step, True)
        for i in range(3):
            flat_id = ids[dest * 3 + i]
            layer = flat_id // HEADS
            lanes = lanes_of(flat_id - layer * HEADS)
            out = outs[step]
            out[i * 4] = rotate(q[layer, 0, :, lanes].astype(F32), cosine, sine).astype(BF16)
            out[i * 4 + 1] = rotate(k[layer, 0, :, lanes].astype(F32), cosine, sine).astype(BF16)
            out[i * 4 + 2] = v[layer, 0, :, lanes]
            out[i * 4 + 3] = g[layer, 0, :, lanes]


def pack_temporal(meta, arrays, tabs):
    shape = (12, ROWS, W)
    return pl.pallas_call(
        pack_temporal_body,
        grid_spec=pltpu.PrefetchScalarGridSpec(
            num_scalar_prefetch=2,
            grid=(1,),
            in_specs=[whole(OUT)] * 4 + [SMALL, SMALL, LOCAL, LOCAL],
            out_specs=[whole(shape)] * FRAMES,
            scratch_shapes=[
                pltpu.SMEM((HEADS,), jnp.int32),
                pltpu.VMEM((ROWS, W), F32),
                pltpu.VMEM((ROWS, W), F32),
            ],
        ),
        out_shape=[jax.ShapeDtypeStruct(shape, BF16)] * FRAMES,
        compiler_params=pltpu.CompilerParams(vmem_limit_bytes=VMEM),
        cost_estimate=PACK_COST,
        name="pack_temporal",
    )(*meta, *arrays, *tabs)


CHUNKS = POSITIONS // KB
PAIR = KB // ROWS


def attend_body(q, k, v, g, ct, st, cp, sp, store, scratch):
    qs, ks, vs, gs, kt, qt, gt, s_a, s_b, d_a, d_b, dk, dv, dq = scratch

    def rows(j):
        return pl.ds(pl.multiple_of(j * KB, KB), KB)

    def queries(i):
        return pl.ds(pl.multiple_of(i * QB, QB), QB)

    tail = pl.ds(POSITIONS, PADDED - POSITIONS)
    qs[tail, :] = jnp.zeros((PADDED - POSITIONS, W), BF16)
    gs[tail, :] = jnp.zeros((PADDED - POSITIONS, W), BF16)

    def load(j, carry):
        two = pl.ds(j * PAIR, PAIR)
        for ref, read in ((qs, q), (vs, v), (gs, g)):
            ref[rows(j), :] = read(two).astype(F32).reshape(KB, W).astype(BF16)
        key = k(two).astype(F32).reshape(KB, W)
        ks[rows(j), :] = key.astype(BF16)
        kt[j] = key.T.astype(BF16)
        dk[rows(j), :] = jnp.zeros((KB, W), F32)
        dv[rows(j), :] = jnp.zeros((KB, W), F32)
        return carry

    lax.fori_loop(0, CHUNKS, load, 0)

    def turn(i, carry):
        qt[i] = qs[queries(i), :].astype(F32).T.astype(BF16)
        gt[i] = gs[queries(i), :].astype(F32).T.astype(BF16)
        return carry

    lax.fori_loop(0, PADDED // QB, turn, 0)

    def products(i, j, top, refs):
        s_ref, d_ref = refs
        s = jnp.dot(ks[rows(j), :], qt[i], preferred_element_type=F32)
        s_ref[rows(j), :] = s
        d_ref[rows(j), :] = jnp.dot(vs[rows(j), :], gt[i], preferred_element_type=F32)
        return jnp.maximum(top, jnp.max(s, 0, keepdims=True))

    low = jnp.full((1, QB), -jnp.inf, F32)
    zero = jnp.zeros((1, QB), F32)

    def block(i, after_i, top, refs, after_refs):
        s_ref, d_ref = refs

        def sums(j, carry):
            total, delta, after = carry
            p = jnp.exp2((s_ref[rows(j), :] - top) * SCALE2)
            total = total + jnp.sum(p, 0, keepdims=True)
            delta = delta + jnp.sum(p * d_ref[rows(j), :], 0, keepdims=True)
            return total, delta, products(after_i, j, after, after_refs)

        total, delta, after = lax.fori_loop(0, CHUNKS, sums, (zero, zero, low))
        delta = delta / total
        shift = jnp.log2(total)

        def grads(j, dqt):
            p = jnp.exp2((s_ref[rows(j), :] - top) * SCALE2 - shift)
            ds = (p * ((d_ref[rows(j), :] - delta) * SCALE)).astype(BF16)
            dv[rows(j), :] += jnp.dot(
                p.astype(BF16), gs[queries(i), :], preferred_element_type=F32
            )
            dk[rows(j), :] += jnp.dot(ds, qs[queries(i), :], preferred_element_type=F32)
            return dqt + jnp.dot(kt[j], ds, preferred_element_type=F32)

        dqt = lax.fori_loop(0, CHUNKS, grads, jnp.zeros((W, QB), F32))
        dq[queries(i), :] = dqt.T
        return after

    one, two = (s_a, d_a), (s_b, d_b)
    top = lax.fori_loop(0, CHUNKS, lambda j, t: products(0, j, t, one), low)

    def blocks(n, top):
        top = block(2 * n, 2 * n + 1, top, one, two)
        return block(2 * n + 1, jnp.minimum(2 * n + 2, PADDED // QB - 1), top, two, one)

    lax.fori_loop(0, PADDED // QB // 2, blocks, top)

    def finish(b, carry):
        at = pl.ds(pl.multiple_of(b * ROWS, ROWS), ROWS)
        cosine = merged(ct, cp[at, :])
        sine = merged(st, sp[at, :])
        store(b, unrotate(dq[at, :], cosine, sine), unrotate(dk[at, :], cosine, sine), dv[at, :])
        return carry

    lax.fori_loop(0, SPACES, finish, 0)


def attend_scratch():
    return (
        [pltpu.VMEM((PADDED, W), BF16), pltpu.VMEM((POSITIONS, W), BF16)]
        + [pltpu.VMEM((POSITIONS, W), BF16), pltpu.VMEM((PADDED, W), BF16)]
        + [pltpu.VMEM((CHUNKS, W, KB), BF16)]
        + [pltpu.VMEM((PADDED // QB, W, QB), BF16)] * 2
        + [pltpu.VMEM((POSITIONS, QB), F32)] * 4
        + [pltpu.VMEM((POSITIONS, W), F32)] * 2
        + [pltpu.VMEM((PADDED, W), F32)]
    )


def own_body(hc, place, x, kept, given, ct, st, cp, sp, out, *scratch):
    frame = pl.ds(place[0], 1)
    even = place[1] % 2 == 0

    def store(b, *grads):
        rest = jnp.where(even, kept[b].astype(F32), given[b].astype(F32))
        out[b] = jnp.concatenate(list(grads) + [rest], 0).astype(BF16)

    parts = [lambda two, a=a: x[two, a] for a in range(4)]
    attend_body(*parts, ct[frame, :], st[frame, :], cp, sp, store, scratch)


def shared_body(hc, place, mine, other, ct, st, cp, sp, out, give, *scratch):
    frame = pl.ds(place[0], 1)

    def store(b, gq, gk, gv):
        zero = jnp.zeros((2 * HALF - ROWS, W), F32)
        out[b] = jnp.concatenate([gq, gk[:HALF]], 0).astype(BF16)
        give[b] = jnp.concatenate([gv, gk[HALF:], zero], 0).astype(BF16)

    @pl.when(place[1] % 2 == 0)
    def _():
        parts = (
            lambda two: mine[two, 0],
            lambda two: other[two, 0],
            lambda two: other[two, 1],
            lambda two: mine[two, 1],
        )
        attend_body(*parts, ct[frame, :], st[frame, :], cp, sp, store, scratch)


ATTEND_COST = pl.CostEstimate(
    flops=10 * POSITIONS * POSITIONS * W,
    bytes_accessed=6_000_000,
    transcendentals=POSITIONS * POSITIONS,
)


def attend_own(meta, received, kept, given, tabs):
    shape = (SPACES, BACK, W)
    return pl.pallas_call(
        own_body,
        grid_spec=pltpu.PrefetchScalarGridSpec(
            num_scalar_prefetch=2,
            grid=(1,),
            in_specs=[whole((SPACES, 4, ROWS, W)), whole(kept.shape), whole(given.shape)]
            + [whole(t.shape) for t in tabs],
            out_specs=whole(shape),
            scratch_shapes=attend_scratch(),
        ),
        out_shape=jax.ShapeDtypeStruct(shape, BF16),
        compiler_params=pltpu.CompilerParams(vmem_limit_bytes=VMEM),
        cost_estimate=pl.CostEstimate(flops=0, bytes_accessed=6_000_000, transcendentals=0),
        name="attend_own",
    )(*meta, received, kept, given, *tabs)


def attend_shared(meta, mine, other, tabs):
    shape = (SPACES, ROWS + HALF, W)
    return pl.pallas_call(
        shared_body,
        grid_spec=pltpu.PrefetchScalarGridSpec(
            num_scalar_prefetch=2,
            grid=(1,),
            in_specs=[whole(mine.shape), whole(other.shape)] + [whole(t.shape) for t in tabs],
            out_specs=[whole(shape), whole(shape)],
            scratch_shapes=attend_scratch(),
        ),
        out_shape=[jax.ShapeDtypeStruct(shape, BF16)] * 2,
        compiler_params=pltpu.CompilerParams(vmem_limit_bytes=VMEM),
        cost_estimate=ATTEND_COST,
        name="attend_shared",
    )(*meta, mine, other, *tabs)


def frames_body(hc, place, *refs):
    xs, (ct, st, cp, sp) = refs[:FRAMES], refs[FRAMES : FRAMES + 4]
    outs, (dq_ref, dk_ref, dv_ref) = refs[FRAMES + 4 : -3], refs[-3:]
    tokens = FRAMES * TP
    key_place = lax.broadcasted_iota(jnp.int32, (tokens, tokens), 0) % TP
    query_place = lax.broadcasted_iota(jnp.int32, (tokens, tokens), 1) % TP
    same = key_place == query_place
    nt = (((1,), (1,)), ((), ()))
    owners = [peer(place, step, False) for step in range(FRAMES)]

    def head(i, carry):
        for c in range(ROWS // TP):
            rows = slice(c * TP, (c + 1) * TP)
            q, k, v, g = (
                jnp.concatenate([x[i * 4 + a].astype(F32)[rows] for x in xs], 0).astype(BF16)
                for a in range(4)
            )
            s = lax.dot_general(k, q, nt, preferred_element_type=F32)
            s = jnp.where(same, s, -jnp.inf)
            p = jnp.exp2((s - jnp.max(s, 0, keepdims=True)) * SCALE2)
            p = p * (1.0 / jnp.sum(p, 0, keepdims=True))
            d = lax.dot_general(v, g, nt, preferred_element_type=F32)
            delta = jnp.sum(p * d, 0, keepdims=True)
            ds = p * ((d - delta) * SCALE)
            dst = ds.T.astype(BF16)
            ds = ds.astype(BF16)
            gv = jnp.dot(p.astype(BF16), g, preferred_element_type=F32)
            gk = jnp.dot(ds, q, preferred_element_type=F32)
            gq = jnp.dot(dst, k, preferred_element_type=F32)
            place_c, place_s = cp[rows, :], sp[rows, :]
            cosine = jnp.concatenate([merged(ct[pl.ds(f, 1), :], place_c) for f in owners], 0)
            sine = jnp.concatenate([merged(st[pl.ds(f, 1), :], place_s) for f in owners], 0)
            dq_ref[:, rows, :] = unrotate(gq, cosine, sine).reshape(FRAMES, TP, W)
            dk_ref[:, rows, :] = unrotate(gk, cosine, sine).reshape(FRAMES, TP, W)
            dv_ref[:, rows, :] = gv.reshape(FRAMES, TP, W)
        for step, out in enumerate(outs):
            out[i * 3] = dq_ref[step].astype(BF16)
            out[i * 3 + 1] = dk_ref[step].astype(BF16)
            out[i * 3 + 2] = dv_ref[step].astype(BF16)
        return carry

    lax.fori_loop(0, 3, head, 0)


def attend_frames(meta, received, tabs):
    shape = (9, ROWS, W)
    return pl.pallas_call(
        frames_body,
        grid_spec=pltpu.PrefetchScalarGridSpec(
            num_scalar_prefetch=2,
            grid=(1,),
            in_specs=[whole(x.shape) for x in received] + [SMALL, SMALL, LOCAL, LOCAL],
            out_specs=[whole(shape)] * FRAMES,
            scratch_shapes=[pltpu.VMEM((FRAMES, ROWS, W), F32)] * 3,
        ),
        out_shape=[jax.ShapeDtypeStruct(shape, BF16)] * FRAMES,
        compiler_params=pltpu.CompilerParams(vmem_limit_bytes=VMEM),
        cost_estimate=pl.CostEstimate(
            flops=2_000_000_000, bytes_accessed=6_000_000, transcendentals=600_000
        ),
        name="attend_frames",
    )(*meta, *received, *tabs)


def unpack_spatial_body(hc, place, x, oq, ok, ov, count):
    count[0] = 0

    def head(i, carry):
        layer = i // HEADS
        h = i - layer * HEADS

        @pl.when(hc[layer, h] == 0)
        def _():
            slot = count[0]
            count[0] = slot + 1
            lanes = pl.ds(pl.multiple_of(h * W, W), W)

            @pl.when(slot < SPACES)
            def _():
                piece = x[slot].astype(F32)
                oq[layer, 0, :, lanes] = piece[:ROWS].astype(BF16)
                ok[layer, 0, :, lanes] = piece[ROWS : 2 * ROWS].astype(BF16)
                ov[layer, 0, :, lanes] = piece[2 * ROWS : 3 * ROWS].astype(BF16)

            @pl.when(slot >= SPACES)
            def _():
                first = (slot - SPACES) * 2
                one = x[first].astype(F32)
                two = x[first + 1].astype(F32)
                oq[layer, 0, :, lanes] = one[3 * ROWS : 4 * ROWS].astype(BF16)
                ov[layer, 0, :, lanes] = two[3 * ROWS : 4 * ROWS].astype(BF16)
                both = jnp.concatenate([one[4 * ROWS :], two[4 * ROWS : 5 * ROWS - HALF]], 0)
                ok[layer, 0, :, lanes] = both.astype(BF16)

        return carry

    lax.fori_loop(0, LAYERS * HEADS, head, 0)


def unpack_spatial(meta, returned):
    return pl.pallas_call(
        unpack_spatial_body,
        grid_spec=pltpu.PrefetchScalarGridSpec(
            num_scalar_prefetch=2,
            grid=(1,),
            in_specs=[whole(returned.shape)],
            out_specs=[whole(OUT)] * 3,
            scratch_shapes=[pltpu.SMEM((1,), jnp.int32)],
        ),
        out_shape=[jax.ShapeDtypeStruct(OUT, BF16)] * 3,
        compiler_params=pltpu.CompilerParams(vmem_limit_bytes=VMEM),
        cost_estimate=pl.CostEstimate(flops=5_000_000, bytes_accessed=7_000_000, transcendentals=0),
        name="unpack_spatial",
    )(*meta, returned)


def unpack_temporal_body(hc, place, *refs):
    xs, outs, (ids, sems) = refs[:FRAMES], refs[FRAMES + 3 : FRAMES + 6], refs[FRAMES + 6 :]
    pick_heads(hc, range(LAYERS), False, ids)
    copies = []
    for step in range(FRAMES):
        dest = peer(place, step, True)
        for i in range(3):
            flat_id = ids[dest * 3 + i]
            layer = flat_id // HEADS
            lanes = lanes_of(flat_id - layer * HEADS)
            for a in range(3):
                copies.append(
                    pltpu.make_async_copy(
                        xs[step].at[i * 3 + a],
                        outs[a].at[layer, 0, :, lanes],
                        sems.at[step * 3 + i, a],
                    )
                )
                copies[-1].start()
    for copy in copies:
        copy.wait()


def unpack_temporal(meta, returned, partial):
    anywhere = pl.BlockSpec(memory_space=pl.ANY)
    return pl.pallas_call(
        unpack_temporal_body,
        grid_spec=pltpu.PrefetchScalarGridSpec(
            num_scalar_prefetch=2,
            grid=(1,),
            in_specs=[whole(x.shape) for x in returned] + [anywhere] * 3,
            out_specs=[anywhere] * 3,
            scratch_shapes=[
                pltpu.SMEM((HEADS,), jnp.int32),
                pltpu.SemaphoreType.DMA((HEADS, 3)),
            ],
        ),
        out_shape=[jax.ShapeDtypeStruct(OUT, BF16)] * 3,
        input_output_aliases={2 + FRAMES + a: a for a in range(3)},
        compiler_params=pltpu.CompilerParams(vmem_limit_bytes=VMEM),
        cost_estimate=pl.CostEstimate(flops=0, bytes_accessed=5_000_000, transcendentals=0),
        name="unpack_temporal",
    )(*meta, *returned, *partial)


def exchange(x):
    return lax.all_to_all(x, "space", split_axis=0, concat_axis=0, tiled=True)


SWAP = [(i, i ^ 1) for i in range(SPACES)]


def along_x(parts, sign):
    def move(step, part):
        dx = sign * (step // 2)
        if dx == 0:
            return part
        pairs = [(f, f // 4 * 4 + (f + dx) % 4) for f in range(FRAMES)]
        return lax.ppermute(part, "frame", pairs)

    return [move(step, part) for step, part in enumerate(parts)]


def along_z(parts):
    pairs = [(f, f ^ 4) for f in range(FRAMES)]
    return [lax.ppermute(x, "frame", pairs) if n % 2 else x for n, x in enumerate(parts)]


def on_device(queries, keys, values, grad_out, head_class):
    place = jnp.stack([lax.axis_index("frame"), lax.axis_index("space")]).astype(jnp.int32)
    meta = (head_class, place)
    tabs = tuple(jnp.asarray(t) for t in tables())
    arrays = (queries, keys, values, grad_out)
    got_s = exchange(pack_spatial(meta, arrays, tabs))
    half_t = along_x(pack_temporal(meta, arrays, tabs), 1)
    got_s, *half_t = lax.optimization_barrier((got_s, *half_t))
    got_t = along_z(half_t)
    mine = got_s[:, 4:6]
    other = lax.ppermute(mine, "space", SWAP)
    kept, give = attend_shared(meta, mine, other, tabs)
    given = lax.ppermute(give, "space", SWAP)
    back_s = attend_own(meta, got_s, kept, given, tabs)
    back_s, *got_t = lax.optimization_barrier((back_s, *got_t))
    home_s = exchange(back_s)
    home_t = along_z(along_x(attend_frames(meta, got_t, tabs), -1))
    partial = unpack_spatial(meta, home_s)
    return tuple(unpack_temporal(meta, home_t, partial))


def solution(mesh):
    placed = P(None, "frame", "space", None)
    return jax.shard_map(
        on_device,
        mesh=mesh,
        in_specs=(placed, placed, placed, placed, P()),
        out_specs=(placed, placed, placed),
        check_vma=False,
    )
```

```python
import math

import jax
import jax.numpy as jnp
import numpy as np
from jax import lax
from jax.experimental import pallas as pl
from jax.experimental.pallas import tpu as pltpu
from jax.sharding import PartitionSpec as P

RT = 16
RS = 56
PW = 80
THETA = 256.0
W = RT + 2 * RS
HEADS = 24
LAYERS = 2
FRAMES = 8
SPACES = 16
ROWS = 120
POSITIONS = SPACES * ROWS
HALF = 64
BACK = 4 * ROWS + HALF
QB = 512
PADDED = 2048
KB = 480
STRIP = 16
TP = 24
GROUP = 4
VMEM = 60 * 1024 * 1024
SCALE = 1.0 / math.sqrt(W)
SCALE2 = SCALE * math.log2(math.e)
F32 = jnp.float32
BF16 = jnp.bfloat16


OUT = (LAYERS, 1, ROWS, HEADS * W)


def whole(shape):
    return pl.BlockSpec(shape, lambda i, h, p: (0,) * len(shape))


def tables():
    channel = np.arange(W)
    pair = channel // 2
    tpairs, spairs = RT // 2, RS // 2
    is_time = pair < tpairs
    is_row = (pair >= tpairs) & (pair < tpairs + spairs)
    local = np.where(is_time, pair, np.where(is_row, pair - tpairs, pair - tpairs - spairs))
    width = np.where(is_time, RT, RS)
    freq = THETA ** (-2.0 * local / width)
    sign = np.where(channel % 2 == 0, -1.0, 1.0)
    time = np.arange(FRAMES)[:, None] * freq
    position = np.arange(POSITIONS)[:, None]
    place = np.where(is_row, position // PW, position % PW) * freq
    return (
        np.cos(time).astype(np.float32),
        (np.sin(time) * sign).astype(np.float32),
        np.cos(place).astype(np.float32),
        (np.sin(place) * sign).astype(np.float32),
    )


def lane_ids(shape):
    return lax.broadcasted_iota(jnp.int32, shape, len(shape) - 1)


def swapped(x):
    row = lax.broadcasted_iota(jnp.int32, (W, W), 0)
    column = lax.broadcasted_iota(jnp.int32, (W, W), 1)
    pairs = jnp.where((row ^ 1) == column, 1.0, 0.0).astype(BF16)
    return jnp.dot(x.astype(BF16), pairs, preferred_element_type=F32)


def merged(time_row, place_rows):
    return jnp.where(lane_ids(place_rows.shape) < RT, time_row, place_rows)


def rotate(x, cosine, sine):
    return x * cosine + swapped(x) * sine


def unrotate(x, cosine, sine):
    x = x.astype(BF16).astype(F32)
    return x * cosine - swapped(x) * sine


def pick_heads(hc, layers, spatial, ids):
    def look(h, n, layer):
        mine = (hc[layer, h] == 0) == spatial

        @pl.when(mine)
        def _():
            ids[n] = layer * HEADS + h

        return n + mine.astype(jnp.int32)

    found = jnp.int32(0)
    for layer in layers:
        found = lax.fori_loop(0, HEADS, lambda h, n: look(h, n, layer), found)
    return found


def lanes_of(h):
    return pl.ds(pl.multiple_of(h * W, W), W)


def pack_body(hc, place, q, k, v, g, ct, st, cp, sp, out, count, ids, cos_ref, sin_ref):
    layer = pl.program_id(0)

    @pl.when(layer == 0)
    def _():
        count[0] = 0
        frame = place[0]
        cos_ref[...] = merged(ct[pl.ds(frame, 1), :], cp[...])
        sin_ref[...] = merged(st[pl.ds(frame, 1), :], sp[...])

    first = count[0]
    found = pick_heads(hc, [layer], True, ids)
    count[0] = first + found

    def group(n, put):
        cosine, sine = cos_ref[...], sin_ref[...]
        for i in range(GROUP):
            lanes = lanes_of(ids[n * GROUP + i] - layer * HEADS)
            rq = rotate(q[0, 0, :, lanes].astype(F32), cosine, sine).astype(BF16)
            rk = rotate(k[0, 0, :, lanes].astype(F32), cosine, sine).astype(BF16)
            put(first + n * GROUP + i, rq, rk, v[0, 0, :, lanes], g[0, 0, :, lanes])

    def put_own(slot, *parts):
        for a in range(4):
            out[slot, a] = parts[a]

    def put_shared(slot, rq, rk, vv, gg):
        dest = (slot - SPACES) * 2
        out[dest, 4] = rq
        out[dest, 5] = gg
        out[dest + 1, 4] = rk
        out[dest + 1, 5] = vv

    def step(n, carry):
        own = first + n * GROUP < SPACES
        pl.when(own)(lambda: group(n, put_own))
        pl.when(jnp.logical_not(own))(lambda: group(n, put_shared))
        return carry

    lax.fori_loop(0, found // GROUP, step, 0)


SMALL = pl.BlockSpec((FRAMES, W), lambda i, h, p: (0, 0))
LOCAL = pl.BlockSpec((ROWS, W), lambda i, h, p: (p[1], 0))
PACK_COST = pl.CostEstimate(flops=20_000_000, bytes_accessed=9_000_000, transcendentals=0)


def pack_spatial(meta, arrays, tabs):
    shape = (SPACES, 6, ROWS, W)
    part = pl.BlockSpec((1, 1, ROWS, HEADS * W), lambda l, h, p: (l, 0, 0, 0))
    return pl.pallas_call(
        pack_body,
        grid_spec=pltpu.PrefetchScalarGridSpec(
            num_scalar_prefetch=2,
            grid=(LAYERS,),
            in_specs=[part] * 4 + [SMALL, SMALL, LOCAL, LOCAL],
            out_specs=pl.BlockSpec(shape, lambda l, h, p: (0, 0, 0, 0)),
            scratch_shapes=[
                pltpu.SMEM((1,), jnp.int32),
                pltpu.SMEM((HEADS,), jnp.int32),
                pltpu.VMEM((ROWS, W), F32),
                pltpu.VMEM((ROWS, W), F32),
            ],
        ),
        out_shape=jax.ShapeDtypeStruct(shape, BF16),
        compiler_params=pltpu.CompilerParams(vmem_limit_bytes=VMEM),
        cost_estimate=PACK_COST,
        name="pack_spatial",
    )(*meta, *arrays, *tabs)


def peer(place, step, forward):
    frame = place[0]
    x, z = frame % 4, frame // 4
    dx, dz = step // 2, step % 2
    x = (x + (dx if forward else 4 - dx)) % 4
    return (1 - z if dz else z) * 4 + x


def pack_temporal_body(hc, place, q, k, v, g, ct, st, cp, sp, *rest):
    outs, (ids, cos_ref, sin_ref) = rest[:FRAMES], rest[FRAMES:]
    frame = place[0]
    cos_ref[...] = merged(ct[pl.ds(frame, 1), :], cp[...])
    sin_ref[...] = merged(st[pl.ds(frame, 1), :], sp[...])
    pick_heads(hc, range(LAYERS), False, ids)
    for step in range(FRAMES):
        cosine, sine = cos_ref[...], sin_ref[...]
        dest = peer(place, step, True)
        for i in range(3):
            flat_id = ids[dest * 3 + i]
            layer = flat_id // HEADS
            lanes = lanes_of(flat_id - layer * HEADS)
            out = outs[step]
            out[i * 4] = rotate(q[layer, 0, :, lanes].astype(F32), cosine, sine).astype(BF16)
            out[i * 4 + 1] = rotate(k[layer, 0, :, lanes].astype(F32), cosine, sine).astype(BF16)
            out[i * 4 + 2] = v[layer, 0, :, lanes]
            out[i * 4 + 3] = g[layer, 0, :, lanes]


def pack_temporal(meta, arrays, tabs):
    shape = (12, ROWS, W)
    return pl.pallas_call(
        pack_temporal_body,
        grid_spec=pltpu.PrefetchScalarGridSpec(
            num_scalar_prefetch=2,
            grid=(1,),
            in_specs=[whole(OUT)] * 4 + [SMALL, SMALL, LOCAL, LOCAL],
            out_specs=[whole(shape)] * FRAMES,
            scratch_shapes=[
                pltpu.SMEM((HEADS,), jnp.int32),
                pltpu.VMEM((ROWS, W), F32),
                pltpu.VMEM((ROWS, W), F32),
            ],
        ),
        out_shape=[jax.ShapeDtypeStruct(shape, BF16)] * FRAMES,
        compiler_params=pltpu.CompilerParams(vmem_limit_bytes=VMEM),
        cost_estimate=PACK_COST,
        name="pack_temporal",
    )(*meta, *arrays, *tabs)


CHUNKS = POSITIONS // KB
PAIR = KB // ROWS


def attend_body(q, k, v, g, ct, st, cp, sp, store, scratch):
    qs, ks, vs, gs, kt, qt, gt, s_a, s_b, d_a, d_b, dk, dv, dq, dqt, p_ref, ds_ref = scratch

    def rows(j):
        return pl.ds(pl.multiple_of(j * KB, KB), KB)

    def queries(i):
        return pl.ds(pl.multiple_of(i * QB, QB), QB)

    tail = pl.ds(POSITIONS, PADDED - POSITIONS)
    qs[tail, :] = jnp.zeros((PADDED - POSITIONS, W), BF16)
    gs[tail, :] = jnp.zeros((PADDED - POSITIONS, W), BF16)

    def load(j, carry):
        two = pl.ds(j * PAIR, PAIR)
        for ref, read in ((qs, q), (vs, v), (gs, g)):
            ref[rows(j), :] = read(two).astype(F32).reshape(KB, W).astype(BF16)
        key = k(two).astype(F32).reshape(KB, W)
        ks[rows(j), :] = key.astype(BF16)
        kt[j] = key.T.astype(BF16)
        dk[rows(j), :] = jnp.zeros((KB, W), F32)
        dv[rows(j), :] = jnp.zeros((KB, W), F32)
        return carry

    lax.fori_loop(0, CHUNKS, load, 0)

    def turn(i, carry):
        qt[i] = qs[queries(i), :].astype(F32).T.astype(BF16)
        gt[i] = gs[queries(i), :].astype(F32).T.astype(BF16)
        return carry

    lax.fori_loop(0, PADDED // QB, turn, 0)

    def products(i, j, refs):
        s_ref, d_ref = refs
        s_ref[rows(j), :] = jnp.dot(ks[rows(j), :], qt[i], preferred_element_type=F32)
        d_ref[rows(j), :] = jnp.dot(vs[rows(j), :], gt[i], preferred_element_type=F32)

    def strips(j):
        return [pl.ds(pl.multiple_of(j * KB + r, STRIP), STRIP) for r in range(0, KB, STRIP)]

    def fold(op, total, strip):
        for r in range(0, STRIP, 8):
            total = op(total, strip[r : r + 8])
        return total

    def highest(j, top, refs):
        for at in strips(j):
            top = fold(jnp.maximum, top, refs[0][at, :])
        return top

    low = jnp.full((8, QB), -jnp.inf, F32)
    zero = jnp.zeros((8, QB), F32)

    def block(i, after_i, top, refs, after_refs):
        s_ref, d_ref = refs
        top = jnp.max(top, 0, keepdims=True) * SCALE2

        def sums(j, carry):
            total, delta = carry
            products(after_i, j, after_refs)
            for at in strips(j):
                p = jnp.exp2(s_ref[at, :] * SCALE2 - top)
                total = fold(jnp.add, total, p)
                delta = fold(jnp.add, delta, p * d_ref[at, :])
            return total, delta

        total, delta = lax.fori_loop(0, CHUNKS, sums, (zero, zero))
        total = jnp.sum(total, 0, keepdims=True)
        delta = jnp.sum(delta, 0, keepdims=True) / total * SCALE
        shift = top + jnp.log2(total)
        dqt[...] = jnp.zeros_like(dqt)

        def grads(j, after):
            for r, at in enumerate(strips(j)):
                p = jnp.exp2(s_ref[at, :] * SCALE2 - shift)
                ds = p * (d_ref[at, :] * SCALE - delta)
                to = slice(r * STRIP, (r + 1) * STRIP)
                p_ref[to, :] = p.astype(BF16)
                ds_ref[to, :] = ds.astype(BF16)
            dv[rows(j), :] += jnp.dot(p_ref[...], gs[queries(i), :], preferred_element_type=F32)
            dk[rows(j), :] += jnp.dot(ds_ref[...], qs[queries(i), :], preferred_element_type=F32)
            dqt[...] += jnp.dot(kt[j], ds_ref[...], preferred_element_type=F32)
            return highest(j, after, after_refs)

        after = lax.fori_loop(0, CHUNKS, grads, low)
        dq[queries(i), :] = dqt[...].T
        return after

    one, two = (s_a, d_a), (s_b, d_b)

    def start(j, top):
        products(0, j, one)
        return highest(j, top, one)

    def blocks(n, top):
        top = block(2 * n, 2 * n + 1, top, one, two)
        return block(2 * n + 1, jnp.minimum(2 * n + 2, PADDED // QB - 1), top, two, one)

    lax.fori_loop(0, PADDED // QB // 2, blocks, lax.fori_loop(0, CHUNKS, start, low))

    def finish(n, carry):
        for b in [n * 4 + u for u in range(4)]:
            at = pl.ds(pl.multiple_of(b * ROWS, ROWS), ROWS)
            cosine = merged(ct, cp[at, :])
            sine = merged(st, sp[at, :])
            gq = unrotate(dq[at, :], cosine, sine)
            store(b, gq, unrotate(dk[at, :], cosine, sine), dv[at, :])
        return carry

    lax.fori_loop(0, SPACES // 4, finish, 0)


def attend_scratch():
    return (
        [pltpu.VMEM((PADDED, W), BF16), pltpu.VMEM((POSITIONS, W), BF16)]
        + [pltpu.VMEM((POSITIONS, W), BF16), pltpu.VMEM((PADDED, W), BF16)]
        + [pltpu.VMEM((CHUNKS, W, KB), BF16)]
        + [pltpu.VMEM((PADDED // QB, W, QB), BF16)] * 2
        + [pltpu.VMEM((POSITIONS, QB), F32)] * 4
        + [pltpu.VMEM((POSITIONS, W), F32)] * 2
        + [pltpu.VMEM((PADDED, W), F32), pltpu.VMEM((W, QB), F32)]
        + [pltpu.VMEM((KB, QB), BF16)] * 2
    )


def own_body(hc, place, x, kept, given, ct, st, cp, sp, out, *scratch):
    frame = pl.ds(place[0], 1)
    even = place[1] % 2 == 0

    def store(b, *grads):
        rest = jnp.where(even, kept[b].astype(F32), given[b].astype(F32))
        out[b] = jnp.concatenate(list(grads) + [rest], 0).astype(BF16)

    parts = [lambda two, a=a: x[two, a] for a in range(4)]
    attend_body(*parts, ct[frame, :], st[frame, :], cp, sp, store, scratch)


def shared_body(hc, place, mine, other, ct, st, cp, sp, out, give, *scratch):
    frame = pl.ds(place[0], 1)

    def store(b, gq, gk, gv):
        zero = jnp.zeros((2 * HALF - ROWS, W), F32)
        out[b] = jnp.concatenate([gq, gk[:HALF]], 0).astype(BF16)
        give[b] = jnp.concatenate([gv, gk[HALF:], zero], 0).astype(BF16)

    @pl.when(place[1] % 2 == 0)
    def _():
        parts = (
            lambda two: mine[two, 0],
            lambda two: other[two, 0],
            lambda two: other[two, 1],
            lambda two: mine[two, 1],
        )
        attend_body(*parts, ct[frame, :], st[frame, :], cp, sp, store, scratch)


ATTEND_COST = pl.CostEstimate(
    flops=10 * POSITIONS * POSITIONS * W,
    bytes_accessed=6_000_000,
    transcendentals=POSITIONS * POSITIONS,
)


def attend_own(meta, received, kept, given, tabs):
    shape = (SPACES, BACK, W)
    return pl.pallas_call(
        own_body,
        grid_spec=pltpu.PrefetchScalarGridSpec(
            num_scalar_prefetch=2,
            grid=(1,),
            in_specs=[whole((SPACES, 4, ROWS, W)), whole(kept.shape), whole(given.shape)]
            + [whole(t.shape) for t in tabs],
            out_specs=whole(shape),
            scratch_shapes=attend_scratch(),
        ),
        out_shape=jax.ShapeDtypeStruct(shape, BF16),
        compiler_params=pltpu.CompilerParams(vmem_limit_bytes=VMEM),
        cost_estimate=pl.CostEstimate(flops=0, bytes_accessed=6_000_000, transcendentals=0),
        name="attend_own",
    )(*meta, received, kept, given, *tabs)


def attend_shared(meta, mine, other, tabs):
    shape = (SPACES, ROWS + HALF, W)
    return pl.pallas_call(
        shared_body,
        grid_spec=pltpu.PrefetchScalarGridSpec(
            num_scalar_prefetch=2,
            grid=(1,),
            in_specs=[whole(mine.shape), whole(other.shape)] + [whole(t.shape) for t in tabs],
            out_specs=[whole(shape), whole(shape)],
            scratch_shapes=attend_scratch(),
        ),
        out_shape=[jax.ShapeDtypeStruct(shape, BF16)] * 2,
        compiler_params=pltpu.CompilerParams(vmem_limit_bytes=VMEM),
        cost_estimate=ATTEND_COST,
        name="attend_shared",
    )(*meta, mine, other, *tabs)


def frames_body(hc, place, *refs):
    xs, (ct, st, cp, sp) = refs[:FRAMES], refs[FRAMES : FRAMES + 4]
    outs, (dq_ref, dk_ref, dv_ref) = refs[FRAMES + 4 : -3], refs[-3:]
    tokens = FRAMES * TP
    key_place = lax.broadcasted_iota(jnp.int32, (tokens, tokens), 0) % TP
    query_place = lax.broadcasted_iota(jnp.int32, (tokens, tokens), 1) % TP
    same = key_place == query_place
    nt = (((1,), (1,)), ((), ()))
    owners = [peer(place, step, False) for step in range(FRAMES)]

    def head(i, carry):
        for c in range(ROWS // TP):
            rows = slice(c * TP, (c + 1) * TP)
            q, k, v, g = (
                jnp.concatenate([x[i * 4 + a].astype(F32)[rows] for x in xs], 0).astype(BF16)
                for a in range(4)
            )
            s = lax.dot_general(k, q, nt, preferred_element_type=F32)
            s = jnp.where(same, s, -jnp.inf)
            p = jnp.exp2((s - jnp.max(s, 0, keepdims=True)) * SCALE2)
            p = p * (1.0 / jnp.sum(p, 0, keepdims=True))
            d = lax.dot_general(v, g, nt, preferred_element_type=F32)
            delta = jnp.sum(p * d, 0, keepdims=True)
            ds = p * ((d - delta) * SCALE)
            dst = ds.T.astype(BF16)
            ds = ds.astype(BF16)
            gv = jnp.dot(p.astype(BF16), g, preferred_element_type=F32)
            gk = jnp.dot(ds, q, preferred_element_type=F32)
            gq = jnp.dot(dst, k, preferred_element_type=F32)
            place_c, place_s = cp[rows, :], sp[rows, :]
            cosine = jnp.concatenate([merged(ct[pl.ds(f, 1), :], place_c) for f in owners], 0)
            sine = jnp.concatenate([merged(st[pl.ds(f, 1), :], place_s) for f in owners], 0)
            dq_ref[:, rows, :] = unrotate(gq, cosine, sine).reshape(FRAMES, TP, W)
            dk_ref[:, rows, :] = unrotate(gk, cosine, sine).reshape(FRAMES, TP, W)
            dv_ref[:, rows, :] = gv.reshape(FRAMES, TP, W)
        for step, out in enumerate(outs):
            out[i * 3] = dq_ref[step].astype(BF16)
            out[i * 3 + 1] = dk_ref[step].astype(BF16)
            out[i * 3 + 2] = dv_ref[step].astype(BF16)
        return carry

    lax.fori_loop(0, 3, head, 0)


def attend_frames(meta, received, tabs):
    shape = (9, ROWS, W)
    return pl.pallas_call(
        frames_body,
        grid_spec=pltpu.PrefetchScalarGridSpec(
            num_scalar_prefetch=2,
            grid=(1,),
            in_specs=[whole(x.shape) for x in received] + [SMALL, SMALL, LOCAL, LOCAL],
            out_specs=[whole(shape)] * FRAMES,
            scratch_shapes=[pltpu.VMEM((FRAMES, ROWS, W), F32)] * 3,
        ),
        out_shape=[jax.ShapeDtypeStruct(shape, BF16)] * FRAMES,
        compiler_params=pltpu.CompilerParams(vmem_limit_bytes=VMEM),
        cost_estimate=pl.CostEstimate(
            flops=2_000_000_000, bytes_accessed=6_000_000, transcendentals=600_000
        ),
        name="attend_frames",
    )(*meta, *received, *tabs)


def unpack_spatial_body(hc, place, x, oq, ok, ov, count):
    count[0] = 0

    def head(i, carry):
        layer = i // HEADS
        h = i - layer * HEADS

        @pl.when(hc[layer, h] == 0)
        def _():
            slot = count[0]
            count[0] = slot + 1
            lanes = pl.ds(pl.multiple_of(h * W, W), W)

            @pl.when(slot < SPACES)
            def _():
                piece = x[slot].astype(F32)
                oq[layer, 0, :, lanes] = piece[:ROWS].astype(BF16)
                ok[layer, 0, :, lanes] = piece[ROWS : 2 * ROWS].astype(BF16)
                ov[layer, 0, :, lanes] = piece[2 * ROWS : 3 * ROWS].astype(BF16)

            @pl.when(slot >= SPACES)
            def _():
                first = (slot - SPACES) * 2
                one = x[first].astype(F32)
                two = x[first + 1].astype(F32)
                oq[layer, 0, :, lanes] = one[3 * ROWS : 4 * ROWS].astype(BF16)
                ov[layer, 0, :, lanes] = two[3 * ROWS : 4 * ROWS].astype(BF16)
                both = jnp.concatenate([one[4 * ROWS :], two[4 * ROWS : 5 * ROWS - HALF]], 0)
                ok[layer, 0, :, lanes] = both.astype(BF16)

        return carry

    lax.fori_loop(0, LAYERS * HEADS, head, 0)


def unpack_spatial(meta, returned):
    return pl.pallas_call(
        unpack_spatial_body,
        grid_spec=pltpu.PrefetchScalarGridSpec(
            num_scalar_prefetch=2,
            grid=(1,),
            in_specs=[whole(returned.shape)],
            out_specs=[whole(OUT)] * 3,
            scratch_shapes=[pltpu.SMEM((1,), jnp.int32)],
        ),
        out_shape=[jax.ShapeDtypeStruct(OUT, BF16)] * 3,
        compiler_params=pltpu.CompilerParams(vmem_limit_bytes=VMEM),
        cost_estimate=pl.CostEstimate(flops=5_000_000, bytes_accessed=7_000_000, transcendentals=0),
        name="unpack_spatial",
    )(*meta, returned)


def unpack_temporal_body(hc, place, *refs):
    xs, outs, (ids, sems) = refs[:FRAMES], refs[FRAMES + 3 : FRAMES + 6], refs[FRAMES + 6 :]
    pick_heads(hc, range(LAYERS), False, ids)
    copies = []
    for step in range(FRAMES):
        dest = peer(place, step, True)
        for i in range(3):
            flat_id = ids[dest * 3 + i]
            layer = flat_id // HEADS
            lanes = lanes_of(flat_id - layer * HEADS)
            for a in range(3):
                copies.append(
                    pltpu.make_async_copy(
                        xs[step].at[i * 3 + a],
                        outs[a].at[layer, 0, :, lanes],
                        sems.at[step * 3 + i, a],
                    )
                )
                copies[-1].start()
    for copy in copies:
        copy.wait()


def unpack_temporal(meta, returned, partial):
    anywhere = pl.BlockSpec(memory_space=pl.ANY)
    return pl.pallas_call(
        unpack_temporal_body,
        grid_spec=pltpu.PrefetchScalarGridSpec(
            num_scalar_prefetch=2,
            grid=(1,),
            in_specs=[whole(x.shape) for x in returned] + [anywhere] * 3,
            out_specs=[anywhere] * 3,
            scratch_shapes=[
                pltpu.SMEM((HEADS,), jnp.int32),
                pltpu.SemaphoreType.DMA((HEADS, 3)),
            ],
        ),
        out_shape=[jax.ShapeDtypeStruct(OUT, BF16)] * 3,
        input_output_aliases={2 + FRAMES + a: a for a in range(3)},
        compiler_params=pltpu.CompilerParams(vmem_limit_bytes=VMEM),
        cost_estimate=pl.CostEstimate(flops=0, bytes_accessed=5_000_000, transcendentals=0),
        name="unpack_temporal",
    )(*meta, *returned, *partial)


def exchange(x):
    return lax.all_to_all(x, "space", split_axis=0, concat_axis=0, tiled=True)


SWAP = [(i, i ^ 1) for i in range(SPACES)]


def along_x(parts, sign):
    def move(step, part):
        dx = sign * (step // 2)
        if dx == 0:
            return part
        pairs = [(f, f // 4 * 4 + (f + dx) % 4) for f in range(FRAMES)]
        return lax.ppermute(part, "frame", pairs)

    return [move(step, part) for step, part in enumerate(parts)]


def along_z(parts):
    pairs = [(f, f ^ 4) for f in range(FRAMES)]
    return [lax.ppermute(x, "frame", pairs) if n % 2 else x for n, x in enumerate(parts)]


def on_device(queries, keys, values, grad_out, head_class):
    place = jnp.stack([lax.axis_index("frame"), lax.axis_index("space")]).astype(jnp.int32)
    meta = (head_class, place)
    tabs = tuple(jnp.asarray(t) for t in tables())
    arrays = (queries, keys, values, grad_out)
    got_s = exchange(pack_spatial(meta, arrays, tabs))
    half_t = along_x(pack_temporal(meta, arrays, tabs), 1)
    got_s, *half_t = lax.optimization_barrier((got_s, *half_t))
    got_t = along_z(half_t)
    mine = got_s[:, 4:6]
    other = lax.ppermute(mine, "space", SWAP)
    kept, give = attend_shared(meta, mine, other, tabs)
    kept, give, got_t[1], got_t[3] = lax.optimization_barrier((kept, give, got_t[1], got_t[3]))
    given = lax.ppermute(give, "space", SWAP)
    back_s = attend_own(meta, got_s, kept, given, tabs)
    back_s, *got_t = lax.optimization_barrier((back_s, *got_t))
    home_s = exchange(back_s)
    home_t = along_x(along_z(attend_frames(meta, got_t, tabs)), -1)
    partial = unpack_spatial(meta, home_s)
    return tuple(unpack_temporal(meta, home_t, partial))


def solution(mesh):
    placed = P(None, "frame", "space", None)
    return jax.shard_map(
        on_device,
        mesh=mesh,
        in_specs=(placed, placed, placed, placed, P()),
        out_specs=(placed, placed, placed),
        check_vma=False,
    )
```

```python
import math

import jax
import jax.numpy as jnp
import numpy as np
from jax import lax
from jax.experimental import pallas as pl
from jax.experimental.pallas import tpu as pltpu
from jax.sharding import PartitionSpec as P

RT = 16
RS = 56
PW = 80
THETA = 256.0
W = RT + 2 * RS
HEADS = 24
LAYERS = 2
FRAMES = 8
SPACES = 16
ROWS = 120
POSITIONS = SPACES * ROWS
HALF = 64
BACK = 4 * ROWS + HALF
QB = 512
PADDED = 2048
KB = 240
STRIP = 16
TP = 24
GROUP = 4
VMEM = 60 * 1024 * 1024
SCALE = 1.0 / math.sqrt(W)
SCALE2 = SCALE * math.log2(math.e)
F32 = jnp.float32
BF16 = jnp.bfloat16


OUT = (LAYERS, 1, ROWS, HEADS * W)


def whole(shape):
    return pl.BlockSpec(shape, lambda i, h, p: (0,) * len(shape))


def tables():
    channel = np.arange(W)
    pair = channel // 2
    tpairs, spairs = RT // 2, RS // 2
    is_time = pair < tpairs
    is_row = (pair >= tpairs) & (pair < tpairs + spairs)
    local = np.where(is_time, pair, np.where(is_row, pair - tpairs, pair - tpairs - spairs))
    width = np.where(is_time, RT, RS)
    freq = THETA ** (-2.0 * local / width)
    sign = np.where(channel % 2 == 0, -1.0, 1.0)
    time = np.arange(FRAMES)[:, None] * freq
    position = np.arange(POSITIONS)[:, None]
    place = np.where(is_row, position // PW, position % PW) * freq
    return (
        np.cos(time).astype(np.float32),
        (np.sin(time) * sign).astype(np.float32),
        np.cos(place).astype(np.float32),
        (np.sin(place) * sign).astype(np.float32),
    )


def lane_ids(shape):
    return lax.broadcasted_iota(jnp.int32, shape, len(shape) - 1)


def swapped(x):
    row = lax.broadcasted_iota(jnp.int32, (W, W), 0)
    column = lax.broadcasted_iota(jnp.int32, (W, W), 1)
    pairs = jnp.where((row ^ 1) == column, 1.0, 0.0).astype(BF16)
    return jnp.dot(x.astype(BF16), pairs, preferred_element_type=F32)


def merged(time_row, place_rows):
    return jnp.where(lane_ids(place_rows.shape) < RT, time_row, place_rows)


def rotate(x, cosine, sine):
    return x * cosine + swapped(x) * sine


def unrotate(x, cosine, sine):
    x = x.astype(BF16).astype(F32)
    return x * cosine - swapped(x) * sine


def pick_heads(hc, layers, spatial, ids):
    def look(h, n, layer):
        mine = (hc[layer, h] == 0) == spatial

        @pl.when(mine)
        def _():
            ids[n] = layer * HEADS + h

        return n + mine.astype(jnp.int32)

    found = jnp.int32(0)
    for layer in layers:
        found = lax.fori_loop(0, HEADS, lambda h, n: look(h, n, layer), found)
    return found


def lanes_of(h):
    return pl.ds(pl.multiple_of(h * W, W), W)


def pack_body(hc, place, q, k, v, g, ct, st, cp, sp, out, count, ids, cos_ref, sin_ref):
    layer = pl.program_id(0)

    @pl.when(layer == 0)
    def _():
        count[0] = 0
        frame = place[0]
        cos_ref[...] = merged(ct[pl.ds(frame, 1), :], cp[...])
        sin_ref[...] = merged(st[pl.ds(frame, 1), :], sp[...])

    first = count[0]
    found = pick_heads(hc, [layer], True, ids)
    count[0] = first + found

    def group(n, put):
        cosine, sine = cos_ref[...], sin_ref[...]
        for i in range(GROUP):
            lanes = lanes_of(ids[n * GROUP + i] - layer * HEADS)
            rq = rotate(q[0, 0, :, lanes].astype(F32), cosine, sine).astype(BF16)
            rk = rotate(k[0, 0, :, lanes].astype(F32), cosine, sine).astype(BF16)
            put(first + n * GROUP + i, rq, rk, v[0, 0, :, lanes], g[0, 0, :, lanes])

    def put_own(slot, *parts):
        for a in range(4):
            out[slot, a] = parts[a]

    def put_shared(slot, rq, rk, vv, gg):
        dest = (slot - SPACES) * 2
        out[dest, 4] = rq
        out[dest, 5] = gg
        out[dest + 1, 4] = rk
        out[dest + 1, 5] = vv

    def step(n, carry):
        own = first + n * GROUP < SPACES
        pl.when(own)(lambda: group(n, put_own))
        pl.when(jnp.logical_not(own))(lambda: group(n, put_shared))
        return carry

    lax.fori_loop(0, found // GROUP, step, 0)


SMALL = pl.BlockSpec((FRAMES, W), lambda i, h, p: (0, 0))
LOCAL = pl.BlockSpec((ROWS, W), lambda i, h, p: (p[1], 0))
PACK_COST = pl.CostEstimate(flops=20_000_000, bytes_accessed=9_000_000, transcendentals=0)


def pack_spatial(meta, arrays, tabs):
    shape = (SPACES, 6, ROWS, W)
    part = pl.BlockSpec((1, 1, ROWS, HEADS * W), lambda l, h, p: (l, 0, 0, 0))
    return pl.pallas_call(
        pack_body,
        grid_spec=pltpu.PrefetchScalarGridSpec(
            num_scalar_prefetch=2,
            grid=(LAYERS,),
            in_specs=[part] * 4 + [SMALL, SMALL, LOCAL, LOCAL],
            out_specs=pl.BlockSpec(shape, lambda l, h, p: (0, 0, 0, 0)),
            scratch_shapes=[
                pltpu.SMEM((1,), jnp.int32),
                pltpu.SMEM((HEADS,), jnp.int32),
                pltpu.VMEM((ROWS, W), F32),
                pltpu.VMEM((ROWS, W), F32),
            ],
        ),
        out_shape=jax.ShapeDtypeStruct(shape, BF16),
        compiler_params=pltpu.CompilerParams(vmem_limit_bytes=VMEM),
        cost_estimate=PACK_COST,
        name="pack_spatial",
    )(*meta, *arrays, *tabs)


def peer(place, step, forward):
    frame = place[0]
    x, z = frame % 4, frame // 4
    dx, dz = step // 2, step % 2
    x = (x + (dx if forward else 4 - dx)) % 4
    return (1 - z if dz else z) * 4 + x


def pack_temporal_body(hc, place, q, k, v, g, ct, st, cp, sp, *rest):
    outs, (ids, cos_ref, sin_ref) = rest[:FRAMES], rest[FRAMES:]
    frame = place[0]
    cos_ref[...] = merged(ct[pl.ds(frame, 1), :], cp[...])
    sin_ref[...] = merged(st[pl.ds(frame, 1), :], sp[...])
    pick_heads(hc, range(LAYERS), False, ids)
    for step in range(FRAMES):
        cosine, sine = cos_ref[...], sin_ref[...]
        dest = peer(place, step, True)
        for i in range(3):
            flat_id = ids[dest * 3 + i]
            layer = flat_id // HEADS
            lanes = lanes_of(flat_id - layer * HEADS)
            out = outs[step]
            out[i * 4] = rotate(q[layer, 0, :, lanes].astype(F32), cosine, sine).astype(BF16)
            out[i * 4 + 1] = rotate(k[layer, 0, :, lanes].astype(F32), cosine, sine).astype(BF16)
            out[i * 4 + 2] = v[layer, 0, :, lanes]
            out[i * 4 + 3] = g[layer, 0, :, lanes]


def pack_temporal(meta, arrays, tabs):
    shape = (12, ROWS, W)
    return pl.pallas_call(
        pack_temporal_body,
        grid_spec=pltpu.PrefetchScalarGridSpec(
            num_scalar_prefetch=2,
            grid=(1,),
            in_specs=[whole(OUT)] * 4 + [SMALL, SMALL, LOCAL, LOCAL],
            out_specs=[whole(shape)] * FRAMES,
            scratch_shapes=[
                pltpu.SMEM((HEADS,), jnp.int32),
                pltpu.VMEM((ROWS, W), F32),
                pltpu.VMEM((ROWS, W), F32),
            ],
        ),
        out_shape=[jax.ShapeDtypeStruct(shape, BF16)] * FRAMES,
        compiler_params=pltpu.CompilerParams(vmem_limit_bytes=VMEM),
        cost_estimate=PACK_COST,
        name="pack_temporal",
    )(*meta, *arrays, *tabs)


CHUNKS = POSITIONS // KB
PAIR = KB // ROWS


def rows_of(j):
    return slice(j * KB, (j + 1) * KB)


def fold(op, total, strip):
    for r in range(0, STRIP, 8):
        total = op(total, strip[r : r + 8])
    return total


def strips(j):
    return [slice(r, r + STRIP) for r in range(j * KB, (j + 1) * KB, STRIP)]


def load_rows(ref, read, blocks):
    def load(j, carry):
        at = pl.ds(pl.multiple_of(j * KB, KB), KB)
        ref[at, :] = read(pl.ds(j * PAIR, PAIR)).astype(F32).reshape(KB, W).astype(BF16)
        return carry

    lax.fori_loop(0, blocks // PAIR, load, 0)
    used = blocks * ROWS
    if used < ref.shape[0]:
        ref[used:, :] = jnp.zeros((ref.shape[0] - used, W), BF16)


def attend_body(q, k, v, g, query_blocks, scratch):
    qs, ks, vs, gs, kt, qt, gt, s_a, s_b, d_a, d_b, p_ref, ds_ref, rows, qt_now, dk, dv, dq = scratch
    nq = -(-query_blocks * ROWS // QB)
    load_rows(qs, q, query_blocks)
    load_rows(gs, g, query_blocks)
    load_rows(ks, k, SPACES)
    load_rows(vs, v, SPACES)

    def queries(i):
        return pl.ds(pl.multiple_of(i * QB, QB), QB)

    def turn(i, carry):
        qt[i] = qs[queries(i), :].astype(F32).T.astype(BF16)
        gt[i] = gs[queries(i), :].astype(F32).T.astype(BF16)
        return carry

    lax.fori_loop(0, nq, turn, 0)
    for j in range(0, POSITIONS, W * 5):
        kt[:, j : j + W * 5] = ks[j : j + W * 5, :].astype(F32).T.astype(BF16)
    dk[...] = jnp.zeros_like(dk)
    dv[...] = jnp.zeros_like(dv)

    def products(j, turned_q, turned_g, refs):
        s_ref, d_ref = refs
        s_ref[rows_of(j), :] = jnp.dot(
            ks[rows_of(j), :], turned_q[...], preferred_element_type=F32
        )
        d_ref[rows_of(j), :] = jnp.dot(
            vs[rows_of(j), :], turned_g[...], preferred_element_type=F32
        )

    def highest(j, top, refs):
        for at in strips(j):
            top = fold(jnp.maximum, top, refs[0][at, :])
        return top

    low = jnp.full((8, QB), -jnp.inf, F32)
    zero = jnp.zeros((8, QB), F32)

    def block(i, qb, gb, top, refs, following):
        s_ref, d_ref = refs
        top = jnp.max(top, 0, keepdims=True) * SCALE2
        total, delta = zero, zero
        for j in range(CHUNKS):
            if following is not None:
                products(j, *following)
            for at in strips(j):
                p = jnp.exp2(s_ref[at, :] * SCALE2 - top)
                s_ref[at, :] = p
                total = fold(jnp.add, total, p)
                delta = fold(jnp.add, delta, p * d_ref[at, :])
        inverse = 1.0 / jnp.sum(total, 0, keepdims=True)
        delta = jnp.sum(delta, 0, keepdims=True) * inverse * SCALE
        after = low
        for j in range(CHUNKS):
            for at in strips(j):
                p = s_ref[at, :] * inverse
                p_ref[at, :] = p.astype(BF16)
                ds_ref[at, :] = (p * (d_ref[at, :] * SCALE - delta)).astype(BF16)
            if following is not None:
                after = highest(j, after, following[2])
            at = rows_of(j)
            dv[at, :] += jnp.dot(p_ref[at, :], gb[...], preferred_element_type=F32)
            dk[at, :] += jnp.dot(ds_ref[at, :], qb[...], preferred_element_type=F32)
        dq[queries(i), :] = jnp.dot(kt[...], ds_ref[...], preferred_element_type=F32).T
        return after

    one, two = (s_a, d_a), (s_b, d_b)

    def start(j, top):
        at = pl.ds(pl.multiple_of(j * KB, KB), KB)
        s = jnp.dot(ks[at, :], qt[0], preferred_element_type=F32)
        s_a[at, :] = s
        d_a[at, :] = jnp.dot(vs[at, :], gt[0], preferred_element_type=F32)
        return jnp.maximum(top, jnp.max(s.reshape(KB // 8, 8, QB), 0))

    top = lax.fori_loop(0, CHUNKS, start, low)

    def pair(n, top, last):
        for u in range(2):
            rows[2 * u] = qs[queries(2 * n + u), :]
            rows[2 * u + 1] = gs[queries(2 * n + u), :]
        for u in range(1 if last else 2):
            qt_now[2 * u] = qt[2 * n + 1 + u]
            qt_now[2 * u + 1] = gt[2 * n + 1 + u]
        top = block(
            2 * n, rows.at[0], rows.at[1], top, one, (qt_now.at[0], qt_now.at[1], two)
        )
        following = None if last else (qt_now.at[2], qt_now.at[3], one)
        return block(2 * n + 1, rows.at[2], rows.at[3], top, two, following)

    for n in range(nq // 2):
        top = pair(n, top, n == nq // 2 - 1)


def own_body(hc, place, x, kept, given, ct, st, cp, sp, out, *scratch):
    frame = pl.ds(place[0], 1)
    even = place[1] % 2 == 0
    attend_body(*[lambda two, a=a: x[two, a] for a in range(4)], SPACES, scratch)
    dk, dv, dq = scratch[-3:]
    time_c, time_s = ct[frame, :], st[frame, :]
    ones, zeros = jnp.ones((ROWS, W), F32), jnp.zeros((ROWS, W), F32)
    extra = 2 * HALF - ROWS

    def finish(n, carry):
        for b in [n * 2 + u for u in range(2)]:
            at = pl.ds(pl.multiple_of(b * ROWS, ROWS), ROWS)
            cosine = merged(time_c, cp[at, :])
            sine = merged(time_s, sp[at, :])
            rest_c = jnp.concatenate(
                [
                    jnp.where(even, cosine, ones),
                    jnp.where(even, cosine[:HALF], jnp.concatenate([cosine[HALF:], ones[:extra]])),
                ]
            )
            rest_s = jnp.concatenate(
                [
                    jnp.where(even, sine, zeros),
                    jnp.where(even, sine[:HALF], jnp.concatenate([sine[HALF:], zeros[:extra]])),
                ]
            )
            parts = [
                unrotate(dq[at, :], cosine, sine),
                unrotate(dk[at, :], cosine, sine),
                dv[at, :],
                unrotate(kept[b] + given[b], rest_c, rest_s),
            ]
            out[b] = jnp.concatenate(parts, 0).astype(BF16)
        return carry

    lax.fori_loop(0, SPACES // 2, finish, 0)


def shared_body(hc, place, mine, other, keep, give, *scratch):
    core = place[1] % 2
    even = core == 0
    blocks = SPACES // 2

    def read(unit, holder):
        def pick(two):
            return jnp.where(core == holder, mine[two, unit], other[two, unit])

        return pick

    def half(pick):
        return lambda two: pick(pl.ds(two.start + core * blocks, two.size))

    attend_body(
        half(read(0, 0)), read(0, 1), read(1, 1), half(read(1, 0)), blocks, scratch
    )
    dk, dv, dq = scratch[-3:]
    empty = jnp.zeros((2 * HALF - ROWS, W), F32)

    def finish(b, carry):
        at = pl.ds(pl.multiple_of(b * ROWS, ROWS), ROWS)
        local = jnp.clip(b - core * blocks, 0, blocks - 1)
        have = (b // blocks) == core
        gq = dq[pl.ds(pl.multiple_of(local * ROWS, ROWS), ROWS), :]
        gq = jnp.where(have, gq, jnp.zeros_like(gq))
        gk = dk[at, :]
        one = jnp.concatenate([gq, gk[:HALF]], 0)
        two = jnp.concatenate([dv[at, :], gk[HALF:], empty], 0)
        keep[b] = jnp.where(even, one, two)
        give[b] = jnp.where(even, two, one)
        return carry

    lax.fori_loop(0, SPACES, finish, 0)


def attend_scratch(padded):
    nq = padded // QB
    return (
        [pltpu.VMEM((padded, W), BF16), pltpu.VMEM((POSITIONS, W), BF16)]
        + [pltpu.VMEM((POSITIONS, W), BF16), pltpu.VMEM((padded, W), BF16)]
        + [pltpu.VMEM((W, POSITIONS), BF16)]
        + [pltpu.VMEM((nq, W, QB), BF16)] * 2
        + [pltpu.VMEM((POSITIONS, QB), F32)] * 4
        + [pltpu.VMEM((POSITIONS, QB), BF16)] * 2
        + [pltpu.VMEM((4, QB, W), BF16), pltpu.VMEM((4, W, QB), BF16)]
        + [pltpu.VMEM((POSITIONS, W), F32)] * 2
        + [pltpu.VMEM((padded, W), F32)]
    )


ATTEND_COST = pl.CostEstimate(
    flops=10 * POSITIONS * POSITIONS * W,
    bytes_accessed=6_000_000,
    transcendentals=POSITIONS * POSITIONS,
)


def attend_own(meta, received, kept, given, tabs):
    shape = (SPACES, BACK, W)
    return pl.pallas_call(
        own_body,
        grid_spec=pltpu.PrefetchScalarGridSpec(
            num_scalar_prefetch=2,
            grid=(1,),
            in_specs=[whole((SPACES, 4, ROWS, W)), whole(kept.shape), whole(given.shape)]
            + [whole(t.shape) for t in tabs],
            out_specs=whole(shape),
            scratch_shapes=attend_scratch(PADDED),
        ),
        out_shape=jax.ShapeDtypeStruct(shape, BF16),
        compiler_params=pltpu.CompilerParams(vmem_limit_bytes=VMEM),
        cost_estimate=pl.CostEstimate(flops=0, bytes_accessed=6_000_000, transcendentals=0),
        name="attend_own",
    )(*meta, received, kept, given, *tabs)


def attend_shared(meta, mine, other):
    shape = (SPACES, ROWS + HALF, W)
    return pl.pallas_call(
        shared_body,
        grid_spec=pltpu.PrefetchScalarGridSpec(
            num_scalar_prefetch=2,
            grid=(1,),
            in_specs=[whole(mine.shape), whole(other.shape)],
            out_specs=[whole(shape), whole(shape)],
            scratch_shapes=attend_scratch(PADDED // 2),
        ),
        out_shape=[jax.ShapeDtypeStruct(shape, F32)] * 2,
        compiler_params=pltpu.CompilerParams(vmem_limit_bytes=VMEM),
        cost_estimate=ATTEND_COST,
        name="attend_shared",
    )(*meta, mine, other)


def frames_body(hc, place, *refs):
    xs, (ct, st, cp, sp) = refs[:FRAMES], refs[FRAMES : FRAMES + 4]
    outs, (dq_ref, dk_ref, dv_ref) = refs[FRAMES + 4 : -3], refs[-3:]
    tokens = FRAMES * TP
    key_place = lax.broadcasted_iota(jnp.int32, (tokens, tokens), 0) % TP
    query_place = lax.broadcasted_iota(jnp.int32, (tokens, tokens), 1) % TP
    same = key_place == query_place
    nt = (((1,), (1,)), ((), ()))
    owners = [peer(place, step, False) for step in range(FRAMES)]

    def head(i, carry):
        for c in range(ROWS // TP):
            rows = slice(c * TP, (c + 1) * TP)
            q, k, v, g = (
                jnp.concatenate([x[i * 4 + a].astype(F32)[rows] for x in xs], 0).astype(BF16)
                for a in range(4)
            )
            s = lax.dot_general(k, q, nt, preferred_element_type=F32)
            s = jnp.where(same, s, -jnp.inf)
            p = jnp.exp2((s - jnp.max(s, 0, keepdims=True)) * SCALE2)
            p = p * (1.0 / jnp.sum(p, 0, keepdims=True))
            d = lax.dot_general(v, g, nt, preferred_element_type=F32)
            delta = jnp.sum(p * d, 0, keepdims=True)
            ds = p * ((d - delta) * SCALE)
            dst = ds.T.astype(BF16)
            ds = ds.astype(BF16)
            gv = jnp.dot(p.astype(BF16), g, preferred_element_type=F32)
            gk = jnp.dot(ds, q, preferred_element_type=F32)
            gq = jnp.dot(dst, k, preferred_element_type=F32)
            place_c, place_s = cp[rows, :], sp[rows, :]
            cosine = jnp.concatenate([merged(ct[pl.ds(f, 1), :], place_c) for f in owners], 0)
            sine = jnp.concatenate([merged(st[pl.ds(f, 1), :], place_s) for f in owners], 0)
            dq_ref[:, rows, :] = unrotate(gq, cosine, sine).reshape(FRAMES, TP, W)
            dk_ref[:, rows, :] = unrotate(gk, cosine, sine).reshape(FRAMES, TP, W)
            dv_ref[:, rows, :] = gv.reshape(FRAMES, TP, W)
        for step, out in enumerate(outs):
            out[i * 3] = dq_ref[step].astype(BF16)
            out[i * 3 + 1] = dk_ref[step].astype(BF16)
            out[i * 3 + 2] = dv_ref[step].astype(BF16)
        return carry

    lax.fori_loop(0, 3, head, 0)


def attend_frames(meta, received, tabs):
    shape = (9, ROWS, W)
    return pl.pallas_call(
        frames_body,
        grid_spec=pltpu.PrefetchScalarGridSpec(
            num_scalar_prefetch=2,
            grid=(1,),
            in_specs=[whole(x.shape) for x in received] + [SMALL, SMALL, LOCAL, LOCAL],
            out_specs=[whole(shape)] * FRAMES,
            scratch_shapes=[pltpu.VMEM((FRAMES, ROWS, W), F32)] * 3,
        ),
        out_shape=[jax.ShapeDtypeStruct(shape, BF16)] * FRAMES,
        compiler_params=pltpu.CompilerParams(vmem_limit_bytes=VMEM),
        cost_estimate=pl.CostEstimate(
            flops=2_000_000_000, bytes_accessed=6_000_000, transcendentals=600_000
        ),
        name="attend_frames",
    )(*meta, *received, *tabs)


def unpack_spatial_body(hc, place, x, oq, ok, ov, count):
    count[0] = 0

    def head(i, carry):
        layer = i // HEADS
        h = i - layer * HEADS

        @pl.when(hc[layer, h] == 0)
        def _():
            slot = count[0]
            count[0] = slot + 1
            lanes = pl.ds(pl.multiple_of(h * W, W), W)

            @pl.when(slot < SPACES)
            def _():
                piece = x[slot].astype(F32)
                oq[layer, 0, :, lanes] = piece[:ROWS].astype(BF16)
                ok[layer, 0, :, lanes] = piece[ROWS : 2 * ROWS].astype(BF16)
                ov[layer, 0, :, lanes] = piece[2 * ROWS : 3 * ROWS].astype(BF16)

            @pl.when(slot >= SPACES)
            def _():
                first = (slot - SPACES) * 2
                one = x[first].astype(F32)
                two = x[first + 1].astype(F32)
                oq[layer, 0, :, lanes] = one[3 * ROWS : 4 * ROWS].astype(BF16)
                ov[layer, 0, :, lanes] = two[3 * ROWS : 4 * ROWS].astype(BF16)
                both = jnp.concatenate([one[4 * ROWS :], two[4 * ROWS : 5 * ROWS - HALF]], 0)
                ok[layer, 0, :, lanes] = both.astype(BF16)

        return carry

    lax.fori_loop(0, LAYERS * HEADS, head, 0)


def unpack_spatial(meta, returned):
    return pl.pallas_call(
        unpack_spatial_body,
        grid_spec=pltpu.PrefetchScalarGridSpec(
            num_scalar_prefetch=2,
            grid=(1,),
            in_specs=[whole(returned.shape)],
            out_specs=[whole(OUT)] * 3,
            scratch_shapes=[pltpu.SMEM((1,), jnp.int32)],
        ),
        out_shape=[jax.ShapeDtypeStruct(OUT, BF16)] * 3,
        compiler_params=pltpu.CompilerParams(vmem_limit_bytes=VMEM),
        cost_estimate=pl.CostEstimate(flops=5_000_000, bytes_accessed=7_000_000, transcendentals=0),
        name="unpack_spatial",
    )(*meta, returned)


def unpack_temporal_body(hc, place, *refs):
    xs, outs, (ids, sems) = refs[:FRAMES], refs[FRAMES + 3 : FRAMES + 6], refs[FRAMES + 6 :]
    pick_heads(hc, range(LAYERS), False, ids)
    copies = []
    for step in range(FRAMES):
        dest = peer(place, step, True)
        for i in range(3):
            flat_id = ids[dest * 3 + i]
            layer = flat_id // HEADS
            lanes = lanes_of(flat_id - layer * HEADS)
            for a in range(3):
                copies.append(
                    pltpu.make_async_copy(
                        xs[step].at[i * 3 + a],
                        outs[a].at[layer, 0, :, lanes],
                        sems.at[step * 3 + i, a],
                    )
                )
                copies[-1].start()
    for copy in copies:
        copy.wait()


def unpack_temporal(meta, returned, partial):
    anywhere = pl.BlockSpec(memory_space=pl.ANY)
    return pl.pallas_call(
        unpack_temporal_body,
        grid_spec=pltpu.PrefetchScalarGridSpec(
            num_scalar_prefetch=2,
            grid=(1,),
            in_specs=[whole(x.shape) for x in returned] + [anywhere] * 3,
            out_specs=[anywhere] * 3,
            scratch_shapes=[
                pltpu.SMEM((HEADS,), jnp.int32),
                pltpu.SemaphoreType.DMA((HEADS, 3)),
            ],
        ),
        out_shape=[jax.ShapeDtypeStruct(OUT, BF16)] * 3,
        input_output_aliases={2 + FRAMES + a: a for a in range(3)},
        compiler_params=pltpu.CompilerParams(vmem_limit_bytes=VMEM),
        cost_estimate=pl.CostEstimate(flops=0, bytes_accessed=5_000_000, transcendentals=0),
        name="unpack_temporal",
    )(*meta, *returned, *partial)


def exchange(x):
    return lax.all_to_all(x, "space", split_axis=0, concat_axis=0, tiled=True)


SWAP = [(i, i ^ 1) for i in range(SPACES)]


def along_x(parts, sign):
    def move(step, part):
        dx = sign * (step // 2)
        if dx == 0:
            return part
        pairs = [(f, f // 4 * 4 + (f + dx) % 4) for f in range(FRAMES)]
        return lax.ppermute(part, "frame", pairs)

    return [move(step, part) for step, part in enumerate(parts)]


def along_z(parts):
    pairs = [(f, f ^ 4) for f in range(FRAMES)]
    return [lax.ppermute(x, "frame", pairs) if n % 2 else x for n, x in enumerate(parts)]


def on_device(queries, keys, values, grad_out, head_class):
    place = jnp.stack([lax.axis_index("frame"), lax.axis_index("space")]).astype(jnp.int32)
    meta = (head_class, place)
    tabs = tuple(jnp.asarray(t) for t in tables())
    arrays = (queries, keys, values, grad_out)
    got_s = exchange(pack_spatial(meta, arrays, tabs))
    half_t = along_x(pack_temporal(meta, arrays, tabs), 1)
    got_s, *half_t = lax.optimization_barrier((got_s, *half_t))
    got_t = along_z(half_t)
    mine = got_s[:, 4:6]
    other = lax.ppermute(mine, "space", SWAP)
    kept, give = attend_shared(meta, mine, other)
    kept, give, got_t[1], got_t[3] = lax.optimization_barrier((kept, give, got_t[1], got_t[3]))
    given = lax.ppermute(give, "space", SWAP)
    back_s = attend_own(meta, got_s, kept, given, tabs)
    back_s, *got_t = lax.optimization_barrier((back_s, *got_t))
    home_s = exchange(back_s)
    home_t = along_x(along_z(attend_frames(meta, got_t, tabs)), -1)
    partial = unpack_spatial(meta, home_s)
    return tuple(unpack_temporal(meta, home_t, partial))


def solution(mesh):
    placed = P(None, "frame", "space", None)
    return jax.shard_map(
        on_device,
        mesh=mesh,
        in_specs=(placed, placed, placed, placed, P()),
        out_specs=(placed, placed, placed),
        check_vma=False,
    )
```

```python
import math

import jax
import jax.numpy as jnp
import numpy as np
from jax import lax
from jax.experimental import pallas as pl
from jax.experimental.pallas import tpu as pltpu
from jax.sharding import PartitionSpec as P

RT = 16
RS = 56
PW = 80
THETA = 256.0
W = RT + 2 * RS
HEADS = 24
LAYERS = 2
FRAMES = 8
SPACES = 16
ROWS = 120
POSITIONS = SPACES * ROWS
HALF = 64
BACK = 4 * ROWS + HALF
QB = 512
PADDED = 2048
KB = 240
STRIP = 16
TP = 24
GROUP = 4
VMEM = 60 * 1024 * 1024
SCALE = 1.0 / math.sqrt(W)
SCALE2 = SCALE * math.log2(math.e)
F32 = jnp.float32
BF16 = jnp.bfloat16


OUT = (LAYERS, 1, ROWS, HEADS * W)


def whole(shape):
    return pl.BlockSpec(shape, lambda i, h, p: (0,) * len(shape))


def tables():
    channel = np.arange(W)
    pair = channel // 2
    tpairs, spairs = RT // 2, RS // 2
    is_time = pair < tpairs
    is_row = (pair >= tpairs) & (pair < tpairs + spairs)
    local = np.where(is_time, pair, np.where(is_row, pair - tpairs, pair - tpairs - spairs))
    width = np.where(is_time, RT, RS)
    freq = THETA ** (-2.0 * local / width)
    sign = np.where(channel % 2 == 0, -1.0, 1.0)
    time = np.arange(FRAMES)[:, None] * freq
    position = np.arange(POSITIONS)[:, None]
    place = np.where(is_row, position // PW, position % PW) * freq
    return (
        np.cos(time).astype(np.float32),
        (np.sin(time) * sign).astype(np.float32),
        np.cos(place).astype(np.float32),
        (np.sin(place) * sign).astype(np.float32),
    )


def lane_ids(shape):
    return lax.broadcasted_iota(jnp.int32, shape, len(shape) - 1)


def swapped(x):
    row = lax.broadcasted_iota(jnp.int32, (W, W), 0)
    column = lax.broadcasted_iota(jnp.int32, (W, W), 1)
    pairs = jnp.where((row ^ 1) == column, 1.0, 0.0).astype(BF16)
    return jnp.dot(x.astype(BF16), pairs, preferred_element_type=F32)


def merged(time_row, place_rows):
    return jnp.where(lane_ids(place_rows.shape) < RT, time_row, place_rows)


def rotate(x, cosine, sine):
    return x * cosine + swapped(x) * sine


def unrotate(x, cosine, sine):
    x = x.astype(BF16).astype(F32)
    return x * cosine - swapped(x) * sine


def pick_heads(hc, layers, spatial, ids):
    def look(h, n, layer):
        mine = (hc[layer, h] == 0) == spatial

        @pl.when(mine)
        def _():
            ids[n] = layer * HEADS + h

        return n + mine.astype(jnp.int32)

    found = jnp.int32(0)
    for layer in layers:
        found = lax.fori_loop(0, HEADS, lambda h, n: look(h, n, layer), found)
    return found


def lanes_of(h):
    return pl.ds(pl.multiple_of(h * W, W), W)


def pack_body(hc, place, q, k, v, g, ct, st, cp, sp, out, count, ids, cos_ref, sin_ref):
    layer = pl.program_id(0)

    @pl.when(layer == 0)
    def _():
        count[0] = 0
        frame = place[0]
        cos_ref[...] = merged(ct[pl.ds(frame, 1), :], cp[...])
        sin_ref[...] = merged(st[pl.ds(frame, 1), :], sp[...])

    first = count[0]
    found = pick_heads(hc, [layer], True, ids)
    count[0] = first + found

    def group(n, put):
        cosine, sine = cos_ref[...], sin_ref[...]
        for i in range(GROUP):
            lanes = lanes_of(ids[n * GROUP + i] - layer * HEADS)
            rq = rotate(q[0, 0, :, lanes].astype(F32), cosine, sine).astype(BF16)
            rk = rotate(k[0, 0, :, lanes].astype(F32), cosine, sine).astype(BF16)
            put(first + n * GROUP + i, rq, rk, v[0, 0, :, lanes], g[0, 0, :, lanes])

    def put_own(slot, *parts):
        for a in range(4):
            out[slot, a] = parts[a]

    def put_shared(slot, rq, rk, vv, gg):
        dest = (slot - SPACES) * 2
        out[dest, 4] = rq
        out[dest, 5] = gg
        out[dest + 1, 4] = rk
        out[dest + 1, 5] = vv

    def step(n, carry):
        own = first + n * GROUP < SPACES
        pl.when(own)(lambda: group(n, put_own))
        pl.when(jnp.logical_not(own))(lambda: group(n, put_shared))
        return carry

    lax.fori_loop(0, found // GROUP, step, 0)


SMALL = pl.BlockSpec((FRAMES, W), lambda i, h, p: (0, 0))
LOCAL = pl.BlockSpec((ROWS, W), lambda i, h, p: (p[1], 0))
PACK_COST = pl.CostEstimate(flops=20_000_000, bytes_accessed=9_000_000, transcendentals=0)


def pack_spatial(meta, arrays, tabs):
    shape = (SPACES, 6, ROWS, W)
    part = pl.BlockSpec((1, 1, ROWS, HEADS * W), lambda l, h, p: (l, 0, 0, 0))
    return pl.pallas_call(
        pack_body,
        grid_spec=pltpu.PrefetchScalarGridSpec(
            num_scalar_prefetch=2,
            grid=(LAYERS,),
            in_specs=[part] * 4 + [SMALL, SMALL, LOCAL, LOCAL],
            out_specs=pl.BlockSpec(shape, lambda l, h, p: (0, 0, 0, 0)),
            scratch_shapes=[
                pltpu.SMEM((1,), jnp.int32),
                pltpu.SMEM((HEADS,), jnp.int32),
                pltpu.VMEM((ROWS, W), F32),
                pltpu.VMEM((ROWS, W), F32),
            ],
        ),
        out_shape=jax.ShapeDtypeStruct(shape, BF16),
        compiler_params=pltpu.CompilerParams(vmem_limit_bytes=VMEM),
        cost_estimate=PACK_COST,
        name="pack_spatial",
    )(*meta, *arrays, *tabs)


def peer(place, step, forward):
    frame = place[0]
    x, z = frame % 4, frame // 4
    dx, dz = step // 2, step % 2
    x = (x + (dx if forward else 4 - dx)) % 4
    return (1 - z if dz else z) * 4 + x


def pack_temporal_body(hc, place, q, k, v, g, ct, st, cp, sp, *rest):
    outs, (ids, cos_ref, sin_ref) = rest[:FRAMES], rest[FRAMES:]
    frame = place[0]
    cos_ref[...] = merged(ct[pl.ds(frame, 1), :], cp[...])
    sin_ref[...] = merged(st[pl.ds(frame, 1), :], sp[...])
    pick_heads(hc, range(LAYERS), False, ids)
    for step in range(FRAMES):
        cosine, sine = cos_ref[...], sin_ref[...]
        dest = peer(place, step, True)
        for i in range(3):
            flat_id = ids[dest * 3 + i]
            layer = flat_id // HEADS
            lanes = lanes_of(flat_id - layer * HEADS)
            out = outs[step]
            out[i * 4] = rotate(q[layer, 0, :, lanes].astype(F32), cosine, sine).astype(BF16)
            out[i * 4 + 1] = rotate(k[layer, 0, :, lanes].astype(F32), cosine, sine).astype(BF16)
            out[i * 4 + 2] = v[layer, 0, :, lanes]
            out[i * 4 + 3] = g[layer, 0, :, lanes]


def pack_temporal(meta, arrays, tabs):
    shape = (12, ROWS, W)
    return pl.pallas_call(
        pack_temporal_body,
        grid_spec=pltpu.PrefetchScalarGridSpec(
            num_scalar_prefetch=2,
            grid=(1,),
            in_specs=[whole(OUT)] * 4 + [SMALL, SMALL, LOCAL, LOCAL],
            out_specs=[whole(shape)] * FRAMES,
            scratch_shapes=[
                pltpu.SMEM((HEADS,), jnp.int32),
                pltpu.VMEM((ROWS, W), F32),
                pltpu.VMEM((ROWS, W), F32),
            ],
        ),
        out_shape=[jax.ShapeDtypeStruct(shape, BF16)] * FRAMES,
        compiler_params=pltpu.CompilerParams(vmem_limit_bytes=VMEM),
        cost_estimate=PACK_COST,
        name="pack_temporal",
    )(*meta, *arrays, *tabs)


CHUNKS = POSITIONS // KB
PAIR = KB // ROWS


def rows_of(j):
    return slice(j * KB, (j + 1) * KB)


def fold(op, total, strip):
    for r in range(0, STRIP, 8):
        total = op(total, strip[r : r + 8])
    return total


def strips(j):
    return [slice(r, r + STRIP) for r in range(j * KB, (j + 1) * KB, STRIP)]


def load_rows(ref, read, blocks):
    def load(j, carry):
        at = pl.ds(pl.multiple_of(j * KB, KB), KB)
        ref[at, :] = read(pl.ds(j * PAIR, PAIR)).astype(F32).reshape(KB, W).astype(BF16)
        return carry

    lax.fori_loop(0, blocks // PAIR, load, 0)
    used = blocks * ROWS
    if used < ref.shape[0]:
        ref[used:, :] = jnp.zeros((ref.shape[0] - used, W), BF16)


def attend_body(q, k, v, g, query_blocks, scratch):
    qs, ks, vs, gs, kt, qt, gt, s_a, s_b, d_a, d_b, p_ref, ds_ref, rows, qt_now, dk, dv, dq = scratch
    nq = -(-query_blocks * ROWS // QB)
    load_rows(qs, q, query_blocks)
    load_rows(gs, g, query_blocks)
    load_rows(ks, k, SPACES)
    load_rows(vs, v, SPACES)

    def queries(i):
        return pl.ds(pl.multiple_of(i * QB, QB), QB)

    def turn(i, carry):
        qt[i] = qs[queries(i), :].astype(F32).T.astype(BF16)
        gt[i] = gs[queries(i), :].astype(F32).T.astype(BF16)
        return carry

    lax.fori_loop(0, nq, turn, 0)
    for j in range(0, POSITIONS, W * 5):
        kt[:, j : j + W * 5] = ks[j : j + W * 5, :].astype(F32).T.astype(BF16)
    dk[...] = jnp.zeros_like(dk)
    dv[...] = jnp.zeros_like(dv)

    def products(j, turned_q, turned_g, refs):
        s_ref, d_ref = refs
        s_ref[rows_of(j), :] = jnp.dot(
            ks[rows_of(j), :], turned_q[...], preferred_element_type=F32
        )
        d_ref[rows_of(j), :] = jnp.dot(
            vs[rows_of(j), :], turned_g[...], preferred_element_type=F32
        )

    def highest(j, top, refs):
        for at in strips(j):
            top = fold(jnp.maximum, top, refs[0][at, :])
        return top

    low = jnp.full((8, QB), -jnp.inf, F32)
    zero = jnp.zeros((8, QB), F32)

    def block(i, qb, gb, top, refs, following):
        s_ref, d_ref = refs
        top = jnp.max(top, 0, keepdims=True) * SCALE2
        total, delta = zero, zero
        for j in range(CHUNKS):
            if following is not None:
                products(j, *following)
            for at in strips(j):
                p = jnp.exp2(s_ref[at, :] * SCALE2 - top)
                s_ref[at, :] = p
                total = fold(jnp.add, total, p)
                delta = fold(jnp.add, delta, p * d_ref[at, :])
        inverse = 1.0 / jnp.sum(total, 0, keepdims=True)
        delta = jnp.sum(delta, 0, keepdims=True) * inverse * SCALE
        after = low
        for j in range(CHUNKS):
            for at in strips(j):
                p = s_ref[at, :] * inverse
                p_ref[at, :] = p.astype(BF16)
                ds_ref[at, :] = (p * (d_ref[at, :] * SCALE - delta)).astype(BF16)
            if following is not None:
                after = highest(j, after, following[2])
            at = rows_of(j)
            dv[at, :] += jnp.dot(p_ref[at, :], gb[...], preferred_element_type=F32)
            dk[at, :] += jnp.dot(ds_ref[at, :], qb[...], preferred_element_type=F32)
        dq[queries(i), :] = jnp.dot(kt[...], ds_ref[...], preferred_element_type=F32).T
        return after

    one, two = (s_a, d_a), (s_b, d_b)

    def start(j, top):
        at = pl.ds(pl.multiple_of(j * KB, KB), KB)
        s = jnp.dot(ks[at, :], qt[0], preferred_element_type=F32)
        s_a[at, :] = s
        d_a[at, :] = jnp.dot(vs[at, :], gt[0], preferred_element_type=F32)
        return jnp.maximum(top, jnp.max(s.reshape(KB // 8, 8, QB), 0))

    top = lax.fori_loop(0, CHUNKS, start, low)

    def pair(n, top, last):
        for u in range(2):
            rows[2 * u] = qs[queries(2 * n + u), :]
            rows[2 * u + 1] = gs[queries(2 * n + u), :]
        for u in range(1 if last else 2):
            qt_now[2 * u] = qt[2 * n + 1 + u]
            qt_now[2 * u + 1] = gt[2 * n + 1 + u]
        top = block(
            2 * n, rows.at[0], rows.at[1], top, one, (qt_now.at[0], qt_now.at[1], two)
        )
        following = None if last else (qt_now.at[2], qt_now.at[3], one)
        return block(2 * n + 1, rows.at[2], rows.at[3], top, two, following)

    for n in range(nq // 2):
        top = pair(n, top, n == nq // 2 - 1)


def own_body(hc, place, x, kept, given, ct, st, cp, sp, out, *scratch):
    frame = pl.ds(place[0], 1)
    even = place[1] % 2 == 0
    attend_body(*[lambda two, a=a: x[two, a] for a in range(4)], SPACES, scratch)
    dk, dv, dq = scratch[-3:]
    time_c, time_s = ct[frame, :], st[frame, :]
    ones, zeros = jnp.ones((ROWS, W), F32), jnp.zeros((ROWS, W), F32)
    extra = 2 * HALF - ROWS

    def finish(n, carry):
        for b in [n * 2 + u for u in range(2)]:
            at = pl.ds(pl.multiple_of(b * ROWS, ROWS), ROWS)
            cosine = merged(time_c, cp[at, :])
            sine = merged(time_s, sp[at, :])
            rest_c = jnp.concatenate(
                [
                    jnp.where(even, cosine, ones),
                    jnp.where(even, cosine[:HALF], jnp.concatenate([cosine[HALF:], ones[:extra]])),
                ]
            )
            rest_s = jnp.concatenate(
                [
                    jnp.where(even, sine, zeros),
                    jnp.where(even, sine[:HALF], jnp.concatenate([sine[HALF:], zeros[:extra]])),
                ]
            )
            parts = [
                unrotate(dq[at, :], cosine, sine),
                unrotate(dk[at, :], cosine, sine),
                dv[at, :],
                unrotate(kept[b] + given[b], rest_c, rest_s),
            ]
            out[b] = jnp.concatenate(parts, 0).astype(BF16)
        return carry

    lax.fori_loop(0, SPACES // 2, finish, 0)


def shared_body(hc, place, mine, other, keep, give, *scratch):
    core = place[1] % 2
    even = core == 0
    blocks = SPACES // 2

    def read(unit, holder):
        def pick(two):
            return jnp.where(core == holder, mine[two, unit], other[two, unit])

        return pick

    def half(pick):
        return lambda two: pick(pl.ds(two.start + core * blocks, two.size))

    attend_body(
        half(read(0, 0)), read(0, 1), read(1, 1), half(read(1, 0)), blocks, scratch
    )
    dk, dv, dq = scratch[-3:]
    empty = jnp.zeros((2 * HALF - ROWS, W), F32)

    def finish(b, carry):
        at = pl.ds(pl.multiple_of(b * ROWS, ROWS), ROWS)
        local = jnp.clip(b - core * blocks, 0, blocks - 1)
        have = (b // blocks) == core
        gq = dq[pl.ds(pl.multiple_of(local * ROWS, ROWS), ROWS), :]
        gq = jnp.where(have, gq, jnp.zeros_like(gq))
        gk = dk[at, :]
        one = jnp.concatenate([gq, gk[:HALF]], 0)
        two = jnp.concatenate([dv[at, :], gk[HALF:], empty], 0)
        keep[b] = jnp.where(even, one, two)
        give[b] = jnp.where(even, two, one)
        return carry

    lax.fori_loop(0, SPACES, finish, 0)


def attend_scratch(padded):
    nq = padded // QB
    return (
        [pltpu.VMEM((padded, W), BF16), pltpu.VMEM((POSITIONS, W), BF16)]
        + [pltpu.VMEM((POSITIONS, W), BF16), pltpu.VMEM((padded, W), BF16)]
        + [pltpu.VMEM((W, POSITIONS), BF16)]
        + [pltpu.VMEM((nq, W, QB), BF16)] * 2
        + [pltpu.VMEM((POSITIONS, QB), F32)] * 4
        + [pltpu.VMEM((POSITIONS, QB), BF16)] * 2
        + [pltpu.VMEM((4, QB, W), BF16), pltpu.VMEM((4, W, QB), BF16)]
        + [pltpu.VMEM((POSITIONS, W), F32)] * 2
        + [pltpu.VMEM((padded, W), F32)]
    )


ATTEND_COST = pl.CostEstimate(
    flops=10 * POSITIONS * POSITIONS * W,
    bytes_accessed=6_000_000,
    transcendentals=POSITIONS * POSITIONS,
)


def attend_own(meta, received, kept, given, tabs):
    shape = (SPACES, BACK, W)
    return pl.pallas_call(
        own_body,
        grid_spec=pltpu.PrefetchScalarGridSpec(
            num_scalar_prefetch=2,
            grid=(1,),
            in_specs=[whole((SPACES, 4, ROWS, W)), whole(kept.shape), whole(given.shape)]
            + [whole(t.shape) for t in tabs],
            out_specs=whole(shape),
            scratch_shapes=attend_scratch(PADDED),
        ),
        out_shape=jax.ShapeDtypeStruct(shape, BF16),
        compiler_params=pltpu.CompilerParams(vmem_limit_bytes=VMEM),
        cost_estimate=pl.CostEstimate(flops=0, bytes_accessed=6_000_000, transcendentals=0),
        name="attend_own",
    )(*meta, received, kept, given, *tabs)


def attend_shared(meta, mine, other):
    shape = (SPACES, ROWS + HALF, W)
    return pl.pallas_call(
        shared_body,
        grid_spec=pltpu.PrefetchScalarGridSpec(
            num_scalar_prefetch=2,
            grid=(1,),
            in_specs=[whole(mine.shape), whole(other.shape)],
            out_specs=[whole(shape), whole(shape)],
            scratch_shapes=attend_scratch(PADDED // 2),
        ),
        out_shape=[jax.ShapeDtypeStruct(shape, F32)] * 2,
        compiler_params=pltpu.CompilerParams(vmem_limit_bytes=VMEM),
        cost_estimate=ATTEND_COST,
        name="attend_shared",
    )(*meta, mine, other)


def frames_body(hc, place, *refs):
    xs, (ct, st, cp, sp) = refs[:FRAMES], refs[FRAMES : FRAMES + 4]
    outs, (dq_ref, dk_ref, dv_ref) = refs[FRAMES + 4 : -3], refs[-3:]
    tokens = FRAMES * TP
    key_place = lax.broadcasted_iota(jnp.int32, (tokens, tokens), 0) % TP
    query_place = lax.broadcasted_iota(jnp.int32, (tokens, tokens), 1) % TP
    same = key_place == query_place
    nt = (((1,), (1,)), ((), ()))
    owners = [peer(place, step, False) for step in range(FRAMES)]

    def head(i, carry):
        for c in range(ROWS // TP):
            rows = slice(c * TP, (c + 1) * TP)
            q, k, v, g = (
                jnp.concatenate([x[i * 4 + a].astype(F32)[rows] for x in xs], 0).astype(BF16)
                for a in range(4)
            )
            s = lax.dot_general(k, q, nt, preferred_element_type=F32)
            s = jnp.where(same, s, -jnp.inf)
            p = jnp.exp2((s - jnp.max(s, 0, keepdims=True)) * SCALE2)
            p = p * (1.0 / jnp.sum(p, 0, keepdims=True))
            d = lax.dot_general(v, g, nt, preferred_element_type=F32)
            delta = jnp.sum(p * d, 0, keepdims=True)
            ds = p * ((d - delta) * SCALE)
            dst = ds.T.astype(BF16)
            ds = ds.astype(BF16)
            gv = jnp.dot(p.astype(BF16), g, preferred_element_type=F32)
            gk = jnp.dot(ds, q, preferred_element_type=F32)
            gq = jnp.dot(dst, k, preferred_element_type=F32)
            place_c, place_s = cp[rows, :], sp[rows, :]
            cosine = jnp.concatenate([merged(ct[pl.ds(f, 1), :], place_c) for f in owners], 0)
            sine = jnp.concatenate([merged(st[pl.ds(f, 1), :], place_s) for f in owners], 0)
            dq_ref[:, rows, :] = unrotate(gq, cosine, sine).reshape(FRAMES, TP, W)
            dk_ref[:, rows, :] = unrotate(gk, cosine, sine).reshape(FRAMES, TP, W)
            dv_ref[:, rows, :] = gv.reshape(FRAMES, TP, W)
        for step, out in enumerate(outs):
            out[i * 3] = dq_ref[step].astype(BF16)
            out[i * 3 + 1] = dk_ref[step].astype(BF16)
            out[i * 3 + 2] = dv_ref[step].astype(BF16)
        return carry

    lax.fori_loop(0, 3, head, 0)


def attend_frames(meta, received, tabs):
    shape = (9, ROWS, W)
    return pl.pallas_call(
        frames_body,
        grid_spec=pltpu.PrefetchScalarGridSpec(
            num_scalar_prefetch=2,
            grid=(1,),
            in_specs=[whole(x.shape) for x in received] + [SMALL, SMALL, LOCAL, LOCAL],
            out_specs=[whole(shape)] * FRAMES,
            scratch_shapes=[pltpu.VMEM((FRAMES, ROWS, W), F32)] * 3,
        ),
        out_shape=[jax.ShapeDtypeStruct(shape, BF16)] * FRAMES,
        compiler_params=pltpu.CompilerParams(vmem_limit_bytes=VMEM),
        cost_estimate=pl.CostEstimate(
            flops=2_000_000_000, bytes_accessed=6_000_000, transcendentals=600_000
        ),
        name="attend_frames",
    )(*meta, *received, *tabs)


def column(flat_id):
    layer = flat_id // HEADS
    return layer, 0, slice(None), lanes_of(flat_id - layer * HEADS)


def unpack_temporal_body(hc, place, *refs):
    xs, outs, (ids,) = refs[:FRAMES], refs[FRAMES : FRAMES + 3], refs[FRAMES + 3 :]
    pick_heads(hc, range(LAYERS), False, ids)
    for step in range(FRAMES):
        dest = peer(place, step, True)
        for i in range(3):
            at = column(ids[dest * 3 + i])
            for a, out in enumerate(outs):
                out[at] = xs[step][i * 3 + a]


def unpack_temporal(meta, returned):
    return pl.pallas_call(
        unpack_temporal_body,
        grid_spec=pltpu.PrefetchScalarGridSpec(
            num_scalar_prefetch=2,
            grid=(1,),
            in_specs=[whole(x.shape) for x in returned],
            out_specs=[whole(OUT)] * 3,
            scratch_shapes=[pltpu.SMEM((HEADS,), jnp.int32)],
        ),
        out_shape=[jax.ShapeDtypeStruct(OUT, BF16)] * 3,
        compiler_params=pltpu.CompilerParams(vmem_limit_bytes=VMEM),
        cost_estimate=pl.CostEstimate(flops=5_000_000, bytes_accessed=7_000_000, transcendentals=0),
        name="unpack_temporal",
    )(*meta, *returned)


def unpack_spatial_body(hc, place, x, iq, ik, iv, oq, ok, ov, ids, pieces, sems):
    outs = (oq, ok, ov)
    pick_heads(hc, range(LAYERS), True, ids)
    copies = []

    def put(slot, parts):
        for a, part in enumerate(parts):
            pieces[slot, a] = part.astype(BF16)
            copies.append(
                pltpu.make_async_copy(
                    pieces.at[slot, a], outs[a].at[column(ids[slot])], sems.at[slot, a]
                )
            )
            copies[-1].start()

    for n in range(SPACES // 2):
        one = x[2 * n].astype(F32)
        two = x[2 * n + 1].astype(F32)
        for slot, piece in ((2 * n, one), (2 * n + 1, two)):
            put(slot, [piece[a * ROWS : (a + 1) * ROWS] for a in range(3)])
        both = jnp.concatenate([one[4 * ROWS :], two[4 * ROWS : 5 * ROWS - HALF]], 0)
        put(SPACES + n, [one[3 * ROWS : 4 * ROWS], both, two[3 * ROWS : 4 * ROWS]])
    for copy in copies:
        copy.wait()


def unpack_spatial(meta, returned, partial):
    anywhere = pl.BlockSpec(memory_space=pl.ANY)
    return pl.pallas_call(
        unpack_spatial_body,
        grid_spec=pltpu.PrefetchScalarGridSpec(
            num_scalar_prefetch=2,
            grid=(1,),
            in_specs=[whole(returned.shape)] + [anywhere] * 3,
            out_specs=[anywhere] * 3,
            scratch_shapes=[
                pltpu.SMEM((HEADS,), jnp.int32),
                pltpu.VMEM((HEADS, 3, ROWS, W), BF16),
                pltpu.SemaphoreType.DMA((HEADS, 3)),
            ],
        ),
        out_shape=[jax.ShapeDtypeStruct(OUT, BF16)] * 3,
        input_output_aliases={3 + a: a for a in range(3)},
        compiler_params=pltpu.CompilerParams(vmem_limit_bytes=VMEM),
        cost_estimate=pl.CostEstimate(flops=0, bytes_accessed=5_000_000, transcendentals=0),
        name="unpack_spatial",
    )(*meta, returned, *partial)


def exchange(x):
    return lax.all_to_all(x, "space", split_axis=0, concat_axis=0, tiled=True)


SWAP = [(i, i ^ 1) for i in range(SPACES)]


def along_x(parts, sign):
    def move(step, part):
        dx = sign * (step // 2)
        if dx == 0:
            return part
        pairs = [(f, f // 4 * 4 + (f + dx) % 4) for f in range(FRAMES)]
        return lax.ppermute(part, "frame", pairs)

    return [move(step, part) for step, part in enumerate(parts)]


def along_z(parts):
    pairs = [(f, f ^ 4) for f in range(FRAMES)]
    return [lax.ppermute(x, "frame", pairs) if n % 2 else x for n, x in enumerate(parts)]


def tie(*values):
    return lax.optimization_barrier(values)


def on_device(queries, keys, values, grad_out, head_class):
    place = jnp.stack([lax.axis_index("frame"), lax.axis_index("space")]).astype(jnp.int32)
    meta = (head_class, place)
    tabs = tuple(jnp.asarray(t) for t in tables())
    arrays = (queries, keys, values, grad_out)
    got_s = exchange(pack_spatial(meta, arrays, tabs))
    half_t = along_x(pack_temporal(meta, arrays, tabs), 1)
    got_t = along_z(half_t)
    got_t[5], got_t[7] = half_t[5], half_t[7]
    got_s, *got_t = tie(got_s, *got_t)
    got_t[5], got_t[7] = along_z([None, got_t[5], None, got_t[7]])[1::2]
    mine = got_s[:, 4:6]
    other = lax.ppermute(mine, "space", SWAP)
    kept, give = attend_shared(meta, mine, other)
    kept, give, got_t[5], got_t[7] = tie(kept, give, got_t[5], got_t[7])
    given = lax.ppermute(give, "space", SWAP)
    grads_t = list(attend_frames(meta, got_t, tabs))
    got_s, grads_t[0] = tie(got_s, grads_t[0])
    back_s = attend_own(meta, got_s, kept, given, tabs)
    half_t = along_z(grads_t)
    back_s, half_t[1], half_t[3], half_t[5], half_t[7] = tie(
        back_s, half_t[1], half_t[3], half_t[5], half_t[7]
    )
    home_s = exchange(back_s)
    partial = unpack_temporal(meta, along_x(half_t, -1))
    return tuple(unpack_spatial(meta, home_s, partial))


def solution(mesh):
    placed = P(None, "frame", "space", None)
    return jax.shard_map(
        on_device,
        mesh=mesh,
        in_specs=(placed, placed, placed, placed, P()),
        out_specs=(placed, placed, placed),
        check_vma=False,
    )
```

```python
import math

import jax
import jax.numpy as jnp
import numpy as np
from jax import lax
from jax.experimental import pallas as pl
from jax.experimental.pallas import tpu as pltpu
from jax.sharding import PartitionSpec as P

RT = 16
RS = 56
PW = 80
THETA = 256.0
W = RT + 2 * RS
HEADS = 24
LAYERS = 2
FRAMES = 8
SPACES = 16
ROWS = 120
POSITIONS = SPACES * ROWS
HALF = 64
BACK = 4 * ROWS + HALF
QB = 512
PADDED = 2048
KB = 240
STRIP = 16
TP = 24
GROUP = 4
MIB = 1024 * 1024
VMEM = 60 * MIB
SCALE = 1.0 / math.sqrt(W)
SCALE2 = SCALE * math.log2(math.e)
F32 = jnp.float32
BF16 = jnp.bfloat16


OUT = (LAYERS, 1, ROWS, HEADS * W)


def whole(shape):
    return pl.BlockSpec(shape, lambda i, h, p: (0,) * len(shape))


def tables():
    channel = np.arange(W)
    pair = channel // 2
    tpairs, spairs = RT // 2, RS // 2
    is_time = pair < tpairs
    is_row = (pair >= tpairs) & (pair < tpairs + spairs)
    local = np.where(is_time, pair, np.where(is_row, pair - tpairs, pair - tpairs - spairs))
    width = np.where(is_time, RT, RS)
    freq = THETA ** (-2.0 * local / width)
    sign = np.where(channel % 2 == 0, -1.0, 1.0)
    time = np.arange(FRAMES)[:, None] * freq
    position = np.arange(POSITIONS)[:, None]
    place = np.where(is_row, position // PW, position % PW) * freq
    return (
        np.cos(time).astype(np.float32),
        (np.sin(time) * sign).astype(np.float32),
        np.cos(place).astype(np.float32),
        (np.sin(place) * sign).astype(np.float32),
    )


def lane_ids(shape):
    return lax.broadcasted_iota(jnp.int32, shape, len(shape) - 1)


def swapped(x):
    up = pltpu.roll(x, W - 1, 1)
    low = pltpu.roll(x, 1, 1)
    return jnp.where(lane_ids(x.shape) % 2 == 0, up, low)


def merged(time_row, place_rows):
    return jnp.where(lane_ids(place_rows.shape) < RT, time_row, place_rows)


def rotate(x, cosine, sine):
    return x * cosine + swapped(x) * sine


def unrotate(x, cosine, sine):
    x = x.astype(BF16).astype(F32)
    return x * cosine - swapped(x) * sine


def pick_heads(hc, layers, spatial, ids):
    def look(h, n, layer):
        mine = (hc[layer, h] == 0) == spatial

        @pl.when(mine)
        def _():
            ids[n] = layer * HEADS + h

        return n + mine.astype(jnp.int32)

    found = jnp.int32(0)
    for layer in layers:
        found = lax.fori_loop(0, HEADS, lambda h, n: look(h, n, layer), found)
    return found


def lanes_of(h):
    return pl.ds(pl.multiple_of(h * W, W), W)


def pack_body(hc, place, q, k, v, g, ct, st, cp, sp, out, count, ids, cos_ref, sin_ref):
    layer = pl.program_id(0)

    @pl.when(layer == 0)
    def _():
        count[0] = 0
        frame = place[0]
        cos_ref[...] = merged(ct[pl.ds(frame, 1), :], cp[...])
        sin_ref[...] = merged(st[pl.ds(frame, 1), :], sp[...])

    first = count[0]
    found = pick_heads(hc, [layer], True, ids)
    count[0] = first + found

    def group(n, put):
        cosine, sine = cos_ref[...], sin_ref[...]
        for i in range(GROUP):
            lanes = lanes_of(ids[n * GROUP + i] - layer * HEADS)
            rq = rotate(q[0, 0, :, lanes].astype(F32), cosine, sine).astype(BF16)
            rk = rotate(k[0, 0, :, lanes].astype(F32), cosine, sine).astype(BF16)
            put(first + n * GROUP + i, rq, rk, v[0, 0, :, lanes], g[0, 0, :, lanes])

    def put_own(slot, *parts):
        for a in range(4):
            out[slot, a] = parts[a]

    def put_shared(slot, rq, rk, vv, gg):
        dest = (slot - SPACES) * 2
        out[dest, 4] = rq
        out[dest, 5] = gg
        out[dest + 1, 4] = rk
        out[dest + 1, 5] = vv

    def step(n, carry):
        own = first + n * GROUP < SPACES
        pl.when(own)(lambda: group(n, put_own))
        pl.when(jnp.logical_not(own))(lambda: group(n, put_shared))
        return carry

    lax.fori_loop(0, found // GROUP, step, 0)


SMALL = pl.BlockSpec((FRAMES, W), lambda i, h, p: (0, 0))
LOCAL = pl.BlockSpec((ROWS, W), lambda i, h, p: (p[1], 0))
PACK_COST = pl.CostEstimate(flops=20_000_000, bytes_accessed=9_000_000, transcendentals=0)


def pack_spatial(meta, arrays, tabs):
    shape = (SPACES, 6, ROWS, W)
    part = pl.BlockSpec((1, 1, ROWS, HEADS * W), lambda l, h, p: (l, 0, 0, 0))
    return pl.pallas_call(
        pack_body,
        grid_spec=pltpu.PrefetchScalarGridSpec(
            num_scalar_prefetch=2,
            grid=(LAYERS,),
            in_specs=[part] * 4 + [SMALL, SMALL, LOCAL, LOCAL],
            out_specs=pl.BlockSpec(shape, lambda l, h, p: (0, 0, 0, 0)),
            scratch_shapes=[
                pltpu.SMEM((1,), jnp.int32),
                pltpu.SMEM((HEADS,), jnp.int32),
                pltpu.VMEM((ROWS, W), F32),
                pltpu.VMEM((ROWS, W), F32),
            ],
        ),
        out_shape=jax.ShapeDtypeStruct(shape, BF16),
        compiler_params=pltpu.CompilerParams(vmem_limit_bytes=VMEM),
        cost_estimate=PACK_COST,
        name="pack_spatial",
    )(*meta, *arrays, *tabs)


def peer(place, step, forward):
    frame = place[0]
    x, z = frame % 4, frame // 4
    dx, dz = step // 2, step % 2
    x = (x + (dx if forward else 4 - dx)) % 4
    return (1 - z if dz else z) * 4 + x


def pack_temporal_body(hc, place, q, k, v, g, ct, st, cp, sp, *rest):
    outs, (ids, cos_ref, sin_ref) = rest[:FRAMES], rest[FRAMES:]
    frame = place[0]
    cos_ref[...] = merged(ct[pl.ds(frame, 1), :], cp[...])
    sin_ref[...] = merged(st[pl.ds(frame, 1), :], sp[...])
    pick_heads(hc, range(LAYERS), False, ids)
    for step in range(FRAMES):
        cosine, sine = cos_ref[...], sin_ref[...]
        dest = peer(place, step, True)
        for i in range(3):
            flat_id = ids[dest * 3 + i]
            layer = flat_id // HEADS
            lanes = lanes_of(flat_id - layer * HEADS)
            out = outs[step]
            out[i * 4] = rotate(q[layer, 0, :, lanes].astype(F32), cosine, sine).astype(BF16)
            out[i * 4 + 1] = rotate(k[layer, 0, :, lanes].astype(F32), cosine, sine).astype(BF16)
            out[i * 4 + 2] = v[layer, 0, :, lanes]
            out[i * 4 + 3] = g[layer, 0, :, lanes]


def pack_temporal(meta, arrays, tabs):
    shape = (12, ROWS, W)
    return pl.pallas_call(
        pack_temporal_body,
        grid_spec=pltpu.PrefetchScalarGridSpec(
            num_scalar_prefetch=2,
            grid=(1,),
            in_specs=[whole(OUT)] * 4 + [SMALL, SMALL, LOCAL, LOCAL],
            out_specs=[whole(shape)] * FRAMES,
            scratch_shapes=[
                pltpu.SMEM((HEADS,), jnp.int32),
                pltpu.VMEM((ROWS, W), F32),
                pltpu.VMEM((ROWS, W), F32),
            ],
        ),
        out_shape=[jax.ShapeDtypeStruct(shape, BF16)] * FRAMES,
        compiler_params=pltpu.CompilerParams(vmem_limit_bytes=VMEM),
        cost_estimate=PACK_COST,
        name="pack_temporal",
    )(*meta, *arrays, *tabs)


CHUNKS = POSITIONS // KB
PAIR = KB // ROWS


def rows_of(j):
    return slice(j * KB, (j + 1) * KB)


def fold(op, total, strip):
    for r in range(0, STRIP, 8):
        total = op(total, strip[r : r + 8])
    return total


def strips(j):
    return [slice(r, r + STRIP) for r in range(j * KB, (j + 1) * KB, STRIP)]


def load_rows(ref, read, blocks):
    def load(j, carry):
        at = pl.ds(pl.multiple_of(j * KB, KB), KB)
        ref[at, :] = read(pl.ds(j * PAIR, PAIR)).astype(F32).reshape(KB, W).astype(BF16)
        return carry

    lax.fori_loop(0, blocks // PAIR, load, 0)
    used = blocks * ROWS
    if used < ref.shape[0]:
        ref[used:, :] = jnp.zeros((ref.shape[0] - used, W), BF16)


def attend_body(q, k, v, g, query_blocks, scratch):
    qs, ks, vs, gs, kt, qt, gt, s_a, s_b, d_a, d_b, p_ref, ds_ref, rows, qt_now, dk, dv, dq = scratch
    nq = -(-query_blocks * ROWS // QB)
    load_rows(qs, q, query_blocks)
    load_rows(gs, g, query_blocks)
    load_rows(ks, k, SPACES)
    load_rows(vs, v, SPACES)

    def queries(i):
        return pl.ds(pl.multiple_of(i * QB, QB), QB)

    def turn(i, carry):
        qt[i] = qs[queries(i), :].astype(F32).T.astype(BF16)
        gt[i] = gs[queries(i), :].astype(F32).T.astype(BF16)
        return carry

    lax.fori_loop(0, nq, turn, 0)
    for j in range(0, POSITIONS, W * 5):
        kt[:, j : j + W * 5] = ks[j : j + W * 5, :].astype(F32).T.astype(BF16)
    dk[...] = jnp.zeros_like(dk)
    dv[...] = jnp.zeros_like(dv)

    def products(j, turned_q, turned_g, refs):
        s_ref, d_ref = refs
        s_ref[rows_of(j), :] = jnp.dot(
            ks[rows_of(j), :], turned_q[...], preferred_element_type=F32
        )
        d_ref[rows_of(j), :] = jnp.dot(
            vs[rows_of(j), :], turned_g[...], preferred_element_type=F32
        )

    def highest(j, top, refs):
        for at in strips(j):
            top = fold(jnp.maximum, top, refs[0][at, :])
        return top

    low = jnp.full((8, QB), -jnp.inf, F32)
    zero = jnp.zeros((8, QB), F32)

    def block(i, qb, gb, top, refs, following):
        s_ref, d_ref = refs
        top = jnp.max(top, 0, keepdims=True) * SCALE2
        total, delta = zero, zero
        for j in range(CHUNKS):
            if following is not None:
                products(j, *following)
            for at in strips(j):
                p = jnp.exp2(s_ref[at, :] * SCALE2 - top)
                s_ref[at, :] = p
                total = fold(jnp.add, total, p)
                delta = fold(jnp.add, delta, p * d_ref[at, :])
        inverse = 1.0 / jnp.sum(total, 0, keepdims=True)
        delta = jnp.sum(delta, 0, keepdims=True) * inverse * SCALE
        after = low
        for j in range(CHUNKS):
            for at in strips(j):
                p = s_ref[at, :] * inverse
                p_ref[at, :] = p.astype(BF16)
                ds_ref[at, :] = (p * (d_ref[at, :] * SCALE - delta)).astype(BF16)
            if following is not None:
                after = highest(j, after, following[2])
            at = rows_of(j)
            dv[at, :] += jnp.dot(p_ref[at, :], gb[...], preferred_element_type=F32)
            dk[at, :] += jnp.dot(ds_ref[at, :], qb[...], preferred_element_type=F32)
        dq[queries(i), :] = jnp.dot(kt[...], ds_ref[...], preferred_element_type=F32).T
        return after

    one, two = (s_a, d_a), (s_b, d_b)

    def start(j, top):
        at = pl.ds(pl.multiple_of(j * KB, KB), KB)
        s = jnp.dot(ks[at, :], qt[0], preferred_element_type=F32)
        s_a[at, :] = s
        d_a[at, :] = jnp.dot(vs[at, :], gt[0], preferred_element_type=F32)
        return jnp.maximum(top, jnp.max(s.reshape(KB // 8, 8, QB), 0))

    top = lax.fori_loop(0, CHUNKS, start, low)

    def pair(n, top, last):
        for u in range(2):
            rows[2 * u] = qs[queries(2 * n + u), :]
            rows[2 * u + 1] = gs[queries(2 * n + u), :]
        for u in range(1 if last else 2):
            qt_now[2 * u] = qt[2 * n + 1 + u]
            qt_now[2 * u + 1] = gt[2 * n + 1 + u]
        top = block(
            2 * n, rows.at[0], rows.at[1], top, one, (qt_now.at[0], qt_now.at[1], two)
        )
        following = None if last else (qt_now.at[2], qt_now.at[3], one)
        return block(2 * n + 1, rows.at[2], rows.at[3], top, two, following)

    for n in range(nq // 2):
        top = pair(n, top, n == nq // 2 - 1)


def own_body(hc, place, x, ct, st, cp, sp, out, *scratch):
    frame = pl.ds(place[0], 1)
    attend_body(*[lambda two, a=a: x[two, a] for a in range(4)], SPACES, scratch)
    dk, dv, dq = scratch[-3:]

    def finish(n, carry):
        for b in [n * 2 + u for u in range(2)]:
            at = pl.ds(pl.multiple_of(b * ROWS, ROWS), ROWS)
            cosine = merged(ct[frame, :], cp[at, :])
            sine = merged(st[frame, :], sp[at, :])
            gq = unrotate(dq[at, :], cosine, sine)
            gk = unrotate(dk[at, :], cosine, sine)
            out[b] = jnp.concatenate([gq, gk, dv[at, :]], 0).astype(BF16)
        return carry

    lax.fori_loop(0, SPACES // 2, finish, 0)


def merge_body(hc, place, own, kept, given, ct, st, cp, sp, out):
    frame = pl.ds(place[0], 1)
    even = place[1] % 2 == 0
    ones, zeros = jnp.ones((ROWS, W), F32), jnp.zeros((ROWS, W), F32)
    extra = 2 * HALF - ROWS

    def rest_of(table, fill):
        tail = jnp.where(even, table[:HALF], jnp.concatenate([table[HALF:], fill[:extra]]))
        return jnp.concatenate([jnp.where(even, table, fill), tail])

    def finish(n, carry):
        for b in [n * 2 + u for u in range(2)]:
            at = pl.ds(pl.multiple_of(b * ROWS, ROWS), ROWS)
            cosine = rest_of(merged(ct[frame, :], cp[at, :]), ones)
            sine = rest_of(merged(st[frame, :], sp[at, :]), zeros)
            rest = unrotate(kept[b] + given[b], cosine, sine)
            out[b] = jnp.concatenate([own[b].astype(F32), rest], 0).astype(BF16)
        return carry

    lax.fori_loop(0, SPACES // 2, finish, 0)


def merge(meta, own, kept, given, tabs):
    shape = (SPACES, BACK, W)
    return pl.pallas_call(
        merge_body,
        grid_spec=pltpu.PrefetchScalarGridSpec(
            num_scalar_prefetch=2,
            grid=(1,),
            in_specs=[whole(x.shape) for x in (own, kept, given, *tabs)],
            out_specs=whole(shape),
        ),
        out_shape=jax.ShapeDtypeStruct(shape, BF16),
        compiler_params=pltpu.CompilerParams(vmem_limit_bytes=VMEM),
        cost_estimate=pl.CostEstimate(flops=5_000_000, bytes_accessed=9_000_000, transcendentals=0),
        name="merge",
    )(*meta, own, kept, given, *tabs)


def shared_body(hc, place, mine, other, keep, give, *scratch):
    core = place[1] % 2
    even = core == 0
    blocks = SPACES // 2

    def read(unit, holder):
        def pick(two):
            return jnp.where(core == holder, mine[two, unit], other[two, unit])

        return pick

    def half(pick):
        return lambda two: pick(pl.ds(two.start + core * blocks, two.size))

    attend_body(
        half(read(0, 0)), read(0, 1), read(1, 1), half(read(1, 0)), blocks, scratch
    )
    dk, dv, dq = scratch[-3:]
    empty = jnp.zeros((2 * HALF - ROWS, W), F32)

    def finish(b, carry):
        at = pl.ds(pl.multiple_of(b * ROWS, ROWS), ROWS)
        local = jnp.clip(b - core * blocks, 0, blocks - 1)
        have = (b // blocks) == core
        gq = dq[pl.ds(pl.multiple_of(local * ROWS, ROWS), ROWS), :]
        gq = jnp.where(have, gq, jnp.zeros_like(gq))
        gk = dk[at, :]
        one = jnp.concatenate([gq, gk[:HALF]], 0)
        two = jnp.concatenate([dv[at, :], gk[HALF:], empty], 0)
        keep[b] = jnp.where(even, one, two)
        give[b] = jnp.where(even, two, one)
        return carry

    lax.fori_loop(0, SPACES, finish, 0)


def attend_scratch(padded):
    nq = padded // QB
    return (
        [pltpu.VMEM((padded, W), BF16), pltpu.VMEM((POSITIONS, W), BF16)]
        + [pltpu.VMEM((POSITIONS, W), BF16), pltpu.VMEM((padded, W), BF16)]
        + [pltpu.VMEM((W, POSITIONS), BF16)]
        + [pltpu.VMEM((nq, W, QB), BF16)] * 2
        + [pltpu.VMEM((POSITIONS, QB), F32)] * 4
        + [pltpu.VMEM((POSITIONS, QB), BF16)] * 2
        + [pltpu.VMEM((4, QB, W), BF16), pltpu.VMEM((4, W, QB), BF16)]
        + [pltpu.VMEM((POSITIONS, W), F32)] * 2
        + [pltpu.VMEM((padded, W), F32)]
    )


ATTEND_COST = pl.CostEstimate(
    flops=10 * POSITIONS * POSITIONS * W,
    bytes_accessed=6_000_000,
    transcendentals=POSITIONS * POSITIONS,
)


def attend_own(meta, received, tabs):
    shape = (SPACES, 3 * ROWS, W)
    return pl.pallas_call(
        own_body,
        grid_spec=pltpu.PrefetchScalarGridSpec(
            num_scalar_prefetch=2,
            grid=(1,),
            in_specs=[whole((SPACES, 4, ROWS, W))] + [whole(t.shape) for t in tabs],
            out_specs=whole(shape),
            scratch_shapes=attend_scratch(PADDED),
        ),
        out_shape=jax.ShapeDtypeStruct(shape, BF16),
        compiler_params=pltpu.CompilerParams(vmem_limit_bytes=46 * MIB),
        cost_estimate=ATTEND_COST,
        name="attend_own",
    )(*meta, received, *tabs)


def attend_shared(meta, mine, other):
    shape = (SPACES, ROWS + HALF, W)
    return pl.pallas_call(
        shared_body,
        grid_spec=pltpu.PrefetchScalarGridSpec(
            num_scalar_prefetch=2,
            grid=(1,),
            in_specs=[whole(mine.shape), whole(other.shape)],
            out_specs=[whole(shape), whole(shape)],
            scratch_shapes=attend_scratch(PADDED // 2),
        ),
        out_shape=[jax.ShapeDtypeStruct(shape, F32)] * 2,
        compiler_params=pltpu.CompilerParams(vmem_limit_bytes=46 * MIB),
        cost_estimate=ATTEND_COST,
        name="attend_shared",
    )(*meta, mine, other)


def frames_body(hc, place, *refs):
    xs, (ct, st, cp, sp) = refs[:FRAMES], refs[FRAMES : FRAMES + 4]
    outs, (dq_ref, dk_ref, dv_ref) = refs[FRAMES + 4 : -3], refs[-3:]
    tokens = FRAMES * TP
    key_place = lax.broadcasted_iota(jnp.int32, (tokens, tokens), 0) % TP
    query_place = lax.broadcasted_iota(jnp.int32, (tokens, tokens), 1) % TP
    same = key_place == query_place
    nt = (((1,), (1,)), ((), ()))
    owners = [peer(place, step, False) for step in range(FRAMES)]

    def head(i, carry):
        for c in range(ROWS // TP):
            rows = slice(c * TP, (c + 1) * TP)
            q, k, v, g = (
                jnp.concatenate([x[i * 4 + a].astype(F32)[rows] for x in xs], 0).astype(BF16)
                for a in range(4)
            )
            s = lax.dot_general(k, q, nt, preferred_element_type=F32)
            s = jnp.where(same, s, -jnp.inf)
            p = jnp.exp2((s - jnp.max(s, 0, keepdims=True)) * SCALE2)
            p = p * (1.0 / jnp.sum(p, 0, keepdims=True))
            d = lax.dot_general(v, g, nt, preferred_element_type=F32)
            delta = jnp.sum(p * d, 0, keepdims=True)
            ds = p * ((d - delta) * SCALE)
            dst = ds.T.astype(BF16)
            ds = ds.astype(BF16)
            gv = jnp.dot(p.astype(BF16), g, preferred_element_type=F32)
            gk = jnp.dot(ds, q, preferred_element_type=F32)
            gq = jnp.dot(dst, k, preferred_element_type=F32)
            place_c, place_s = cp[rows, :], sp[rows, :]
            cosine = jnp.concatenate([merged(ct[pl.ds(f, 1), :], place_c) for f in owners], 0)
            sine = jnp.concatenate([merged(st[pl.ds(f, 1), :], place_s) for f in owners], 0)
            dq_ref[:, rows, :] = unrotate(gq, cosine, sine).reshape(FRAMES, TP, W)
            dk_ref[:, rows, :] = unrotate(gk, cosine, sine).reshape(FRAMES, TP, W)
            dv_ref[:, rows, :] = gv.reshape(FRAMES, TP, W)
        for step, out in enumerate(outs):
            out[i * 3] = dq_ref[step].astype(BF16)
            out[i * 3 + 1] = dk_ref[step].astype(BF16)
            out[i * 3 + 2] = dv_ref[step].astype(BF16)
        return carry

    lax.fori_loop(0, 3, head, 0)


def attend_frames(meta, received, tabs):
    shape = (9, ROWS, W)
    return pl.pallas_call(
        frames_body,
        grid_spec=pltpu.PrefetchScalarGridSpec(
            num_scalar_prefetch=2,
            grid=(1,),
            in_specs=[whole(x.shape) for x in received] + [SMALL, SMALL, LOCAL, LOCAL],
            out_specs=[whole(shape)] * FRAMES,
            scratch_shapes=[pltpu.VMEM((FRAMES, ROWS, W), F32)] * 3,
        ),
        out_shape=[jax.ShapeDtypeStruct(shape, BF16)] * FRAMES,
        compiler_params=pltpu.CompilerParams(vmem_limit_bytes=20 * MIB),
        cost_estimate=pl.CostEstimate(
            flops=2_000_000_000, bytes_accessed=6_000_000, transcendentals=600_000
        ),
        name="attend_frames",
    )(*meta, *received, *tabs)


def column(flat_id):
    layer = flat_id // HEADS
    return layer, 0, slice(None), lanes_of(flat_id - layer * HEADS)


def unpack_temporal_body(hc, place, *refs):
    xs, outs, (ids,) = refs[:FRAMES], refs[FRAMES : FRAMES + 3], refs[FRAMES + 3 :]
    pick_heads(hc, range(LAYERS), False, ids)
    for step in range(FRAMES):
        dest = peer(place, step, True)
        for i in range(3):
            at = column(ids[dest * 3 + i])
            for a, out in enumerate(outs):
                out[at] = xs[step][i * 3 + a]


def unpack_temporal(meta, returned):
    return pl.pallas_call(
        unpack_temporal_body,
        grid_spec=pltpu.PrefetchScalarGridSpec(
            num_scalar_prefetch=2,
            grid=(1,),
            in_specs=[whole(x.shape) for x in returned],
            out_specs=[whole(OUT)] * 3,
            scratch_shapes=[pltpu.SMEM((HEADS,), jnp.int32)],
        ),
        out_shape=[jax.ShapeDtypeStruct(OUT, BF16)] * 3,
        compiler_params=pltpu.CompilerParams(vmem_limit_bytes=20 * MIB),
        cost_estimate=pl.CostEstimate(flops=5_000_000, bytes_accessed=7_000_000, transcendentals=0),
        name="unpack_temporal",
    )(*meta, *returned)


def unpack_spatial_body(hc, place, x, iq, ik, iv, oq, ok, ov, ids, pieces, sems):
    outs = (oq, ok, ov)
    pick_heads(hc, range(LAYERS), True, ids)
    copies = []

    def put(slot, parts):
        for a, part in enumerate(parts):
            pieces[slot, a] = part.astype(BF16)
            copies.append(
                pltpu.make_async_copy(
                    pieces.at[slot, a], outs[a].at[column(ids[slot])], sems.at[slot, a]
                )
            )
            copies[-1].start()

    for n in range(SPACES // 2):
        one = x[2 * n].astype(F32)
        two = x[2 * n + 1].astype(F32)
        for slot, piece in ((2 * n, one), (2 * n + 1, two)):
            put(slot, [piece[a * ROWS : (a + 1) * ROWS] for a in range(3)])
        both = jnp.concatenate([one[4 * ROWS :], two[4 * ROWS : 5 * ROWS - HALF]], 0)
        put(SPACES + n, [one[3 * ROWS : 4 * ROWS], both, two[3 * ROWS : 4 * ROWS]])
    for copy in copies:
        copy.wait()


def unpack_spatial(meta, returned, partial):
    anywhere = pl.BlockSpec(memory_space=pl.ANY)
    return pl.pallas_call(
        unpack_spatial_body,
        grid_spec=pltpu.PrefetchScalarGridSpec(
            num_scalar_prefetch=2,
            grid=(1,),
            in_specs=[whole(returned.shape)] + [anywhere] * 3,
            out_specs=[anywhere] * 3,
            scratch_shapes=[
                pltpu.SMEM((HEADS,), jnp.int32),
                pltpu.VMEM((HEADS, 3, ROWS, W), BF16),
                pltpu.SemaphoreType.DMA((HEADS, 3)),
            ],
        ),
        out_shape=[jax.ShapeDtypeStruct(OUT, BF16)] * 3,
        input_output_aliases={3 + a: a for a in range(3)},
        compiler_params=pltpu.CompilerParams(vmem_limit_bytes=16 * MIB),
        cost_estimate=pl.CostEstimate(flops=0, bytes_accessed=5_000_000, transcendentals=0),
        name="unpack_spatial",
    )(*meta, returned, *partial)


def exchange(x):
    return lax.all_to_all(x, "space", split_axis=0, concat_axis=0, tiled=True)


SWAP = [(i, i ^ 1) for i in range(SPACES)]


def along_x(parts, sign):
    def move(step, part):
        dx = sign * (step // 2)
        if dx == 0:
            return part
        pairs = [(f, f // 4 * 4 + (f + dx) % 4) for f in range(FRAMES)]
        return lax.ppermute(part, "frame", pairs)

    return [move(step, part) for step, part in enumerate(parts)]


def along_z(parts):
    pairs = [(f, f ^ 4) for f in range(FRAMES)]
    return [lax.ppermute(x, "frame", pairs) if n % 2 else x for n, x in enumerate(parts)]


def tie(*values):
    return lax.optimization_barrier(values)


def on_device(queries, keys, values, grad_out, head_class):
    place = jnp.stack([lax.axis_index("frame"), lax.axis_index("space")]).astype(jnp.int32)
    meta = (head_class, place)
    tabs = tuple(jnp.asarray(t) for t in tables())
    arrays = (queries, keys, values, grad_out)
    got_s = exchange(pack_spatial(meta, arrays, tabs))
    half_t = along_x(pack_temporal(meta, arrays, tabs), 1)
    got_s, *half_t = tie(got_s, *half_t)
    got_t = along_z(half_t)
    mine = got_s[:, 4:6]
    other = lax.ppermute(mine, "space", SWAP)
    own = attend_own(meta, got_s, tabs)
    own, *got_t = tie(own, *got_t)
    grads_t = list(attend_frames(meta, got_t, tabs))
    mine, grads_t[0] = tie(mine, grads_t[0])
    kept, give = attend_shared(meta, mine, other)
    half_t = along_z(grads_t)
    kept, give, half_t[1], half_t[3], half_t[5] = tie(kept, give, half_t[1], half_t[3], half_t[5])
    given = lax.ppermute(give, "space", SWAP)
    back_s, *half_t = tie(merge(meta, own, kept, given, tabs), *half_t)
    home_s = exchange(back_s)
    partial = unpack_temporal(meta, along_x(half_t, -1))
    return tuple(unpack_spatial(meta, home_s, partial))


def solution(mesh):
    placed = P(None, "frame", "space", None)
    return jax.shard_map(
        on_device,
        mesh=mesh,
        in_specs=(placed, placed, placed, placed, P()),
        out_specs=(placed, placed, placed),
        check_vma=False,
    )
```

```python
import math

import jax
import jax.numpy as jnp
import numpy as np
from jax import lax
from jax.experimental import pallas as pl
from jax.experimental.pallas import tpu as pltpu
from jax.sharding import PartitionSpec as P

RT = 16
RS = 56
PW = 80
THETA = 256.0
W = RT + 2 * RS
HEADS = 24
LAYERS = 2
FRAMES = 8
SPACES = 16
ROWS = 120
POSITIONS = SPACES * ROWS
HALF = 64
BACK = 4 * ROWS + HALF
QB = 512
PADDED = 2048
KB = 240
STRIP = 16
TP = 24
GROUP = 4
MIB = 1024 * 1024
VMEM = 60 * MIB
SCALE = 1.0 / math.sqrt(W)
SCALE2 = SCALE * math.log2(math.e)
F32 = jnp.float32
BF16 = jnp.bfloat16


OUT = (LAYERS, 1, ROWS, HEADS * W)


def whole(shape):
    return pl.BlockSpec(shape, lambda i, h, p: (0,) * len(shape))


def tables():
    channel = np.arange(W)
    pair = channel // 2
    tpairs, spairs = RT // 2, RS // 2
    is_time = pair < tpairs
    is_row = (pair >= tpairs) & (pair < tpairs + spairs)
    local = np.where(is_time, pair, np.where(is_row, pair - tpairs, pair - tpairs - spairs))
    width = np.where(is_time, RT, RS)
    freq = THETA ** (-2.0 * local / width)
    sign = np.where(channel % 2 == 0, -1.0, 1.0)
    time = np.arange(FRAMES)[:, None] * freq
    position = np.arange(POSITIONS)[:, None]
    place = np.where(is_row, position // PW, position % PW) * freq
    return (
        np.cos(time).astype(np.float32),
        (np.sin(time) * sign).astype(np.float32),
        np.cos(place).astype(np.float32),
        (np.sin(place) * sign).astype(np.float32),
    )


def lane_ids(shape):
    return lax.broadcasted_iota(jnp.int32, shape, len(shape) - 1)


def swapped(x):
    up = pltpu.roll(x, W - 1, 1)
    low = pltpu.roll(x, 1, 1)
    return jnp.where(lane_ids(x.shape) % 2 == 0, up, low)


def merged(time_row, place_rows):
    return jnp.where(lane_ids(place_rows.shape) < RT, time_row, place_rows)


def rotate(x, cosine, sine):
    return x * cosine + swapped(x) * sine


def unrotate(x, cosine, sine):
    x = x.astype(BF16).astype(F32)
    return x * cosine - swapped(x) * sine


def pick_heads(hc, layers, spatial, ids):
    def look(h, n, layer):
        mine = (hc[layer, h] == 0) == spatial

        @pl.when(mine)
        def _():
            ids[n] = layer * HEADS + h

        return n + mine.astype(jnp.int32)

    found = jnp.int32(0)
    for layer in layers:
        found = lax.fori_loop(0, HEADS, lambda h, n: look(h, n, layer), found)
    return found


def lanes_of(h):
    return pl.ds(pl.multiple_of(h * W, W), W)


def pack_body(hc, place, q, k, v, g, ct, st, cp, sp, out, count, ids, cos_ref, sin_ref):
    layer = pl.program_id(0)

    @pl.when(layer == 0)
    def _():
        count[0] = 0
        frame = place[0]
        cos_ref[...] = merged(ct[pl.ds(frame, 1), :], cp[...])
        sin_ref[...] = merged(st[pl.ds(frame, 1), :], sp[...])

    first = count[0]
    found = pick_heads(hc, [layer], True, ids)
    count[0] = first + found

    def group(n, put):
        cosine, sine = cos_ref[...], sin_ref[...]
        for i in range(GROUP):
            lanes = lanes_of(ids[n * GROUP + i] - layer * HEADS)
            rq = rotate(q[0, 0, :, lanes].astype(F32), cosine, sine).astype(BF16)
            rk = rotate(k[0, 0, :, lanes].astype(F32), cosine, sine).astype(BF16)
            put(first + n * GROUP + i, rq, rk, v[0, 0, :, lanes], g[0, 0, :, lanes])

    def put_own(slot, *parts):
        for a in range(4):
            out[slot, a] = parts[a]

    def put_shared(slot, rq, rk, vv, gg):
        dest = (slot - SPACES) * 2
        out[dest, 4] = rq
        out[dest, 5] = gg
        out[dest + 1, 4] = rk
        out[dest + 1, 5] = vv

    def step(n, carry):
        own = first + n * GROUP < SPACES
        pl.when(own)(lambda: group(n, put_own))
        pl.when(jnp.logical_not(own))(lambda: group(n, put_shared))
        return carry

    lax.fori_loop(0, found // GROUP, step, 0)


SMALL = pl.BlockSpec((FRAMES, W), lambda i, h, p: (0, 0))
LOCAL = pl.BlockSpec((ROWS, W), lambda i, h, p: (p[1], 0))
PACK_COST = pl.CostEstimate(flops=20_000_000, bytes_accessed=9_000_000, transcendentals=0)


def pack_spatial(meta, arrays, tabs):
    shape = (SPACES, 6, ROWS, W)
    part = pl.BlockSpec((1, 1, ROWS, HEADS * W), lambda l, h, p: (l, 0, 0, 0))
    return pl.pallas_call(
        pack_body,
        grid_spec=pltpu.PrefetchScalarGridSpec(
            num_scalar_prefetch=2,
            grid=(LAYERS,),
            in_specs=[part] * 4 + [SMALL, SMALL, LOCAL, LOCAL],
            out_specs=pl.BlockSpec(shape, lambda l, h, p: (0, 0, 0, 0)),
            scratch_shapes=[
                pltpu.SMEM((1,), jnp.int32),
                pltpu.SMEM((HEADS,), jnp.int32),
                pltpu.VMEM((ROWS, W), F32),
                pltpu.VMEM((ROWS, W), F32),
            ],
        ),
        out_shape=jax.ShapeDtypeStruct(shape, BF16),
        compiler_params=pltpu.CompilerParams(vmem_limit_bytes=VMEM),
        cost_estimate=PACK_COST,
        name="pack_spatial",
    )(*meta, *arrays, *tabs)


def peer(place, step, forward):
    frame = place[0]
    x, z = frame % 4, frame // 4
    dx, dz = step // 2, step % 2
    x = (x + (dx if forward else 4 - dx)) % 4
    return (1 - z if dz else z) * 4 + x


def pack_temporal_body(hc, place, q, k, v, g, ct, st, cp, sp, *rest):
    outs, (ids, cos_ref, sin_ref) = rest[:FRAMES], rest[FRAMES:]
    frame = place[0]
    cos_ref[...] = merged(ct[pl.ds(frame, 1), :], cp[...])
    sin_ref[...] = merged(st[pl.ds(frame, 1), :], sp[...])
    pick_heads(hc, range(LAYERS), False, ids)
    for step in range(FRAMES):
        cosine, sine = cos_ref[...], sin_ref[...]
        dest = peer(place, step, True)
        for i in range(3):
            flat_id = ids[dest * 3 + i]
            layer = flat_id // HEADS
            lanes = lanes_of(flat_id - layer * HEADS)
            out = outs[step]
            out[i * 4] = rotate(q[layer, 0, :, lanes].astype(F32), cosine, sine).astype(BF16)
            out[i * 4 + 1] = rotate(k[layer, 0, :, lanes].astype(F32), cosine, sine).astype(BF16)
            out[i * 4 + 2] = v[layer, 0, :, lanes]
            out[i * 4 + 3] = g[layer, 0, :, lanes]


def pack_temporal(meta, arrays, tabs):
    shape = (12, ROWS, W)
    return pl.pallas_call(
        pack_temporal_body,
        grid_spec=pltpu.PrefetchScalarGridSpec(
            num_scalar_prefetch=2,
            grid=(1,),
            in_specs=[whole(OUT)] * 4 + [SMALL, SMALL, LOCAL, LOCAL],
            out_specs=[whole(shape)] * FRAMES,
            scratch_shapes=[
                pltpu.SMEM((HEADS,), jnp.int32),
                pltpu.VMEM((ROWS, W), F32),
                pltpu.VMEM((ROWS, W), F32),
            ],
        ),
        out_shape=[jax.ShapeDtypeStruct(shape, BF16)] * FRAMES,
        compiler_params=pltpu.CompilerParams(vmem_limit_bytes=VMEM),
        cost_estimate=PACK_COST,
        name="pack_temporal",
    )(*meta, *arrays, *tabs)


CHUNKS = POSITIONS // KB
PAIR = KB // ROWS


def rows_of(j):
    return slice(j * KB, (j + 1) * KB)


def fold(op, total, strip):
    for r in range(0, STRIP, 8):
        total = op(total, strip[r : r + 8])
    return total


def strips(j):
    return [slice(r, r + STRIP) for r in range(j * KB, (j + 1) * KB, STRIP)]


def load_rows(ref, read, blocks):
    def load(j, carry):
        at = pl.ds(pl.multiple_of(j * KB, KB), KB)
        ref[at, :] = read(pl.ds(j * PAIR, PAIR)).astype(F32).reshape(KB, W).astype(BF16)
        return carry

    lax.fori_loop(0, blocks // PAIR, load, 0)
    used = blocks * ROWS
    if used < ref.shape[0]:
        ref[used:, :] = jnp.zeros((ref.shape[0] - used, W), BF16)


def attend_body(q, k, v, g, query_blocks, scratch):
    qs, ks, vs, gs, kt, qt, gt, s_a, s_b, d_a, d_b, p_ref, ds_ref, rows, qt_now, dk, dv, dq = scratch
    nq = -(-query_blocks * ROWS // QB)
    load_rows(qs, q, query_blocks)
    load_rows(gs, g, query_blocks)
    load_rows(ks, k, SPACES)
    load_rows(vs, v, SPACES)

    def queries(i):
        return pl.ds(pl.multiple_of(i * QB, QB), QB)

    def turn(i, carry):
        qt[i] = qs[queries(i), :].astype(F32).T.astype(BF16)
        gt[i] = gs[queries(i), :].astype(F32).T.astype(BF16)
        return carry

    lax.fori_loop(0, nq, turn, 0)
    for j in range(0, POSITIONS, W * 5):
        kt[:, j : j + W * 5] = ks[j : j + W * 5, :].astype(F32).T.astype(BF16)
    dk[...] = jnp.zeros_like(dk)
    dv[...] = jnp.zeros_like(dv)

    def products(j, turned_q, turned_g, refs):
        s_ref, d_ref = refs
        s_ref[rows_of(j), :] = jnp.dot(
            ks[rows_of(j), :], turned_q[...], preferred_element_type=F32
        )
        d_ref[rows_of(j), :] = jnp.dot(
            vs[rows_of(j), :], turned_g[...], preferred_element_type=F32
        )

    def highest(j, top, refs):
        for at in strips(j):
            top = fold(jnp.maximum, top, refs[0][at, :])
        return top

    low = jnp.full((8, QB), -jnp.inf, F32)
    zero = jnp.zeros((8, QB), F32)

    def block(i, qb, gb, top, refs, following):
        s_ref, d_ref = refs
        top = jnp.max(top, 0, keepdims=True) * SCALE2
        total, delta = zero, zero
        for j in range(CHUNKS):
            if following is not None:
                products(j, *following)
            for at in strips(j):
                p = jnp.exp2(s_ref[at, :] * SCALE2 - top)
                s_ref[at, :] = p
                total = fold(jnp.add, total, p)
                delta = fold(jnp.add, delta, p * d_ref[at, :])
        inverse = 1.0 / jnp.sum(total, 0, keepdims=True)
        delta = jnp.sum(delta, 0, keepdims=True) * inverse * SCALE
        after = low
        for j in range(CHUNKS):
            for at in strips(j):
                p = s_ref[at, :] * inverse
                p_ref[at, :] = p.astype(BF16)
                ds_ref[at, :] = (p * (d_ref[at, :] * SCALE - delta)).astype(BF16)
            if following is not None:
                after = highest(j, after, following[2])
            at = rows_of(j)
            dv[at, :] += jnp.dot(p_ref[at, :], gb[...], preferred_element_type=F32)
            dk[at, :] += jnp.dot(ds_ref[at, :], qb[...], preferred_element_type=F32)
        dq[queries(i), :] = jnp.dot(kt[...], ds_ref[...], preferred_element_type=F32).T
        return after

    one, two = (s_a, d_a), (s_b, d_b)

    def start(j, top):
        at = pl.ds(pl.multiple_of(j * KB, KB), KB)
        s = jnp.dot(ks[at, :], qt[0], preferred_element_type=F32)
        s_a[at, :] = s
        d_a[at, :] = jnp.dot(vs[at, :], gt[0], preferred_element_type=F32)
        return jnp.maximum(top, jnp.max(s.reshape(KB // 8, 8, QB), 0))

    top = lax.fori_loop(0, CHUNKS, start, low)

    def pair(n, top, last):
        for u in range(2):
            rows[2 * u] = qs[queries(2 * n + u), :]
            rows[2 * u + 1] = gs[queries(2 * n + u), :]
        for u in range(1 if last else 2):
            qt_now[2 * u] = qt[2 * n + 1 + u]
            qt_now[2 * u + 1] = gt[2 * n + 1 + u]
        top = block(
            2 * n, rows.at[0], rows.at[1], top, one, (qt_now.at[0], qt_now.at[1], two)
        )
        following = None if last else (qt_now.at[2], qt_now.at[3], one)
        return block(2 * n + 1, rows.at[2], rows.at[3], top, two, following)

    for n in range(nq // 2):
        top = pair(n, top, n == nq // 2 - 1)


def own_body(hc, place, x, ct, st, cp, sp, out, *scratch):
    frame = pl.ds(place[0], 1)
    attend_body(*[lambda two, a=a: x[two, a] for a in range(4)], SPACES, scratch)
    dk, dv, dq = scratch[-3:]

    def finish(n, carry):
        for b in [n * 2 + u for u in range(2)]:
            at = pl.ds(pl.multiple_of(b * ROWS, ROWS), ROWS)
            cosine = merged(ct[frame, :], cp[at, :])
            sine = merged(st[frame, :], sp[at, :])
            gq = unrotate(dq[at, :], cosine, sine)
            gk = unrotate(dk[at, :], cosine, sine)
            out[b] = jnp.concatenate([gq, gk, dv[at, :]], 0).astype(BF16)
        return carry

    lax.fori_loop(0, SPACES // 2, finish, 0)


def merge_body(hc, place, own, kept, given, ct, st, cp, sp, out):
    frame = pl.ds(place[0], 1)
    even = place[1] % 2 == 0
    ones, zeros = jnp.ones((ROWS, W), F32), jnp.zeros((ROWS, W), F32)
    extra = 2 * HALF - ROWS

    def rest_of(table, fill):
        tail = jnp.where(even, table[:HALF], jnp.concatenate([table[HALF:], fill[:extra]]))
        return jnp.concatenate([jnp.where(even, table, fill), tail])

    def finish(n, carry):
        for b in [n * 2 + u for u in range(2)]:
            at = pl.ds(pl.multiple_of(b * ROWS, ROWS), ROWS)
            cosine = rest_of(merged(ct[frame, :], cp[at, :]), ones)
            sine = rest_of(merged(st[frame, :], sp[at, :]), zeros)
            rest = unrotate(kept[b] + given[b], cosine, sine)
            out[b] = jnp.concatenate([own[b].astype(F32), rest], 0).astype(BF16)
        return carry

    lax.fori_loop(0, SPACES // 2, finish, 0)


def merge(meta, own, kept, given, tabs):
    shape = (SPACES, BACK, W)
    return pl.pallas_call(
        merge_body,
        grid_spec=pltpu.PrefetchScalarGridSpec(
            num_scalar_prefetch=2,
            grid=(1,),
            in_specs=[whole(x.shape) for x in (own, kept, given, *tabs)],
            out_specs=whole(shape),
        ),
        out_shape=jax.ShapeDtypeStruct(shape, BF16),
        compiler_params=pltpu.CompilerParams(vmem_limit_bytes=32 * MIB),
        cost_estimate=pl.CostEstimate(flops=5_000_000, bytes_accessed=9_000_000, transcendentals=0),
        name="merge",
    )(*meta, own, kept, given, *tabs)


def shared_body(hc, place, mine, other, keep, give, *scratch):
    core = place[1] % 2
    even = core == 0
    blocks = SPACES // 2

    def read(unit, holder):
        def pick(two):
            return jnp.where(core == holder, mine[two, unit], other[two, unit])

        return pick

    def half(pick):
        return lambda two: pick(pl.ds(two.start + core * blocks, two.size))

    attend_body(
        half(read(0, 0)), read(0, 1), read(1, 1), half(read(1, 0)), blocks, scratch
    )
    dk, dv, dq = scratch[-3:]
    empty = jnp.zeros((2 * HALF - ROWS, W), F32)

    def finish(b, carry):
        at = pl.ds(pl.multiple_of(b * ROWS, ROWS), ROWS)
        local = jnp.clip(b - core * blocks, 0, blocks - 1)
        have = (b // blocks) == core
        gq = dq[pl.ds(pl.multiple_of(local * ROWS, ROWS), ROWS), :]
        gq = jnp.where(have, gq, jnp.zeros_like(gq))
        gk = dk[at, :]
        one = jnp.concatenate([gq, gk[:HALF]], 0)
        two = jnp.concatenate([dv[at, :], gk[HALF:], empty], 0)
        keep[b] = jnp.where(even, one, two)
        give[b] = jnp.where(even, two, one)
        return carry

    lax.fori_loop(0, SPACES, finish, 0)


def attend_scratch(padded):
    nq = padded // QB
    return (
        [pltpu.VMEM((padded, W), BF16), pltpu.VMEM((POSITIONS, W), BF16)]
        + [pltpu.VMEM((POSITIONS, W), BF16), pltpu.VMEM((padded, W), BF16)]
        + [pltpu.VMEM((W, POSITIONS), BF16)]
        + [pltpu.VMEM((nq, W, QB), BF16)] * 2
        + [pltpu.VMEM((POSITIONS, QB), F32)] * 4
        + [pltpu.VMEM((POSITIONS, QB), BF16)] * 2
        + [pltpu.VMEM((4, QB, W), BF16), pltpu.VMEM((4, W, QB), BF16)]
        + [pltpu.VMEM((POSITIONS, W), F32)] * 2
        + [pltpu.VMEM((padded, W), F32)]
    )


ATTEND_COST = pl.CostEstimate(
    flops=10 * POSITIONS * POSITIONS * W,
    bytes_accessed=6_000_000,
    transcendentals=POSITIONS * POSITIONS,
)


def attend_own(meta, received, tabs):
    shape = (SPACES, 3 * ROWS, W)
    return pl.pallas_call(
        own_body,
        grid_spec=pltpu.PrefetchScalarGridSpec(
            num_scalar_prefetch=2,
            grid=(1,),
            in_specs=[whole((SPACES, 4, ROWS, W))] + [whole(t.shape) for t in tabs],
            out_specs=whole(shape),
            scratch_shapes=attend_scratch(PADDED),
        ),
        out_shape=jax.ShapeDtypeStruct(shape, BF16),
        compiler_params=pltpu.CompilerParams(vmem_limit_bytes=46 * MIB),
        cost_estimate=ATTEND_COST,
        name="attend_own",
    )(*meta, received, *tabs)


def attend_shared(meta, mine, other):
    shape = (SPACES, ROWS + HALF, W)
    return pl.pallas_call(
        shared_body,
        grid_spec=pltpu.PrefetchScalarGridSpec(
            num_scalar_prefetch=2,
            grid=(1,),
            in_specs=[whole(mine.shape), whole(other.shape)],
            out_specs=[whole(shape), whole(shape)],
            scratch_shapes=attend_scratch(PADDED // 2),
        ),
        out_shape=[jax.ShapeDtypeStruct(shape, F32)] * 2,
        compiler_params=pltpu.CompilerParams(vmem_limit_bytes=46 * MIB),
        cost_estimate=ATTEND_COST,
        name="attend_shared",
    )(*meta, mine, other)


def frames_body(hc, place, *refs):
    xs, (ct, st, cp, sp) = refs[:FRAMES], refs[FRAMES : FRAMES + 4]
    outs, (dq_ref, dk_ref, dv_ref) = refs[FRAMES + 4 : -3], refs[-3:]
    tokens = FRAMES * TP
    key_place = lax.broadcasted_iota(jnp.int32, (tokens, tokens), 0) % TP
    query_place = lax.broadcasted_iota(jnp.int32, (tokens, tokens), 1) % TP
    same = key_place == query_place
    nt = (((1,), (1,)), ((), ()))
    owners = [peer(place, step, False) for step in range(FRAMES)]

    def head(i, carry):
        for c in range(ROWS // TP):
            rows = slice(c * TP, (c + 1) * TP)
            q, k, v, g = (
                jnp.concatenate([x[i * 4 + a].astype(F32)[rows] for x in xs], 0).astype(BF16)
                for a in range(4)
            )
            s = lax.dot_general(k, q, nt, preferred_element_type=F32)
            s = jnp.where(same, s, -jnp.inf)
            p = jnp.exp2((s - jnp.max(s, 0, keepdims=True)) * SCALE2)
            p = p * (1.0 / jnp.sum(p, 0, keepdims=True))
            d = lax.dot_general(v, g, nt, preferred_element_type=F32)
            delta = jnp.sum(p * d, 0, keepdims=True)
            ds = p * ((d - delta) * SCALE)
            dst = ds.T.astype(BF16)
            ds = ds.astype(BF16)
            gv = jnp.dot(p.astype(BF16), g, preferred_element_type=F32)
            gk = jnp.dot(ds, q, preferred_element_type=F32)
            gq = jnp.dot(dst, k, preferred_element_type=F32)
            place_c, place_s = cp[rows, :], sp[rows, :]
            cosine = jnp.concatenate([merged(ct[pl.ds(f, 1), :], place_c) for f in owners], 0)
            sine = jnp.concatenate([merged(st[pl.ds(f, 1), :], place_s) for f in owners], 0)
            dq_ref[:, rows, :] = unrotate(gq, cosine, sine).reshape(FRAMES, TP, W)
            dk_ref[:, rows, :] = unrotate(gk, cosine, sine).reshape(FRAMES, TP, W)
            dv_ref[:, rows, :] = gv.reshape(FRAMES, TP, W)
        for step, out in enumerate(outs):
            out[i * 3] = dq_ref[step].astype(BF16)
            out[i * 3 + 1] = dk_ref[step].astype(BF16)
            out[i * 3 + 2] = dv_ref[step].astype(BF16)
        return carry

    lax.fori_loop(0, 3, head, 0)


def attend_frames(meta, received, tabs):
    shape = (9, ROWS, W)
    return pl.pallas_call(
        frames_body,
        grid_spec=pltpu.PrefetchScalarGridSpec(
            num_scalar_prefetch=2,
            grid=(1,),
            in_specs=[whole(x.shape) for x in received] + [SMALL, SMALL, LOCAL, LOCAL],
            out_specs=[whole(shape)] * FRAMES,
            scratch_shapes=[pltpu.VMEM((FRAMES, ROWS, W), F32)] * 3,
        ),
        out_shape=[jax.ShapeDtypeStruct(shape, BF16)] * FRAMES,
        compiler_params=pltpu.CompilerParams(vmem_limit_bytes=20 * MIB),
        cost_estimate=pl.CostEstimate(
            flops=2_000_000_000, bytes_accessed=6_000_000, transcendentals=600_000
        ),
        name="attend_frames",
    )(*meta, *received, *tabs)


def column(flat_id):
    layer = flat_id // HEADS
    return layer, 0, slice(None), lanes_of(flat_id - layer * HEADS)


def unpack_temporal_body(hc, place, *refs):
    xs, outs, (ids,) = refs[:FRAMES], refs[FRAMES : FRAMES + 3], refs[FRAMES + 3 :]
    pick_heads(hc, range(LAYERS), False, ids)
    for step in range(FRAMES):
        dest = peer(place, step, True)
        for i in range(3):
            at = column(ids[dest * 3 + i])
            for a, out in enumerate(outs):
                out[at] = xs[step][i * 3 + a]


def unpack_temporal(meta, returned):
    return pl.pallas_call(
        unpack_temporal_body,
        grid_spec=pltpu.PrefetchScalarGridSpec(
            num_scalar_prefetch=2,
            grid=(1,),
            in_specs=[whole(x.shape) for x in returned],
            out_specs=[whole(OUT)] * 3,
            scratch_shapes=[pltpu.SMEM((HEADS,), jnp.int32)],
        ),
        out_shape=[jax.ShapeDtypeStruct(OUT, BF16)] * 3,
        compiler_params=pltpu.CompilerParams(vmem_limit_bytes=20 * MIB),
        cost_estimate=pl.CostEstimate(flops=5_000_000, bytes_accessed=7_000_000, transcendentals=0),
        name="unpack_temporal",
    )(*meta, *returned)


def unpack_spatial_body(hc, place, x, iq, ik, iv, oq, ok, ov, ids, pieces, sems):
    outs = (oq, ok, ov)
    pick_heads(hc, range(LAYERS), True, ids)
    copies = []

    def put(slot, parts):
        for a, part in enumerate(parts):
            pieces[slot, a] = part.astype(BF16)
            copies.append(
                pltpu.make_async_copy(
                    pieces.at[slot, a], outs[a].at[column(ids[slot])], sems.at[slot, a]
                )
            )
            copies[-1].start()

    for n in range(SPACES // 2):
        one = x[2 * n].astype(F32)
        two = x[2 * n + 1].astype(F32)
        for slot, piece in ((2 * n, one), (2 * n + 1, two)):
            put(slot, [piece[a * ROWS : (a + 1) * ROWS] for a in range(3)])
        both = jnp.concatenate([one[4 * ROWS :], two[4 * ROWS : 5 * ROWS - HALF]], 0)
        put(SPACES + n, [one[3 * ROWS : 4 * ROWS], both, two[3 * ROWS : 4 * ROWS]])
    for copy in copies:
        copy.wait()


def unpack_spatial(meta, returned, partial):
    anywhere = pl.BlockSpec(memory_space=pl.ANY)
    return pl.pallas_call(
        unpack_spatial_body,
        grid_spec=pltpu.PrefetchScalarGridSpec(
            num_scalar_prefetch=2,
            grid=(1,),
            in_specs=[whole(returned.shape)] + [anywhere] * 3,
            out_specs=[anywhere] * 3,
            scratch_shapes=[
                pltpu.SMEM((HEADS,), jnp.int32),
                pltpu.VMEM((HEADS, 3, ROWS, W), BF16),
                pltpu.SemaphoreType.DMA((HEADS, 3)),
            ],
        ),
        out_shape=[jax.ShapeDtypeStruct(OUT, BF16)] * 3,
        input_output_aliases={3 + a: a for a in range(3)},
        compiler_params=pltpu.CompilerParams(vmem_limit_bytes=16 * MIB),
        cost_estimate=pl.CostEstimate(flops=0, bytes_accessed=5_000_000, transcendentals=0),
        name="unpack_spatial",
    )(*meta, returned, *partial)


def exchange(x):
    return lax.all_to_all(x, "space", split_axis=0, concat_axis=0, tiled=True)


SWAP = [(i, i ^ 1) for i in range(SPACES)]


def along_x(parts, sign):
    def move(step, part):
        dx = sign * (step // 2)
        if dx == 0:
            return part
        pairs = [(f, f // 4 * 4 + (f + dx) % 4) for f in range(FRAMES)]
        return lax.ppermute(part, "frame", pairs)

    return [move(step, part) for step, part in enumerate(parts)]


def along_z(parts):
    pairs = [(f, f ^ 4) for f in range(FRAMES)]
    return [lax.ppermute(x, "frame", pairs) if n % 2 else x for n, x in enumerate(parts)]


def tie(*values):
    return lax.optimization_barrier(values)


def on_device(queries, keys, values, grad_out, head_class):
    place = jnp.stack([lax.axis_index("frame"), lax.axis_index("space")]).astype(jnp.int32)
    meta = (head_class, place)
    tabs = tuple(jnp.asarray(t) for t in tables())
    arrays = (queries, keys, values, grad_out)
    got_s = exchange(pack_spatial(meta, arrays, tabs))
    half_t = along_x(pack_temporal(meta, arrays, tabs), 1)
    got_s, *half_t = tie(got_s, *half_t)
    got_t = along_z(half_t)
    mine = got_s[:, 4:6]
    other = lax.ppermute(mine, "space", SWAP)
    own = attend_own(meta, got_s, tabs)
    own, mine, got_t[1], got_t[3], got_t[5] = tie(own, mine, got_t[1], got_t[3], got_t[5])
    kept, give = attend_shared(meta, mine, other)
    kept, give, *got_t = tie(kept, give, *got_t)
    given = lax.ppermute(give, "space", SWAP)
    grads_t = list(attend_frames(meta, got_t, tabs))
    kept, grads_t[0] = tie(kept, grads_t[0])
    half_t = along_z(grads_t)
    back_s, half_t[1] = tie(merge(meta, own, kept, given, tabs), half_t[1])
    home_s = exchange(back_s)
    partial = unpack_temporal(meta, along_x(half_t, -1))
    return tuple(unpack_spatial(meta, home_s, partial))


def solution(mesh):
    placed = P(None, "frame", "space", None)
    return jax.shard_map(
        on_device,
        mesh=mesh,
        in_specs=(placed, placed, placed, placed, P()),
        out_specs=(placed, placed, placed),
        check_vma=False,
    )
```

```python
import math

import jax
import jax.numpy as jnp
import numpy as np
from jax import lax
from jax.experimental import pallas as pl
from jax.experimental.pallas import tpu as pltpu
from jax.sharding import PartitionSpec as P

RT = 16
RS = 56
PW = 80
THETA = 256.0
W = RT + 2 * RS
HEADS = 24
LAYERS = 2
FRAMES = 8
SPACES = 16
ROWS = 120
POSITIONS = SPACES * ROWS
HALF = 64
BACK = 4 * ROWS + HALF
QB = 512
PADDED = 2048
KB = 240
STRIP = 16
TP = 24
GROUP = 4
MIB = 1024 * 1024
VMEM = 60 * MIB
SCALE = 1.0 / math.sqrt(W)
SCALE2 = SCALE * math.log2(math.e)
F32 = jnp.float32
BF16 = jnp.bfloat16


OUT = (LAYERS, 1, ROWS, HEADS * W)


def whole(shape):
    return pl.BlockSpec(shape, lambda i, h, p: (0,) * len(shape))


def tables():
    channel = np.arange(W)
    pair = channel // 2
    tpairs, spairs = RT // 2, RS // 2
    is_time = pair < tpairs
    is_row = (pair >= tpairs) & (pair < tpairs + spairs)
    local = np.where(is_time, pair, np.where(is_row, pair - tpairs, pair - tpairs - spairs))
    width = np.where(is_time, RT, RS)
    freq = THETA ** (-2.0 * local / width)
    sign = np.where(channel % 2 == 0, -1.0, 1.0)
    time = np.arange(FRAMES)[:, None] * freq
    position = np.arange(POSITIONS)[:, None]
    place = np.where(is_row, position // PW, position % PW) * freq
    return (
        np.cos(time).astype(np.float32),
        (np.sin(time) * sign).astype(np.float32),
        np.cos(place).astype(np.float32),
        (np.sin(place) * sign).astype(np.float32),
    )


def lane_ids(shape):
    return lax.broadcasted_iota(jnp.int32, shape, len(shape) - 1)


def swapped(x):
    up = pltpu.roll(x, W - 1, 1)
    low = pltpu.roll(x, 1, 1)
    return jnp.where(lane_ids(x.shape) % 2 == 0, up, low)


def merged(time_row, place_rows):
    return jnp.where(lane_ids(place_rows.shape) < RT, time_row, place_rows)


def rotate(x, cosine, sine):
    return x * cosine + swapped(x) * sine


def unrotate(x, cosine, sine):
    x = x.astype(BF16).astype(F32)
    return x * cosine - swapped(x) * sine


def pick_heads(hc, layers, spatial, ids):
    def look(h, n, layer):
        mine = (hc[layer, h] == 0) == spatial

        @pl.when(mine)
        def _():
            ids[n] = layer * HEADS + h

        return n + mine.astype(jnp.int32)

    found = jnp.int32(0)
    for layer in layers:
        found = lax.fori_loop(0, HEADS, lambda h, n: look(h, n, layer), found)
    return found


def lanes_of(h):
    return pl.ds(pl.multiple_of(h * W, W), W)


def pack_body(hc, place, q, k, v, g, ct, st, cp, sp, out, count, ids, cos_ref, sin_ref):
    layer = pl.program_id(0)

    @pl.when(layer == 0)
    def _():
        count[0] = 0
        frame = place[0]
        cos_ref[...] = merged(ct[pl.ds(frame, 1), :], cp[...])
        sin_ref[...] = merged(st[pl.ds(frame, 1), :], sp[...])

    first = count[0]
    found = pick_heads(hc, [layer], True, ids)
    count[0] = first + found

    def group(n, put):
        cosine, sine = cos_ref[...], sin_ref[...]
        for i in range(GROUP):
            lanes = lanes_of(ids[n * GROUP + i] - layer * HEADS)
            rq = rotate(q[0, 0, :, lanes].astype(F32), cosine, sine).astype(BF16)
            rk = rotate(k[0, 0, :, lanes].astype(F32), cosine, sine).astype(BF16)
            put(first + n * GROUP + i, rq, rk, v[0, 0, :, lanes], g[0, 0, :, lanes])

    def put_own(slot, *parts):
        for a in range(4):
            out[slot, a] = parts[a]

    def put_shared(slot, rq, rk, vv, gg):
        dest = (slot - SPACES) * 2
        out[dest, 4] = rq
        out[dest, 5] = gg
        out[dest + 1, 4] = rk
        out[dest + 1, 5] = vv

    def step(n, carry):
        own = first + n * GROUP < SPACES
        pl.when(own)(lambda: group(n, put_own))
        pl.when(jnp.logical_not(own))(lambda: group(n, put_shared))
        return carry

    lax.fori_loop(0, found // GROUP, step, 0)


SMALL = pl.BlockSpec((FRAMES, W), lambda i, h, p: (0, 0))
LOCAL = pl.BlockSpec((ROWS, W), lambda i, h, p: (p[1], 0))
PACK_COST = pl.CostEstimate(flops=20_000_000, bytes_accessed=9_000_000, transcendentals=0)


def pack_spatial(meta, arrays, tabs):
    shape = (SPACES, 6, ROWS, W)
    part = pl.BlockSpec((1, 1, ROWS, HEADS * W), lambda l, h, p: (l, 0, 0, 0))
    return pl.pallas_call(
        pack_body,
        grid_spec=pltpu.PrefetchScalarGridSpec(
            num_scalar_prefetch=2,
            grid=(LAYERS,),
            in_specs=[part] * 4 + [SMALL, SMALL, LOCAL, LOCAL],
            out_specs=pl.BlockSpec(shape, lambda l, h, p: (0, 0, 0, 0)),
            scratch_shapes=[
                pltpu.SMEM((1,), jnp.int32),
                pltpu.SMEM((HEADS,), jnp.int32),
                pltpu.VMEM((ROWS, W), F32),
                pltpu.VMEM((ROWS, W), F32),
            ],
        ),
        out_shape=jax.ShapeDtypeStruct(shape, BF16),
        compiler_params=pltpu.CompilerParams(vmem_limit_bytes=VMEM),
        cost_estimate=PACK_COST,
        name="pack_spatial",
    )(*meta, *arrays, *tabs)


def peer(place, step, forward):
    frame = place[0]
    x, z = frame % 4, frame // 4
    dx, dz = step // 2, step % 2
    x = (x + (dx if forward else 4 - dx)) % 4
    return (1 - z if dz else z) * 4 + x


def pack_temporal_body(hc, place, q, k, v, g, ct, st, cp, sp, *rest):
    outs, (ids, cos_ref, sin_ref) = rest[:FRAMES], rest[FRAMES:]
    frame = place[0]
    cos_ref[...] = merged(ct[pl.ds(frame, 1), :], cp[...])
    sin_ref[...] = merged(st[pl.ds(frame, 1), :], sp[...])
    pick_heads(hc, range(LAYERS), False, ids)
    for step in range(FRAMES):
        cosine, sine = cos_ref[...], sin_ref[...]
        dest = peer(place, step, True)
        for i in range(3):
            flat_id = ids[dest * 3 + i]
            layer = flat_id // HEADS
            lanes = lanes_of(flat_id - layer * HEADS)
            out = outs[step]
            out[i * 4] = rotate(q[layer, 0, :, lanes].astype(F32), cosine, sine).astype(BF16)
            out[i * 4 + 1] = rotate(k[layer, 0, :, lanes].astype(F32), cosine, sine).astype(BF16)
            out[i * 4 + 2] = v[layer, 0, :, lanes]
            out[i * 4 + 3] = g[layer, 0, :, lanes]


def pack_temporal(meta, arrays, tabs):
    shape = (12, ROWS, W)
    return pl.pallas_call(
        pack_temporal_body,
        grid_spec=pltpu.PrefetchScalarGridSpec(
            num_scalar_prefetch=2,
            grid=(1,),
            in_specs=[whole(OUT)] * 4 + [SMALL, SMALL, LOCAL, LOCAL],
            out_specs=[whole(shape)] * FRAMES,
            scratch_shapes=[
                pltpu.SMEM((HEADS,), jnp.int32),
                pltpu.VMEM((ROWS, W), F32),
                pltpu.VMEM((ROWS, W), F32),
            ],
        ),
        out_shape=[jax.ShapeDtypeStruct(shape, BF16)] * FRAMES,
        compiler_params=pltpu.CompilerParams(vmem_limit_bytes=VMEM),
        cost_estimate=PACK_COST,
        name="pack_temporal",
    )(*meta, *arrays, *tabs)


CHUNKS = POSITIONS // KB
PAIR = KB // ROWS


def rows_of(j):
    return slice(j * KB, (j + 1) * KB)


def fold(op, total, strip):
    for r in range(0, STRIP, 8):
        total = op(total, strip[r : r + 8])
    return total


def strips(j):
    return [slice(r, r + STRIP) for r in range(j * KB, (j + 1) * KB, STRIP)]


def load_rows(ref, read, blocks):
    def load(j, carry):
        at = pl.ds(pl.multiple_of(j * KB, KB), KB)
        ref[at, :] = read(pl.ds(j * PAIR, PAIR)).astype(F32).reshape(KB, W).astype(BF16)
        return carry

    lax.fori_loop(0, blocks // PAIR, load, 0)
    used = blocks * ROWS
    if used < ref.shape[0]:
        ref[used:, :] = jnp.zeros((ref.shape[0] - used, W), BF16)


def attend_body(q, k, v, g, query_blocks, scratch):
    qs, ks, vs, gs, kt, qt, gt, s_a, s_b, d_a, d_b, p_ref, ds_ref, rows, qt_now, dk, dv, dq = scratch
    nq = -(-query_blocks * ROWS // QB)
    load_rows(qs, q, query_blocks)
    load_rows(gs, g, query_blocks)
    load_rows(ks, k, SPACES)
    load_rows(vs, v, SPACES)

    def queries(i):
        return pl.ds(pl.multiple_of(i * QB, QB), QB)

    def turn(i, carry):
        qt[i] = qs[queries(i), :].astype(F32).T.astype(BF16)
        gt[i] = gs[queries(i), :].astype(F32).T.astype(BF16)
        return carry

    lax.fori_loop(0, nq, turn, 0)
    for j in range(0, POSITIONS, W * 5):
        kt[:, j : j + W * 5] = ks[j : j + W * 5, :].astype(F32).T.astype(BF16)
    dk[...] = jnp.zeros_like(dk)
    dv[...] = jnp.zeros_like(dv)

    def products(j, turned_q, turned_g, refs):
        s_ref, d_ref = refs
        s_ref[rows_of(j), :] = jnp.dot(
            ks[rows_of(j), :], turned_q[...], preferred_element_type=F32
        )
        d_ref[rows_of(j), :] = jnp.dot(
            vs[rows_of(j), :], turned_g[...], preferred_element_type=F32
        )

    def highest(j, top, refs):
        for at in strips(j):
            top = fold(jnp.maximum, top, refs[0][at, :])
        return top

    low = jnp.full((8, QB), -jnp.inf, F32)
    zero = jnp.zeros((8, QB), F32)

    def block(i, qb, gb, top, refs, following):
        s_ref, d_ref = refs
        top = jnp.max(top, 0, keepdims=True) * SCALE2
        total, delta = zero, zero
        for j in range(CHUNKS):
            if following is not None:
                products(j, *following)
            for at in strips(j):
                p = jnp.exp2(s_ref[at, :] * SCALE2 - top)
                s_ref[at, :] = p
                total = fold(jnp.add, total, p)
                delta = fold(jnp.add, delta, p * d_ref[at, :])
        inverse = 1.0 / jnp.sum(total, 0, keepdims=True)
        delta = jnp.sum(delta, 0, keepdims=True) * inverse * SCALE
        after = low
        for j in range(CHUNKS):
            for at in strips(j):
                p = s_ref[at, :] * inverse
                p_ref[at, :] = p.astype(BF16)
                ds_ref[at, :] = (p * (d_ref[at, :] * SCALE - delta)).astype(BF16)
            if following is not None:
                after = highest(j, after, following[2])
            at = rows_of(j)
            dv[at, :] += jnp.dot(p_ref[at, :], gb[...], preferred_element_type=F32)
            dk[at, :] += jnp.dot(ds_ref[at, :], qb[...], preferred_element_type=F32)
        dq[queries(i), :] = jnp.dot(kt[...], ds_ref[...], preferred_element_type=F32).T
        return after

    one, two = (s_a, d_a), (s_b, d_b)

    def start(j, top):
        at = pl.ds(pl.multiple_of(j * KB, KB), KB)
        s = jnp.dot(ks[at, :], qt[0], preferred_element_type=F32)
        s_a[at, :] = s
        d_a[at, :] = jnp.dot(vs[at, :], gt[0], preferred_element_type=F32)
        return jnp.maximum(top, jnp.max(s.reshape(KB // 8, 8, QB), 0))

    top = lax.fori_loop(0, CHUNKS, start, low)

    def pair(n, top, last):
        for u in range(2):
            rows[2 * u] = qs[queries(2 * n + u), :]
            rows[2 * u + 1] = gs[queries(2 * n + u), :]
        for u in range(1 if last else 2):
            qt_now[2 * u] = qt[2 * n + 1 + u]
            qt_now[2 * u + 1] = gt[2 * n + 1 + u]
        top = block(
            2 * n, rows.at[0], rows.at[1], top, one, (qt_now.at[0], qt_now.at[1], two)
        )
        following = None if last else (qt_now.at[2], qt_now.at[3], one)
        return block(2 * n + 1, rows.at[2], rows.at[3], top, two, following)

    for n in range(nq // 2):
        top = pair(n, top, n == nq // 2 - 1)


def own_body(hc, place, x, ct, st, cp, sp, out, *scratch):
    frame = pl.ds(place[0], 1)
    attend_body(*[lambda two, a=a: x[two, a] for a in range(4)], SPACES, scratch)
    dk, dv, dq = scratch[-3:]

    def finish(n, carry):
        for b in [n * 2 + u for u in range(2)]:
            at = pl.ds(pl.multiple_of(b * ROWS, ROWS), ROWS)
            cosine = merged(ct[frame, :], cp[at, :])
            sine = merged(st[frame, :], sp[at, :])
            gq = unrotate(dq[at, :], cosine, sine)
            gk = unrotate(dk[at, :], cosine, sine)
            out[b] = jnp.concatenate([gq, gk, dv[at, :]], 0).astype(BF16)
        return carry

    lax.fori_loop(0, SPACES // 2, finish, 0)


def merge_body(hc, place, own, kept, given, ct, st, cp, sp, out):
    frame = pl.ds(place[0], 1)
    even = place[1] % 2 == 0
    ones, zeros = jnp.ones((ROWS, W), F32), jnp.zeros((ROWS, W), F32)
    extra = 2 * HALF - ROWS

    def rest_of(table, fill):
        tail = jnp.where(even, table[:HALF], jnp.concatenate([table[HALF:], fill[:extra]]))
        return jnp.concatenate([jnp.where(even, table, fill), tail])

    def finish(n, carry):
        for b in [n * 2 + u for u in range(2)]:
            at = pl.ds(pl.multiple_of(b * ROWS, ROWS), ROWS)
            cosine = rest_of(merged(ct[frame, :], cp[at, :]), ones)
            sine = rest_of(merged(st[frame, :], sp[at, :]), zeros)
            rest = unrotate(kept[b] + given[b], cosine, sine)
            out[b] = jnp.concatenate([own[b].astype(F32), rest], 0).astype(BF16)
        return carry

    lax.fori_loop(0, SPACES // 2, finish, 0)


def merge(meta, own, kept, given, tabs):
    shape = (SPACES, BACK, W)
    return pl.pallas_call(
        merge_body,
        grid_spec=pltpu.PrefetchScalarGridSpec(
            num_scalar_prefetch=2,
            grid=(1,),
            in_specs=[whole(x.shape) for x in (own, kept, given, *tabs)],
            out_specs=whole(shape),
        ),
        out_shape=jax.ShapeDtypeStruct(shape, BF16),
        compiler_params=pltpu.CompilerParams(vmem_limit_bytes=32 * MIB),
        cost_estimate=pl.CostEstimate(flops=5_000_000, bytes_accessed=9_000_000, transcendentals=0),
        name="merge",
    )(*meta, own, kept, given, *tabs)


def shared_body(hc, place, mine, other, keep, give, *scratch):
    core = place[1] % 2
    even = core == 0
    blocks = SPACES // 2

    def read(unit, holder):
        def pick(two):
            return jnp.where(core == holder, mine[two, unit], other[two, unit])

        return pick

    def half(pick):
        return lambda two: pick(pl.ds(two.start + core * blocks, two.size))

    attend_body(
        half(read(0, 0)), read(0, 1), read(1, 1), half(read(1, 0)), blocks, scratch
    )
    dk, dv, dq = scratch[-3:]
    empty = jnp.zeros((2 * HALF - ROWS, W), F32)

    def finish(b, carry):
        at = pl.ds(pl.multiple_of(b * ROWS, ROWS), ROWS)
        local = jnp.clip(b - core * blocks, 0, blocks - 1)
        have = (b // blocks) == core
        gq = dq[pl.ds(pl.multiple_of(local * ROWS, ROWS), ROWS), :]
        gq = jnp.where(have, gq, jnp.zeros_like(gq))
        gk = dk[at, :]
        one = jnp.concatenate([gq, gk[:HALF]], 0)
        two = jnp.concatenate([dv[at, :], gk[HALF:], empty], 0)
        keep[b] = jnp.where(even, one, two)
        give[b] = jnp.where(even, two, one)
        return carry

    lax.fori_loop(0, SPACES, finish, 0)


def attend_scratch(padded):
    nq = padded // QB
    return (
        [pltpu.VMEM((padded, W), BF16), pltpu.VMEM((POSITIONS, W), BF16)]
        + [pltpu.VMEM((POSITIONS, W), BF16), pltpu.VMEM((padded, W), BF16)]
        + [pltpu.VMEM((W, POSITIONS), BF16)]
        + [pltpu.VMEM((nq, W, QB), BF16)] * 2
        + [pltpu.VMEM((POSITIONS, QB), F32)] * 4
        + [pltpu.VMEM((POSITIONS, QB), BF16)] * 2
        + [pltpu.VMEM((4, QB, W), BF16), pltpu.VMEM((4, W, QB), BF16)]
        + [pltpu.VMEM((POSITIONS, W), F32)] * 2
        + [pltpu.VMEM((padded, W), F32)]
    )


ATTEND_COST = pl.CostEstimate(
    flops=10 * POSITIONS * POSITIONS * W,
    bytes_accessed=6_000_000,
    transcendentals=POSITIONS * POSITIONS,
)


def attend_own(meta, received, tabs):
    shape = (SPACES, 3 * ROWS, W)
    return pl.pallas_call(
        own_body,
        grid_spec=pltpu.PrefetchScalarGridSpec(
            num_scalar_prefetch=2,
            grid=(1,),
            in_specs=[whole((SPACES, 4, ROWS, W))] + [whole(t.shape) for t in tabs],
            out_specs=whole(shape),
            scratch_shapes=attend_scratch(PADDED),
        ),
        out_shape=jax.ShapeDtypeStruct(shape, BF16),
        compiler_params=pltpu.CompilerParams(vmem_limit_bytes=46 * MIB),
        cost_estimate=ATTEND_COST,
        name="attend_own",
    )(*meta, received, *tabs)


def attend_shared(meta, mine, other):
    shape = (SPACES, ROWS + HALF, W)
    return pl.pallas_call(
        shared_body,
        grid_spec=pltpu.PrefetchScalarGridSpec(
            num_scalar_prefetch=2,
            grid=(1,),
            in_specs=[whole(mine.shape), whole(other.shape)],
            out_specs=[whole(shape), whole(shape)],
            scratch_shapes=attend_scratch(PADDED // 2),
        ),
        out_shape=[jax.ShapeDtypeStruct(shape, F32)] * 2,
        compiler_params=pltpu.CompilerParams(vmem_limit_bytes=46 * MIB),
        cost_estimate=ATTEND_COST,
        name="attend_shared",
    )(*meta, mine, other)


def frames_body(hc, place, *refs):
    xs, (ct, st, cp, sp) = refs[:FRAMES], refs[FRAMES : FRAMES + 4]
    outs, (dq_ref, dk_ref, dv_ref) = refs[FRAMES + 4 : -3], refs[-3:]
    tokens = FRAMES * TP
    key_place = lax.broadcasted_iota(jnp.int32, (tokens, tokens), 0) % TP
    query_place = lax.broadcasted_iota(jnp.int32, (tokens, tokens), 1) % TP
    same = key_place == query_place
    nt = (((1,), (1,)), ((), ()))
    owners = [peer(place, step, False) for step in range(FRAMES)]

    def head(i, carry):
        for c in range(ROWS // TP):
            rows = slice(c * TP, (c + 1) * TP)
            q, k, v, g = (
                jnp.concatenate([x[i * 4 + a].astype(F32)[rows] for x in xs], 0).astype(BF16)
                for a in range(4)
            )
            s = lax.dot_general(k, q, nt, preferred_element_type=F32)
            s = jnp.where(same, s, -jnp.inf)
            p = jnp.exp2((s - jnp.max(s, 0, keepdims=True)) * SCALE2)
            p = p * (1.0 / jnp.sum(p, 0, keepdims=True))
            d = lax.dot_general(v, g, nt, preferred_element_type=F32)
            delta = jnp.sum(p * d, 0, keepdims=True)
            ds = p * ((d - delta) * SCALE)
            dst = ds.T.astype(BF16)
            ds = ds.astype(BF16)
            gv = jnp.dot(p.astype(BF16), g, preferred_element_type=F32)
            gk = jnp.dot(ds, q, preferred_element_type=F32)
            gq = jnp.dot(dst, k, preferred_element_type=F32)
            place_c, place_s = cp[rows, :], sp[rows, :]
            cosine = jnp.concatenate([merged(ct[pl.ds(f, 1), :], place_c) for f in owners], 0)
            sine = jnp.concatenate([merged(st[pl.ds(f, 1), :], place_s) for f in owners], 0)
            dq_ref[:, rows, :] = unrotate(gq, cosine, sine).reshape(FRAMES, TP, W)
            dk_ref[:, rows, :] = unrotate(gk, cosine, sine).reshape(FRAMES, TP, W)
            dv_ref[:, rows, :] = gv.reshape(FRAMES, TP, W)
        for step, out in enumerate(outs):
            out[i * 3] = dq_ref[step].astype(BF16)
            out[i * 3 + 1] = dk_ref[step].astype(BF16)
            out[i * 3 + 2] = dv_ref[step].astype(BF16)
        return carry

    lax.fori_loop(0, 3, head, 0)


def attend_frames(meta, received, tabs):
    shape = (9, ROWS, W)
    return pl.pallas_call(
        frames_body,
        grid_spec=pltpu.PrefetchScalarGridSpec(
            num_scalar_prefetch=2,
            grid=(1,),
            in_specs=[whole(x.shape) for x in received] + [SMALL, SMALL, LOCAL, LOCAL],
            out_specs=[whole(shape)] * FRAMES,
            scratch_shapes=[pltpu.VMEM((FRAMES, ROWS, W), F32)] * 3,
        ),
        out_shape=[jax.ShapeDtypeStruct(shape, BF16)] * FRAMES,
        compiler_params=pltpu.CompilerParams(vmem_limit_bytes=20 * MIB),
        cost_estimate=pl.CostEstimate(
            flops=2_000_000_000, bytes_accessed=6_000_000, transcendentals=600_000
        ),
        name="attend_frames",
    )(*meta, *received, *tabs)


def column(flat_id):
    layer = flat_id // HEADS
    return layer, 0, slice(None), lanes_of(flat_id - layer * HEADS)


def unpack_temporal_body(hc, place, *refs):
    xs, outs, (ids,) = refs[:FRAMES], refs[FRAMES : FRAMES + 3], refs[FRAMES + 3 :]
    pick_heads(hc, range(LAYERS), False, ids)
    for step in range(FRAMES):
        dest = peer(place, step, True)
        for i in range(3):
            at = column(ids[dest * 3 + i])
            for a, out in enumerate(outs):
                out[at] = xs[step][i * 3 + a]


def unpack_temporal(meta, returned):
    return pl.pallas_call(
        unpack_temporal_body,
        grid_spec=pltpu.PrefetchScalarGridSpec(
            num_scalar_prefetch=2,
            grid=(1,),
            in_specs=[whole(x.shape) for x in returned],
            out_specs=[whole(OUT)] * 3,
            scratch_shapes=[pltpu.SMEM((HEADS,), jnp.int32)],
        ),
        out_shape=[jax.ShapeDtypeStruct(OUT, BF16)] * 3,
        compiler_params=pltpu.CompilerParams(vmem_limit_bytes=20 * MIB),
        cost_estimate=pl.CostEstimate(flops=5_000_000, bytes_accessed=7_000_000, transcendentals=0),
        name="unpack_temporal",
    )(*meta, *returned)


def unpack_spatial_body(hc, place, x, iq, ik, iv, oq, ok, ov, ids, pieces, sems):
    outs = (oq, ok, ov)
    pick_heads(hc, range(LAYERS), True, ids)
    copies = []

    def put(slot, parts):
        for a, part in enumerate(parts):
            pieces[slot, a] = part.astype(BF16)
            copies.append(
                pltpu.make_async_copy(
                    pieces.at[slot, a], outs[a].at[column(ids[slot])], sems.at[slot, a]
                )
            )
            copies[-1].start()

    for n in range(SPACES // 2):
        one = x[2 * n].astype(F32)
        two = x[2 * n + 1].astype(F32)
        for slot, piece in ((2 * n, one), (2 * n + 1, two)):
            put(slot, [piece[a * ROWS : (a + 1) * ROWS] for a in range(3)])
        both = jnp.concatenate([one[4 * ROWS :], two[4 * ROWS : 5 * ROWS - HALF]], 0)
        put(SPACES + n, [one[3 * ROWS : 4 * ROWS], both, two[3 * ROWS : 4 * ROWS]])
    for copy in copies:
        copy.wait()


def unpack_spatial(meta, returned, partial):
    anywhere = pl.BlockSpec(memory_space=pl.ANY)
    return pl.pallas_call(
        unpack_spatial_body,
        grid_spec=pltpu.PrefetchScalarGridSpec(
            num_scalar_prefetch=2,
            grid=(1,),
            in_specs=[whole(returned.shape)] + [anywhere] * 3,
            out_specs=[anywhere] * 3,
            scratch_shapes=[
                pltpu.SMEM((HEADS,), jnp.int32),
                pltpu.VMEM((HEADS, 3, ROWS, W), BF16),
                pltpu.SemaphoreType.DMA((HEADS, 3)),
            ],
        ),
        out_shape=[jax.ShapeDtypeStruct(OUT, BF16)] * 3,
        input_output_aliases={3 + a: a for a in range(3)},
        compiler_params=pltpu.CompilerParams(vmem_limit_bytes=16 * MIB),
        cost_estimate=pl.CostEstimate(flops=0, bytes_accessed=5_000_000, transcendentals=0),
        name="unpack_spatial",
    )(*meta, returned, *partial)


def exchange(x):
    return lax.all_to_all(x, "space", split_axis=0, concat_axis=0, tiled=True)


SWAP = [(i, i ^ 1) for i in range(SPACES)]


def along_x(parts, sign):
    def move(step, part):
        dx = sign * (step // 2)
        if dx == 0 or part is None:
            return part
        pairs = [(f, f // 4 * 4 + (f + dx) % 4) for f in range(FRAMES)]
        return lax.ppermute(part, "frame", pairs)

    return [move(step, part) for step, part in enumerate(parts)]


def along_z(parts):
    pairs = [(f, f ^ 4) for f in range(FRAMES)]
    return [lax.ppermute(x, "frame", pairs) if n % 2 else x for n, x in enumerate(parts)]


def tie(*values):
    return lax.optimization_barrier(values)


def on_device(queries, keys, values, grad_out, head_class):
    place = jnp.stack([lax.axis_index("frame"), lax.axis_index("space")]).astype(jnp.int32)
    meta = (head_class, place)
    tabs = tuple(jnp.asarray(t) for t in tables())
    arrays = (queries, keys, values, grad_out)
    got_s = exchange(pack_spatial(meta, arrays, tabs))
    half_t = along_x(pack_temporal(meta, arrays, tabs), 1)
    got_s, *half_t = tie(got_s, *half_t)
    got_t = along_z(half_t)
    mine = got_s[:, 4:6]
    other = lax.ppermute(mine, "space", SWAP)
    own = attend_own(meta, got_s, tabs)
    own, mine, got_t[1], got_t[3], got_t[5] = tie(own, mine, got_t[1], got_t[3], got_t[5])
    kept, give = attend_shared(meta, mine, other)
    kept, give, *got_t = tie(kept, give, *got_t)
    given = lax.ppermute(give, "space", SWAP)
    grads_t = list(attend_frames(meta, got_t, tabs))
    kept, grads_t[0] = tie(kept, grads_t[0])
    flipped = along_z(grads_t)[1::2]
    level = along_x([x if n % 2 == 0 else None for n, x in enumerate(grads_t)], -1)[::2]
    back_s, *others = tie(merge(meta, own, kept, given, tabs), *flipped, *level)
    flipped, level = others[:4], others[4:]
    home_s = exchange(back_s)
    flipped = along_x([x for part in flipped for x in (None, part)], -1)[1::2]
    home_t = [x for two in zip(level, flipped) for x in two]
    partial = unpack_temporal(meta, home_t)
    return tuple(unpack_spatial(meta, home_s, partial))


def solution(mesh):
    placed = P(None, "frame", "space", None)
    return jax.shard_map(
        on_device,
        mesh=mesh,
        in_specs=(placed, placed, placed, placed, P()),
        out_specs=(placed, placed, placed),
        check_vma=False,
    )
```

```python
import math

import jax
import jax.numpy as jnp
import numpy as np
from jax import lax
from jax.experimental import pallas as pl
from jax.experimental.pallas import tpu as pltpu
from jax.sharding import PartitionSpec as P

RT = 16
RS = 56
PW = 80
THETA = 256.0
W = RT + 2 * RS
HEADS = 24
LAYERS = 2
FRAMES = 8
SPACES = 16
ROWS = 120
POSITIONS = SPACES * ROWS
HALF = 64
BACK = 4 * ROWS + HALF
QB = 512
PADDED = 2048
KB = 240
STRIP = 16
TP = 24
GROUP = 4
MIB = 1024 * 1024
VMEM = 60 * MIB
SCALE = 1.0 / math.sqrt(W)
SCALE2 = SCALE * math.log2(math.e)
F32 = jnp.float32
BF16 = jnp.bfloat16


OUT = (LAYERS, 1, ROWS, HEADS * W)


def whole(shape):
    return pl.BlockSpec(shape, lambda i, h, p: (0,) * len(shape))


def tables():
    channel = np.arange(W)
    pair = channel // 2
    tpairs, spairs = RT // 2, RS // 2
    is_time = pair < tpairs
    is_row = (pair >= tpairs) & (pair < tpairs + spairs)
    local = np.where(is_time, pair, np.where(is_row, pair - tpairs, pair - tpairs - spairs))
    width = np.where(is_time, RT, RS)
    freq = THETA ** (-2.0 * local / width)
    sign = np.where(channel % 2 == 0, -1.0, 1.0)
    time = np.arange(FRAMES)[:, None] * freq
    position = np.arange(POSITIONS)[:, None]
    place = np.where(is_row, position // PW, position % PW) * freq
    return (
        np.cos(time).astype(np.float32),
        (np.sin(time) * sign).astype(np.float32),
        np.cos(place).astype(np.float32),
        (np.sin(place) * sign).astype(np.float32),
    )


def lane_ids(shape):
    return lax.broadcasted_iota(jnp.int32, shape, len(shape) - 1)


def swapped(x):
    up = pltpu.roll(x, W - 1, 1)
    low = pltpu.roll(x, 1, 1)
    return jnp.where(lane_ids(x.shape) % 2 == 0, up, low)


def merged(time_row, place_rows):
    return jnp.where(lane_ids(place_rows.shape) < RT, time_row, place_rows)


def rotate(x, cosine, sine):
    return x * cosine + swapped(x) * sine


def unrotate(x, cosine, sine):
    x = x.astype(BF16).astype(F32)
    return x * cosine - swapped(x) * sine


def pick_heads(hc, layers, spatial, ids):
    def look(h, n, layer):
        mine = (hc[layer, h] == 0) == spatial

        @pl.when(mine)
        def _():
            ids[n] = layer * HEADS + h

        return n + mine.astype(jnp.int32)

    found = jnp.int32(0)
    for layer in layers:
        found = lax.fori_loop(0, HEADS, lambda h, n: look(h, n, layer), found)
    return found


def lanes_of(h):
    return pl.ds(pl.multiple_of(h * W, W), W)


def pack_body(hc, place, q, k, v, g, ct, st, cp, sp, out, count, ids, cos_ref, sin_ref):
    layer = pl.program_id(0)

    @pl.when(layer == 0)
    def _():
        count[0] = 0
        frame = place[0]
        cos_ref[...] = merged(ct[pl.ds(frame, 1), :], cp[...])
        sin_ref[...] = merged(st[pl.ds(frame, 1), :], sp[...])

    first = count[0]
    found = pick_heads(hc, [layer], True, ids)
    count[0] = first + found

    def group(n, put):
        cosine, sine = cos_ref[...], sin_ref[...]
        for i in range(GROUP):
            lanes = lanes_of(ids[n * GROUP + i] - layer * HEADS)
            rq = rotate(q[0, 0, :, lanes].astype(F32), cosine, sine).astype(BF16)
            rk = rotate(k[0, 0, :, lanes].astype(F32), cosine, sine).astype(BF16)
            put(first + n * GROUP + i, rq, rk, v[0, 0, :, lanes], g[0, 0, :, lanes])

    def put_own(slot, *parts):
        for a in range(4):
            out[slot, a] = parts[a]

    def put_shared(slot, rq, rk, vv, gg):
        dest = (slot - SPACES) * 2
        out[dest, 4] = rq
        out[dest, 5] = gg
        out[dest + 1, 4] = rk
        out[dest + 1, 5] = vv

    def step(n, carry):
        own = first + n * GROUP < SPACES
        pl.when(own)(lambda: group(n, put_own))
        pl.when(jnp.logical_not(own))(lambda: group(n, put_shared))
        return carry

    lax.fori_loop(0, found // GROUP, step, 0)


SMALL = pl.BlockSpec((FRAMES, W), lambda i, h, p: (0, 0))
LOCAL = pl.BlockSpec((ROWS, W), lambda i, h, p: (p[1], 0))
PACK_COST = pl.CostEstimate(flops=20_000_000, bytes_accessed=9_000_000, transcendentals=0)


def pack_spatial(meta, arrays, tabs):
    shape = (SPACES, 6, ROWS, W)
    part = pl.BlockSpec((1, 1, ROWS, HEADS * W), lambda l, h, p: (l, 0, 0, 0))
    return pl.pallas_call(
        pack_body,
        grid_spec=pltpu.PrefetchScalarGridSpec(
            num_scalar_prefetch=2,
            grid=(LAYERS,),
            in_specs=[part] * 4 + [SMALL, SMALL, LOCAL, LOCAL],
            out_specs=pl.BlockSpec(shape, lambda l, h, p: (0, 0, 0, 0)),
            scratch_shapes=[
                pltpu.SMEM((1,), jnp.int32),
                pltpu.SMEM((HEADS,), jnp.int32),
                pltpu.VMEM((ROWS, W), F32),
                pltpu.VMEM((ROWS, W), F32),
            ],
        ),
        out_shape=jax.ShapeDtypeStruct(shape, BF16),
        compiler_params=pltpu.CompilerParams(vmem_limit_bytes=VMEM),
        cost_estimate=PACK_COST,
        name="pack_spatial",
    )(*meta, *arrays, *tabs)


def peer(place, step, forward):
    frame = place[0]
    x, z = frame % 4, frame // 4
    dx, dz = step // 2, step % 2
    x = (x + (dx if forward else 4 - dx)) % 4
    return (1 - z if dz else z) * 4 + x


def pack_temporal_body(hc, place, q, k, v, g, ct, st, cp, sp, *rest):
    outs, (ids, cos_ref, sin_ref) = rest[:FRAMES], rest[FRAMES:]
    frame = place[0]
    cos_ref[...] = merged(ct[pl.ds(frame, 1), :], cp[...])
    sin_ref[...] = merged(st[pl.ds(frame, 1), :], sp[...])
    pick_heads(hc, range(LAYERS), False, ids)
    for step in range(FRAMES):
        cosine, sine = cos_ref[...], sin_ref[...]
        dest = peer(place, step, True)
        for i in range(3):
            flat_id = ids[dest * 3 + i]
            layer = flat_id // HEADS
            lanes = lanes_of(flat_id - layer * HEADS)
            out = outs[step]
            out[i * 4] = rotate(q[layer, 0, :, lanes].astype(F32), cosine, sine).astype(BF16)
            out[i * 4 + 1] = rotate(k[layer, 0, :, lanes].astype(F32), cosine, sine).astype(BF16)
            out[i * 4 + 2] = v[layer, 0, :, lanes]
            out[i * 4 + 3] = g[layer, 0, :, lanes]


def pack_temporal(meta, arrays, tabs):
    shape = (12, ROWS, W)
    return pl.pallas_call(
        pack_temporal_body,
        grid_spec=pltpu.PrefetchScalarGridSpec(
            num_scalar_prefetch=2,
            grid=(1,),
            in_specs=[whole(OUT)] * 4 + [SMALL, SMALL, LOCAL, LOCAL],
            out_specs=[whole(shape)] * FRAMES,
            scratch_shapes=[
                pltpu.SMEM((HEADS,), jnp.int32),
                pltpu.VMEM((ROWS, W), F32),
                pltpu.VMEM((ROWS, W), F32),
            ],
        ),
        out_shape=[jax.ShapeDtypeStruct(shape, BF16)] * FRAMES,
        compiler_params=pltpu.CompilerParams(vmem_limit_bytes=VMEM),
        cost_estimate=PACK_COST,
        name="pack_temporal",
    )(*meta, *arrays, *tabs)


CHUNKS = POSITIONS // KB
PAIR = KB // ROWS


def rows_of(j):
    return slice(j * KB, (j + 1) * KB)


def fold(op, total, strip):
    for r in range(0, STRIP, 8):
        total = op(total, strip[r : r + 8])
    return total


def strips(j):
    return [slice(r, r + STRIP) for r in range(j * KB, (j + 1) * KB, STRIP)]


def load_rows(ref, read, blocks):
    def load(j, carry):
        at = pl.ds(pl.multiple_of(j * KB, KB), KB)
        ref[at, :] = read(pl.ds(j * PAIR, PAIR)).astype(F32).reshape(KB, W).astype(BF16)
        return carry

    lax.fori_loop(0, blocks // PAIR, load, 0)
    used = blocks * ROWS
    if used < ref.shape[0]:
        ref[used:, :] = jnp.zeros((ref.shape[0] - used, W), BF16)


def attend_body(q, k, v, g, query_blocks, scratch):
    qs, ks, vs, gs, kt, qt, gt, s_a, s_b, d_a, d_b, p_ref, ds_ref, rows, qt_now, dk, dv, dq = scratch
    nq = -(-query_blocks * ROWS // QB)
    load_rows(qs, q, query_blocks)
    load_rows(gs, g, query_blocks)
    load_rows(ks, k, SPACES)
    load_rows(vs, v, SPACES)

    def queries(i):
        return pl.ds(pl.multiple_of(i * QB, QB), QB)

    def turn(i, carry):
        qt[i] = qs[queries(i), :].astype(F32).T.astype(BF16)
        gt[i] = gs[queries(i), :].astype(F32).T.astype(BF16)
        return carry

    lax.fori_loop(0, nq, turn, 0)
    for j in range(0, POSITIONS, W * 5):
        kt[:, j : j + W * 5] = ks[j : j + W * 5, :].astype(F32).T.astype(BF16)
    dk[...] = jnp.zeros_like(dk)
    dv[...] = jnp.zeros_like(dv)

    def products(j, turned_q, turned_g, refs):
        s_ref, d_ref = refs
        s_ref[rows_of(j), :] = jnp.dot(
            ks[rows_of(j), :], turned_q[...], preferred_element_type=F32
        )
        d_ref[rows_of(j), :] = jnp.dot(
            vs[rows_of(j), :], turned_g[...], preferred_element_type=F32
        )

    def highest(j, top, refs):
        for at in strips(j):
            top = fold(jnp.maximum, top, refs[0][at, :])
        return top

    low = jnp.full((8, QB), -jnp.inf, F32)
    zero = jnp.zeros((8, QB), F32)

    def block(i, qb, gb, top, refs, following):
        s_ref, d_ref = refs
        top = jnp.max(top, 0, keepdims=True) * SCALE2
        total, delta = zero, zero
        for j in range(CHUNKS):
            if following is not None:
                products(j, *following)
            for at in strips(j):
                p = jnp.exp2(s_ref[at, :] * SCALE2 - top)
                s_ref[at, :] = p
                total = fold(jnp.add, total, p)
                delta = fold(jnp.add, delta, p * d_ref[at, :])
        inverse = 1.0 / jnp.sum(total, 0, keepdims=True)
        delta = jnp.sum(delta, 0, keepdims=True) * inverse * SCALE
        after = low
        for j in range(CHUNKS):
            for at in strips(j):
                p = s_ref[at, :] * inverse
                p_ref[at, :] = p.astype(BF16)
                ds_ref[at, :] = (p * (d_ref[at, :] * SCALE - delta)).astype(BF16)
            if following is not None:
                after = highest(j, after, following[2])
            at = rows_of(j)
            dv[at, :] += jnp.dot(p_ref[at, :], gb[...], preferred_element_type=F32)
            dk[at, :] += jnp.dot(ds_ref[at, :], qb[...], preferred_element_type=F32)
        dq[queries(i), :] = jnp.dot(kt[...], ds_ref[...], preferred_element_type=F32).T
        return after

    one, two = (s_a, d_a), (s_b, d_b)

    def start(j, top):
        at = pl.ds(pl.multiple_of(j * KB, KB), KB)
        s = jnp.dot(ks[at, :], qt[0], preferred_element_type=F32)
        s_a[at, :] = s
        d_a[at, :] = jnp.dot(vs[at, :], gt[0], preferred_element_type=F32)
        return jnp.maximum(top, jnp.max(s.reshape(KB // 8, 8, QB), 0))

    top = lax.fori_loop(0, CHUNKS, start, low)

    def pair(n, top, last):
        for u in range(2):
            rows[2 * u] = qs[queries(2 * n + u), :]
            rows[2 * u + 1] = gs[queries(2 * n + u), :]
        for u in range(1 if last else 2):
            qt_now[2 * u] = qt[2 * n + 1 + u]
            qt_now[2 * u + 1] = gt[2 * n + 1 + u]
        top = block(
            2 * n, rows.at[0], rows.at[1], top, one, (qt_now.at[0], qt_now.at[1], two)
        )
        following = None if last else (qt_now.at[2], qt_now.at[3], one)
        return block(2 * n + 1, rows.at[2], rows.at[3], top, two, following)

    for n in range(nq // 2):
        top = pair(n, top, n == nq // 2 - 1)


def own_body(hc, place, x, ct, st, cp, sp, out, *scratch):
    frame = pl.ds(place[0], 1)
    attend_body(*[lambda two, a=a: x[two, a] for a in range(4)], SPACES, scratch)
    dk, dv, dq = scratch[-3:]

    def finish(n, carry):
        for b in [n * 2 + u for u in range(2)]:
            at = pl.ds(pl.multiple_of(b * ROWS, ROWS), ROWS)
            cosine = merged(ct[frame, :], cp[at, :])
            sine = merged(st[frame, :], sp[at, :])
            gq = unrotate(dq[at, :], cosine, sine)
            gk = unrotate(dk[at, :], cosine, sine)
            out[b] = jnp.concatenate([gq, gk, dv[at, :]], 0).astype(BF16)
        return carry

    lax.fori_loop(0, SPACES // 2, finish, 0)


def merge_body(hc, place, own, kept, given, ct, st, cp, sp, out):
    frame = pl.ds(place[0], 1)
    even = place[1] % 2 == 0
    ones, zeros = jnp.ones((ROWS, W), F32), jnp.zeros((ROWS, W), F32)
    extra = 2 * HALF - ROWS

    def rest_of(table, fill):
        tail = jnp.where(even, table[:HALF], jnp.concatenate([table[HALF:], fill[:extra]]))
        return jnp.concatenate([jnp.where(even, table, fill), tail])

    def finish(n, carry):
        for b in [n * 2 + u for u in range(2)]:
            at = pl.ds(pl.multiple_of(b * ROWS, ROWS), ROWS)
            cosine = rest_of(merged(ct[frame, :], cp[at, :]), ones)
            sine = rest_of(merged(st[frame, :], sp[at, :]), zeros)
            rest = unrotate(kept[b] + given[b], cosine, sine)
            out[b] = jnp.concatenate([own[b].astype(F32), rest], 0).astype(BF16)
        return carry

    lax.fori_loop(0, SPACES // 2, finish, 0)


def merge(meta, own, kept, given, tabs):
    shape = (SPACES, BACK, W)
    return pl.pallas_call(
        merge_body,
        grid_spec=pltpu.PrefetchScalarGridSpec(
            num_scalar_prefetch=2,
            grid=(1,),
            in_specs=[whole(x.shape) for x in (own, kept, given, *tabs)],
            out_specs=whole(shape),
        ),
        out_shape=jax.ShapeDtypeStruct(shape, BF16),
        compiler_params=pltpu.CompilerParams(vmem_limit_bytes=32 * MIB),
        cost_estimate=pl.CostEstimate(flops=5_000_000, bytes_accessed=9_000_000, transcendentals=0),
        name="merge",
    )(*meta, own, kept, given, *tabs)


def shared_body(hc, place, mine, other, keep, give, *scratch):
    core = place[1] % 2
    even = core == 0
    blocks = SPACES // 2

    def read(unit, holder):
        def pick(two):
            return jnp.where(core == holder, mine[two, unit], other[two, unit])

        return pick

    def half(pick):
        return lambda two: pick(pl.ds(two.start + core * blocks, two.size))

    attend_body(
        half(read(0, 0)), read(0, 1), read(1, 1), half(read(1, 0)), blocks, scratch
    )
    dk, dv, dq = scratch[-3:]
    empty = jnp.zeros((2 * HALF - ROWS, W), F32)

    def finish(b, carry):
        at = pl.ds(pl.multiple_of(b * ROWS, ROWS), ROWS)
        local = jnp.clip(b - core * blocks, 0, blocks - 1)
        have = (b // blocks) == core
        gq = dq[pl.ds(pl.multiple_of(local * ROWS, ROWS), ROWS), :]
        gq = jnp.where(have, gq, jnp.zeros_like(gq))
        gk = dk[at, :]
        one = jnp.concatenate([gq, gk[:HALF]], 0)
        two = jnp.concatenate([dv[at, :], gk[HALF:], empty], 0)
        keep[b] = jnp.where(even, one, two)
        give[b] = jnp.where(even, two, one)
        return carry

    lax.fori_loop(0, SPACES, finish, 0)


def attend_scratch(padded):
    nq = padded // QB
    return (
        [pltpu.VMEM((padded, W), BF16), pltpu.VMEM((POSITIONS, W), BF16)]
        + [pltpu.VMEM((POSITIONS, W), BF16), pltpu.VMEM((padded, W), BF16)]
        + [pltpu.VMEM((W, POSITIONS), BF16)]
        + [pltpu.VMEM((nq, W, QB), BF16)] * 2
        + [pltpu.VMEM((POSITIONS, QB), F32)] * 4
        + [pltpu.VMEM((POSITIONS, QB), BF16)] * 2
        + [pltpu.VMEM((4, QB, W), BF16), pltpu.VMEM((4, W, QB), BF16)]
        + [pltpu.VMEM((POSITIONS, W), F32)] * 2
        + [pltpu.VMEM((padded, W), F32)]
    )


ATTEND_COST = pl.CostEstimate(
    flops=10 * POSITIONS * POSITIONS * W,
    bytes_accessed=6_000_000,
    transcendentals=POSITIONS * POSITIONS,
)


def attend_own(meta, received, tabs):
    shape = (SPACES, 3 * ROWS, W)
    return pl.pallas_call(
        own_body,
        grid_spec=pltpu.PrefetchScalarGridSpec(
            num_scalar_prefetch=2,
            grid=(1,),
            in_specs=[whole((SPACES, 4, ROWS, W))] + [whole(t.shape) for t in tabs],
            out_specs=whole(shape),
            scratch_shapes=attend_scratch(PADDED),
        ),
        out_shape=jax.ShapeDtypeStruct(shape, BF16),
        compiler_params=pltpu.CompilerParams(vmem_limit_bytes=46 * MIB),
        cost_estimate=ATTEND_COST,
        name="attend_own",
    )(*meta, received, *tabs)


def attend_shared(meta, mine, other):
    shape = (SPACES, ROWS + HALF, W)
    return pl.pallas_call(
        shared_body,
        grid_spec=pltpu.PrefetchScalarGridSpec(
            num_scalar_prefetch=2,
            grid=(1,),
            in_specs=[whole(mine.shape), whole(other.shape)],
            out_specs=[whole(shape), whole(shape)],
            scratch_shapes=attend_scratch(PADDED // 2),
        ),
        out_shape=[jax.ShapeDtypeStruct(shape, F32)] * 2,
        compiler_params=pltpu.CompilerParams(vmem_limit_bytes=46 * MIB),
        cost_estimate=ATTEND_COST,
        name="attend_shared",
    )(*meta, mine, other)


def frames_body(hc, place, *refs):
    xs, (ct, st, cp, sp) = refs[:FRAMES], refs[FRAMES : FRAMES + 4]
    outs, (dq_ref, dk_ref, dv_ref) = refs[FRAMES + 4 : -3], refs[-3:]
    tokens = FRAMES * TP
    key_place = lax.broadcasted_iota(jnp.int32, (tokens, tokens), 0) % TP
    query_place = lax.broadcasted_iota(jnp.int32, (tokens, tokens), 1) % TP
    same = key_place == query_place
    nt = (((1,), (1,)), ((), ()))
    owners = [peer(place, step, False) for step in range(FRAMES)]

    def head(i, carry):
        for c in range(ROWS // TP):
            rows = slice(c * TP, (c + 1) * TP)
            q, k, v, g = (
                jnp.concatenate([x[i * 4 + a].astype(F32)[rows] for x in xs], 0).astype(BF16)
                for a in range(4)
            )
            s = lax.dot_general(k, q, nt, preferred_element_type=F32)
            s = jnp.where(same, s, -jnp.inf)
            p = jnp.exp2((s - jnp.max(s, 0, keepdims=True)) * SCALE2)
            p = p * (1.0 / jnp.sum(p, 0, keepdims=True))
            d = lax.dot_general(v, g, nt, preferred_element_type=F32)
            delta = jnp.sum(p * d, 0, keepdims=True)
            ds = p * ((d - delta) * SCALE)
            dst = ds.T.astype(BF16)
            ds = ds.astype(BF16)
            gv = jnp.dot(p.astype(BF16), g, preferred_element_type=F32)
            gk = jnp.dot(ds, q, preferred_element_type=F32)
            gq = jnp.dot(dst, k, preferred_element_type=F32)
            place_c, place_s = cp[rows, :], sp[rows, :]
            cosine = jnp.concatenate([merged(ct[pl.ds(f, 1), :], place_c) for f in owners], 0)
            sine = jnp.concatenate([merged(st[pl.ds(f, 1), :], place_s) for f in owners], 0)
            dq_ref[:, rows, :] = unrotate(gq, cosine, sine).reshape(FRAMES, TP, W)
            dk_ref[:, rows, :] = unrotate(gk, cosine, sine).reshape(FRAMES, TP, W)
            dv_ref[:, rows, :] = gv.reshape(FRAMES, TP, W)
        for step, out in enumerate(outs):
            out[i * 3] = dq_ref[step].astype(BF16)
            out[i * 3 + 1] = dk_ref[step].astype(BF16)
            out[i * 3 + 2] = dv_ref[step].astype(BF16)
        return carry

    lax.fori_loop(0, 3, head, 0)


def attend_frames(meta, received, tabs):
    shape = (9, ROWS, W)
    return pl.pallas_call(
        frames_body,
        grid_spec=pltpu.PrefetchScalarGridSpec(
            num_scalar_prefetch=2,
            grid=(1,),
            in_specs=[whole(x.shape) for x in received] + [SMALL, SMALL, LOCAL, LOCAL],
            out_specs=[whole(shape)] * FRAMES,
            scratch_shapes=[pltpu.VMEM((FRAMES, ROWS, W), F32)] * 3,
        ),
        out_shape=[jax.ShapeDtypeStruct(shape, BF16)] * FRAMES,
        compiler_params=pltpu.CompilerParams(vmem_limit_bytes=20 * MIB),
        cost_estimate=pl.CostEstimate(
            flops=2_000_000_000, bytes_accessed=6_000_000, transcendentals=600_000
        ),
        name="attend_frames",
    )(*meta, *received, *tabs)


def column(flat_id):
    layer = flat_id // HEADS
    return layer, 0, slice(None), lanes_of(flat_id - layer * HEADS)


def unpack_temporal_body(hc, place, *refs):
    xs, outs, (ids,) = refs[:FRAMES], refs[FRAMES : FRAMES + 3], refs[FRAMES + 3 :]
    pick_heads(hc, range(LAYERS), False, ids)
    for step in range(FRAMES):
        dest = peer(place, step, True)
        for i in range(3):
            at = column(ids[dest * 3 + i])
            for a, out in enumerate(outs):
                out[at] = xs[step][i * 3 + a]


def unpack_temporal(meta, returned):
    return pl.pallas_call(
        unpack_temporal_body,
        grid_spec=pltpu.PrefetchScalarGridSpec(
            num_scalar_prefetch=2,
            grid=(1,),
            in_specs=[whole(x.shape) for x in returned],
            out_specs=[whole(OUT)] * 3,
            scratch_shapes=[pltpu.SMEM((HEADS,), jnp.int32)],
        ),
        out_shape=[jax.ShapeDtypeStruct(OUT, BF16)] * 3,
        compiler_params=pltpu.CompilerParams(vmem_limit_bytes=20 * MIB),
        cost_estimate=pl.CostEstimate(flops=5_000_000, bytes_accessed=7_000_000, transcendentals=0),
        name="unpack_temporal",
    )(*meta, *returned)


def unpack_spatial_body(hc, place, x, iq, ik, iv, oq, ok, ov, ids, pieces, sems):
    outs = (oq, ok, ov)
    pick_heads(hc, range(LAYERS), True, ids)
    copies = []

    def put(slot, parts):
        for a, part in enumerate(parts):
            pieces[slot, a] = part.astype(BF16)
            copies.append(
                pltpu.make_async_copy(
                    pieces.at[slot, a], outs[a].at[column(ids[slot])], sems.at[slot, a]
                )
            )
            copies[-1].start()

    for n in range(SPACES // 2):
        one = x[2 * n].astype(F32)
        two = x[2 * n + 1].astype(F32)
        for slot, piece in ((2 * n, one), (2 * n + 1, two)):
            put(slot, [piece[a * ROWS : (a + 1) * ROWS] for a in range(3)])
        both = jnp.concatenate([one[4 * ROWS :], two[4 * ROWS : 5 * ROWS - HALF]], 0)
        put(SPACES + n, [one[3 * ROWS : 4 * ROWS], both, two[3 * ROWS : 4 * ROWS]])
    for copy in copies:
        copy.wait()


def unpack_spatial(meta, returned, partial):
    anywhere = pl.BlockSpec(memory_space=pl.ANY)
    return pl.pallas_call(
        unpack_spatial_body,
        grid_spec=pltpu.PrefetchScalarGridSpec(
            num_scalar_prefetch=2,
            grid=(1,),
            in_specs=[whole(returned.shape)] + [anywhere] * 3,
            out_specs=[anywhere] * 3,
            scratch_shapes=[
                pltpu.SMEM((HEADS,), jnp.int32),
                pltpu.VMEM((HEADS, 3, ROWS, W), BF16),
                pltpu.SemaphoreType.DMA((HEADS, 3)),
            ],
        ),
        out_shape=[jax.ShapeDtypeStruct(OUT, BF16)] * 3,
        input_output_aliases={3 + a: a for a in range(3)},
        compiler_params=pltpu.CompilerParams(vmem_limit_bytes=16 * MIB),
        cost_estimate=pl.CostEstimate(flops=0, bytes_accessed=5_000_000, transcendentals=0),
        name="unpack_spatial",
    )(*meta, returned, *partial)


def exchange(x):
    return lax.all_to_all(x, "space", split_axis=0, concat_axis=0, tiled=True)


SWAP = [(i, i ^ 1) for i in range(SPACES)]


def along_x(parts, sign):
    def move(step, part):
        dx = sign * (step // 2)
        if dx == 0 or part is None:
            return part
        pairs = [(f, f // 4 * 4 + (f + dx) % 4) for f in range(FRAMES)]
        return lax.ppermute(part, "frame", pairs)

    return [move(step, part) for step, part in enumerate(parts)]


def along_z(parts):
    pairs = [(f, f ^ 4) for f in range(FRAMES)]
    return [lax.ppermute(x, "frame", pairs) if n % 2 else x for n, x in enumerate(parts)]


def tie(*values):
    return lax.optimization_barrier(values)


def on_device(queries, keys, values, grad_out, head_class):
    place = jnp.stack([lax.axis_index("frame"), lax.axis_index("space")]).astype(jnp.int32)
    meta = (head_class, place)
    tabs = tuple(jnp.asarray(t) for t in tables())
    arrays = (queries, keys, values, grad_out)
    got_s = exchange(pack_spatial(meta, arrays, tabs))
    half_t = along_x(pack_temporal(meta, arrays, tabs), 1)
    got_s, *half_t = tie(got_s, *half_t)
    got_t = along_z(half_t)
    mine = got_s[:, 4:6]
    other = lax.ppermute(mine, "space", SWAP)
    own = attend_own(meta, got_s, tabs)
    own, mine, got_t[1], got_t[3], got_t[5] = tie(own, mine, got_t[1], got_t[3], got_t[5])
    kept, give = attend_shared(meta, mine, other)
    kept, give, *got_t = tie(kept, give, *got_t)
    given = lax.ppermute(give, "space", SWAP)
    grads_t = list(attend_frames(meta, got_t, tabs))
    kept, grads_t[0] = tie(kept, grads_t[0])
    flipped = along_z(grads_t)[1::2]
    level = along_x([x if n % 2 == 0 else None for n, x in enumerate(grads_t)], -1)[::2]
    back_s, *others = tie(merge(meta, own, kept, given, tabs), *flipped, *level[1:3])
    flipped, level[1:3] = others[:4], others[4:]
    home_s = exchange(back_s)
    flipped = along_x([x for part in flipped for x in (None, part)], -1)[1::2]
    home_t = [x for two in zip(level, flipped) for x in two]
    partial = unpack_temporal(meta, home_t)
    return tuple(unpack_spatial(meta, home_s, partial))


def solution(mesh):
    placed = P(None, "frame", "space", None)
    return jax.shard_map(
        on_device,
        mesh=mesh,
        in_specs=(placed, placed, placed, placed, P()),
        out_specs=(placed, placed, placed),
        check_vma=False,
    )
```
